32 devices in a mesh: seq: 8 (over z, x), chan: 4 (over y, core).
Axes of the slice: x: 2, y: 2, z: 4, core: 2. Of those that a mesh axis runs over, the one named last changes fastest.
Arguments:
- tokens: bfloat16 [16384, 1024], P('seq', 'chan'), may hold values from -6 to 6
- norm_gain: float32 [1024], P(('chan', 'seq')), may hold values from 0.25 to 1.75
- norm_shift: float32 [1024], P(('chan', 'seq')), may hold values from -3 to 3
- up_weight: bfloat16 [1024, 3072], P('seq', 'chan'), may hold values from -1 to 1
- up_bias: float32 [3072], P(('chan', 'seq')), may hold values from -3 to 3
- input_weight: bfloat16 [1024, 512], P('seq', 'chan'), may hold values from -0.1875 to 0.1875
- input_bias: float32 [512], P(('chan', 'seq')), may hold values from -3 to 3
- mix_weight: bfloat16 [512, 3072], P('seq', 'chan'), may hold values from -0.25 to 0.25
- mix_bias: float32 [3072], P(('chan', 'seq')), may hold values from -3 to 3
- down_weight: bfloat16 [3072, 1024], P('chan', 'seq'), may hold values from -0.21875 to 0.21875
- down_bias: float32 [1024], P(('chan', 'seq')), may hold values from -3 to 3
- decay_rate: float32 [512], P('seq'), may hold values from 6.1035157e-06 to 0.03
- decay_freq: float32 [512], P('seq'), may hold values from 0 to 0.5
- step_log: float32 [512], P(('chan', 'seq')), may hold values from -0.5 to 0.5
- read_real: float32 [512, 512], P('chan', 'seq'), may hold values from -0.5 to 0.5
- read_imag: float32 [512, 512], P('chan', 'seq'), may hold values from -0.5 to 0.5
- skip_gain: float32 [512], P(('chan', 'seq')), may hold values from -3 to 3
- out_grad: bfloat16 [16384, 1024], P('seq'), may hold values from -6 to 6
Outputs:
- output: float32 [16384, 1024], P('seq', 'chan')
- input_grad: float32 [16384, 1024], P('seq', 'chan')
- norm_gain_grad: float32 [1024], P(('chan', 'seq'))
- norm_shift_grad: float32 [1024], P(('chan', 'seq'))
- up_weight_grad: float32 [1024, 3072], P('seq', 'chan')
- up_bias_grad: float32 [3072], P(('chan', 'seq'))
- input_weight_grad: float32 [1024, 512], P('seq', 'chan')
- input_bias_grad: float32 [512], P(('chan', 'seq'))
- mix_weight_grad: float32 [512, 3072], P('seq', 'chan')
- mix_bias_grad: float32 [3072], P(('chan', 'seq'))
- down_weight_grad: float32 [3072, 1024], P('chan', 'seq')
- down_bias_grad: float32 [1024], P(('chan', 'seq'))
- decay_rate_grad: float32 [512], P('seq')
- decay_freq_grad: float32 [512], P('seq')
- step_log_grad: float32 [512], P(('chan', 'seq'))
- read_real_grad: float32 [512, 512], P('chan', 'seq')
- read_imag_grad: float32 [512, 512], P('chan', 'seq')
- skip_gain_grad: float32 [512], P(('chan', 'seq'))
The draws below stay inside these ranges and needn't reach their ends.
All inputs are finite; a program needn't handle non-finite values.
Results may differ from the reference program's by a relative error of at most 0.0097.
Values may be sent and summed in bfloat16 or wider, within the bound.
No kernel may reach another device: no remote copies, remote signals or barrier semaphores. Data moves between devices by JAX's collectives and lax.ppermute only.
A program may use at most 320 MiB of HBM per device.

```python
import math
import jax
import jax.numpy as jnp
from jax import lax

D = 1024
FF = 3072
CH = 512
MODES = 512
LENGTH = 16384
SEQS = 1
ROWS = 2048
TOKENS = 16384


def draw_up_weight(key, part):
    key = jax.random.fold_in(key, 11)
    entry_key, column_key = jax.random.split(key)
    entries = jnp.clip(jax.random.normal(entry_key, (D, FF), jnp.float32), -4.0, 4.0)
    column = 0.3 * jnp.clip(jax.random.normal(column_key, (1, FF), jnp.float32), -3.0, 3.0)
    return ((entries + column) * (1.0 / math.sqrt(D))).astype(jnp.bfloat16)


def levels(stream_key, shape, cuts, least, largest):
    factor_of = 1.0
    for dim, shards_of in cuts:
        heights = jax.random.uniform(jax.random.fold_in(jax.random.fold_in(stream_key, 6), dim), (shards_of,), jnp.float32, least / len(cuts), largest / len(cuts))
        factor_of = factor_of * jnp.repeat(jnp.exp(heights), shape[dim] // shards_of).reshape((-1,) + (1,) * (len(shape) - 1 - dim))
    return factor_of


def centred(stream_key, extent, scale, bound, shards=(), dtype=jnp.bfloat16):
    array = jax.random.normal(stream_key, extent, jnp.float32) * scale
    if len(shards) > 0:
        array = levels(stream_key, extent, shards, -0.22, 0.18) * array
    return jnp.clip(array, min=-bound, max=bound).astype(dtype)


def setup_inputs(seed: int = 0) -> dict:
    streams_of = jax.random.split(jax.random.key(seed), 19)
    return {
        "tokens": centred(streams_of[0], (TOKENS, D), 1.0, 6.0, ((0, 8), (1, 4))),
        "norm_gain": jnp.clip(1.0 + 0.15 * jax.random.normal(streams_of[1], (D,), jnp.float32), 0.25, 1.75),
        "norm_shift": centred(streams_of[2], (D,), 0.5, 3.0, ((0, 32),), jnp.float32),
        "up_weight": draw_up_weight(jax.random.fold_in(streams_of[18], 71), 0),
        "up_bias": centred(streams_of[4], (FF,), 0.5, 3.0, ((0, 32),), jnp.float32),
        "input_weight": centred(streams_of[5], (D, CH), D ** -0.5, 0.1875, ((0, 8), (1, 4))),
        "input_bias": centred(streams_of[6], (CH,), 0.5, 3.0, ((0, 32),), jnp.float32),
        "mix_weight": centred(streams_of[7], (CH, FF), CH ** -0.5, 0.25, ((0, 8), (1, 4))),
        "mix_bias": centred(streams_of[8], (FF,), 0.5, 3.0, ((0, 32),), jnp.float32),
        "down_weight": centred(streams_of[9], (FF, D), (FF // 4) ** -0.5, 0.21875, ((0, 4), (1, 8))),
        "down_bias": centred(streams_of[10], (D,), 0.5, 3.0, ((0, 32),), jnp.float32),
        "decay_rate": jnp.clip(jnp.exp(math.log(0.03) - 8.500088 * jax.random.uniform(streams_of[11], (MODES,), jnp.float32) ** levels(streams_of[11], (MODES,), ((0, 8),), -0.2, 0.2)), 6.10351571594947e-06, 0.03),
        "decay_freq": jnp.clip(0.5 * jax.random.uniform(streams_of[12], (MODES,), jnp.float32) ** levels(streams_of[12], (MODES,), ((0, 8),), -0.2, 0.2), 0.0, 0.5),
        "step_log": jnp.clip(jax.random.uniform(streams_of[13], (CH,), jnp.float32, -0.5, 0.5) * levels(streams_of[13], (CH,), ((0, 32),), -0.4, 0.0), -0.5, 0.5),
        "read_real": centred(streams_of[14], (CH, MODES), (MODES // 4) ** -0.5, 0.5, ((0, 4), (1, 8)), jnp.float32),
        "read_imag": centred(streams_of[15], (CH, MODES), (MODES // 4) ** -0.5, 0.5, ((0, 4), (1, 8)), jnp.float32),
        "skip_gain": centred(streams_of[16], (CH,), 0.5, 3.0, ((0, 32),), jnp.float32),
        "out_grad": centred(streams_of[17], (TOKENS, D), 1.0, 6.0, ((0, 8),)),
    }


PRECISE = lax.Precision.HIGHEST
EPSILON = 1e-05

@jax.custom_vjp
def low(v):
    return lax.optimization_barrier(v.astype(jnp.bfloat16)).astype(jnp.float32)

@jax.custom_vjp
def low_back(v):
    return v

def low_keep(v):
    return (low(v), None)

def low_pass(kept, grad):
    return (grad,)

def back_keep(v):
    return (v, None)

def back_low(kept, grad):
    return (low(grad),)
low.defvjp(low_keep, low_pass)
low_back.defvjp(back_keep, back_low)

def matmul(left, right):
    return jnp.dot(left, right, precision=PRECISE, preferred_element_type=jnp.float32)

def mode_rates(decay_rate, decay_freq, step_log):
    spacing = jnp.exp(step_log)
    return (spacing[:, None] * decay_rate[None, :], spacing[:, None] * decay_freq[None, :])

def powers(damping, rotation, block_len):
    offsets = jnp.arange(block_len).astype(jnp.float32)[:, None, None]
    length = jnp.exp(-damping[None] * offsets)
    return (length * jnp.cos(rotation[None] * offsets), length * jnp.sin(rotation[None] * offsets))

def prepare_modes(decay_rate, decay_freq, step_log, block_len):
    damping, rotation = mode_rates(decay_rate, decay_freq, step_log)
    power_re, power_im = powers(damping, rotation, block_len)
    return (damping, rotation, power_re, power_im)

def block_states(values, damping, low_re, low_im):
    block_len = low_re.shape[0]
    blocks = values.reshape(-1, block_len, values.shape[1])[:, ::-1, :]
    inflow = -jnp.expm1(-damping)
    state_re = inflow * low_back(jnp.einsum('dhn,qdh->qhn', low_re, blocks, precision=PRECISE))
    state_im = inflow * low_back(jnp.einsum('dhn,qdh->qhn', low_im, blocks, precision=PRECISE))
    return (state_re, state_im)

def chain_starts(ends_re, ends_im, damping, rotation, block_len, begin_re, begin_im):
    factor = jnp.exp(-damping * block_len)
    jump_re = factor * jnp.cos(rotation * block_len)
    jump_im = factor * jnp.sin(rotation * block_len)

    def advance(carried, element):
        state_re, state_im = carried
        after_re = jump_re * state_re - jump_im * state_im + element[0]
        after_im = jump_re * state_im + jump_im * state_re + element[1]
        return ((after_re, after_im), (state_re, state_im))
    return lax.scan(advance, (begin_re, begin_im), (ends_re, ends_im))

def start_readout(starts_re, starts_im, damping, rotation, read_re, read_im, low_re, low_im):
    factor = jnp.exp(-damping)
    step_re = factor * jnp.cos(rotation)
    step_im = factor * jnp.sin(rotation)
    weigh_re = read_re * step_re - read_im * step_im
    weigh_im = read_re * step_im + read_im * step_re
    mixed_re = low(weigh_re * starts_re - weigh_im * starts_im)
    mixed_im = low(weigh_re * starts_im + weigh_im * starts_re)
    return low_back(jnp.einsum('qhn,dhn->qdh', mixed_re, low_re, precision=PRECISE) - jnp.einsum('qhn,dhn->qdh', mixed_im, low_im, precision=PRECISE))

def local_conv(values, damping, read_re, read_im, power_re, power_im):
    block_len = power_re.shape[0]
    inflow = -jnp.expm1(-damping)
    kernel = jnp.einsum('hn,dhn->dh', read_re * inflow, power_re, precision=PRECISE) - jnp.einsum('hn,dhn->dh', read_im * inflow, power_im, precision=PRECISE)
    offsets = jnp.arange(block_len)
    lag_table = offsets[:, None] - offsets[None, :]
    toeplitz = jnp.where((lag_table >= 0)[:, :, None], kernel[jnp.clip(lag_table, 0, block_len - 1)], 0.0)
    blocks = values.reshape(-1, block_len, values.shape[1])
    return jnp.einsum('tuh,quh->qth', toeplitz, blocks, precision=PRECISE)

def dss_open(values, damping, rotation, power_re, power_im, read_re, read_im, skip_gain):
    block_len = power_re.shape[0]
    low_re = low(power_re)
    low_im = low(power_im)
    ends_re, ends_im = block_states(values, damping, low_re, low_im)
    blank_state = jnp.zeros(damping.shape, jnp.float32)
    finals, starts = chain_starts(ends_re, ends_im, damping, rotation, block_len, blank_state, blank_state)
    mixed = local_conv(values, damping, read_re, read_im, power_re, power_im)
    mixed = mixed + start_readout(starts[0], starts[1], damping, rotation, read_re, read_im, low_re, low_im)
    return (mixed.reshape(values.shape) + skip_gain * values, finals[0], finals[1])

def gss_layer(tokens, norm_gain, norm_shift, up_weight, up_bias, input_weight, input_bias, mix_weight, mix_bias, down_weight, down_bias, decay_rate, decay_freq, step_log, read_real, read_imag, skip_gain):
    average = lax.optimization_barrier(jnp.mean(tokens, axis=1, keepdims=True))
    spread = lax.optimization_barrier(jnp.mean(tokens * tokens, axis=1, keepdims=True)) - average * average
    normed = low((tokens - average) * lax.rsqrt(spread + EPSILON) * norm_gain + norm_shift)
    pre_up = low_back(matmul(normed, up_weight) + up_bias)
    pre_in = low_back(matmul(normed, input_weight) + input_bias)
    upper_act = jax.nn.gelu(pre_up, approximate=False)
    values = low(jax.nn.gelu(pre_in, approximate=False))
    block_len = math.gcd(ROWS, 64)
    damping, rotation, power_re, power_im = prepare_modes(decay_rate, decay_freq, step_log, block_len)
    mixed, end_re, end_im = dss_open(values, damping, rotation, power_re, power_im, read_real, read_imag, skip_gain)
    mixed = low(mixed)
    lifted = low_back(matmul(mixed, mix_weight) + mix_bias)
    hidden = low(upper_act * lifted)
    return tokens + matmul(hidden, down_weight) + down_bias

def reference(tokens, norm_gain, norm_shift, up_weight, up_bias, input_weight, input_bias, mix_weight, mix_bias, down_weight, down_bias, decay_rate, decay_freq, step_log, read_real, read_imag, skip_gain, out_grad):
    weights = (norm_gain, norm_shift, up_weight.astype(jnp.float32), up_bias, input_weight.astype(jnp.float32), input_bias, mix_weight.astype(jnp.float32), mix_bias, down_weight.astype(jnp.float32), down_bias, decay_rate, decay_freq, step_log, read_real, read_imag, skip_gain)
    stacked = tokens.astype(jnp.float32).reshape(SEQS, LENGTH, D)

    def forward(stacked, weights):

        def sequence(rows):
            return gss_layer(rows, *weights)
        return lax.map(jax.checkpoint(sequence), stacked)
    output, pullback = jax.vjp(forward, stacked, weights)
    stacked_grad, gradients = pullback(out_grad.astype(jnp.float32).reshape(SEQS, LENGTH, D))
    return (output.reshape(TOKENS, D), stacked_grad.reshape(TOKENS, D), gradients[0], gradients[1], gradients[2], gradients[3], gradients[4], gradients[5], gradients[6], gradients[7], gradients[8], gradients[9], gradients[10], gradients[11], gradients[12], gradients[13], gradients[14], gradients[15])
```

```python
from functools import partial
import math

import jax
import jax.numpy as jnp
from jax import lax
from jax.experimental import pallas as pl
from jax.experimental.pallas import tpu as pltpu
from jax.sharding import PartitionSpec as P

D = 1024
LENGTH = 16384
EPSILON = 1e-05


BLOCK = 128
VMEM = 56 * 1024 * 1024


def dot(left, right, left_dim, right_dim):
    return lax.dot_general(
        left, right, (((left_dim,), (right_dim,)), ((), ())), preferred_element_type=jnp.float32
    )


def cmul(a_re, a_im, b_re, b_im):
    return (a_re * b_re - a_im * b_im, a_re * b_im + a_im * b_re)


def grow(first, reversed_rows, mode_powers, store):
    row = lax.broadcasted_iota(jnp.int32, (8, first[0].shape[1]), 0)
    exponent = 7 - row if reversed_rows else row
    part = (
        jnp.broadcast_to(first[0], row.shape),
        jnp.broadcast_to(first[1], row.shape),
    )
    for level in range(3):
        factor_re, factor_im = mode_powers(level)
        taken = (exponent >> level) & 1 == 1
        part = cmul(*part, jnp.where(taken, factor_re, 1.0), jnp.where(taken, factor_im, 0.0))
    spot = BLOCK - 8 if reversed_rows else 0
    store(spot, part[0], part[1])
    whole = part
    size, level = 8, 3
    while size < BLOCK:
        factor = mode_powers(level)
        fresh = cmul(*whole, *factor)
        spot = BLOCK - 2 * size if reversed_rows else size
        store(spot, *fresh)
        pair = (fresh, whole) if reversed_rows else (whole, fresh)
        whole = tuple(jnp.concatenate([p, q], axis=0) for p, q in zip(*pair))
        size, level = 2 * size, level + 1


def tables_kernel(
    power_re_ref,
    power_im_ref,
    read_re_ref,
    read_im_ref,
    inflow_ref,
    power_ref,
    out_table_ref,
    in_table_ref,
    toeplitz_ref,
):
    modes = power_re_ref.shape[2]
    lower, upper = slice(0, modes), slice(modes, 2 * modes)

    def mode_powers(level):
        return (power_re_ref[0, level : level + 1, :], power_im_ref[0, level : level + 1, :])

    inflow = inflow_ref[0]
    one, none = jnp.ones_like(inflow), jnp.zeros_like(inflow)

    def store_power(spot, part_re, part_im):
        rows = slice(spot, spot + part_re.shape[0])
        power_ref[0, rows, lower] = part_re
        power_ref[0, rows, upper] = part_im

    grow((one, none), False, mode_powers, store_power)
    exact = jnp.concatenate([power_ref[0, :, lower], -power_ref[0, :, upper]], axis=1)
    rounded = exact.astype(jnp.bfloat16)
    out_table_ref[0] = rounded
    rest = (exact - rounded.astype(jnp.float32)).astype(jnp.bfloat16)
    backward = []

    def store_in(spot, part_re, part_im):
        backward.append((spot, part_re, part_im))

    grow((one, none), True, mode_powers, store_in)
    backward.sort(key=lambda entry: entry[0])
    in_table_ref[0, :, lower] = jnp.concatenate([e[1] for e in backward], 0).astype(jnp.bfloat16)
    in_table_ref[0, :, upper] = jnp.concatenate([e[2] for e in backward], 0).astype(jnp.bfloat16)
    weight = jnp.concatenate([read_re_ref[0] * inflow, read_im_ref[0] * inflow], axis=1)
    high = weight.astype(jnp.bfloat16).astype(jnp.float32)
    row = lax.broadcasted_iota(jnp.int32, (16, 2 * modes), 0)
    probe = jnp.where(row == 0, high, jnp.where(row == 1, weight - high, 0.0))
    probe = probe.astype(jnp.bfloat16)
    lags = dot(probe, rounded, 1, 1) + dot(probe, rest, 1, 1)
    kernel_row = jnp.sum(lags, axis=0, keepdims=True)
    skewed = pltpu.roll(
        jnp.broadcast_to(kernel_row, (BLOCK, BLOCK)), 0, 1, stride=1, stride_axis=0
    )
    source = lax.broadcasted_iota(jnp.int32, (BLOCK, BLOCK), 0)
    target = lax.broadcasted_iota(jnp.int32, (BLOCK, BLOCK), 1)
    skewed = jnp.where(target >= source, skewed, 0.0)
    coarse = skewed.astype(jnp.bfloat16)
    toeplitz_ref[0, :BLOCK, :] = coarse
    toeplitz_ref[0, BLOCK:, :] = (skewed - coarse.astype(jnp.float32)).astype(jnp.bfloat16)


def make_tables(power_re, power_im, read_re, read_im, inflow):
    count, levels, modes = power_re.shape

    def spec(*shape):
        return pl.BlockSpec((1,) + shape, lambda i: (i, 0, 0))

    return pl.pallas_call(
        tables_kernel,
        grid=(count,),
        in_specs=[spec(levels, modes)] * 2 + [spec(1, modes)] * 3,
        out_specs=[
            spec(BLOCK, 2 * modes),
            spec(BLOCK, 2 * modes),
            spec(BLOCK, 2 * modes),
            spec(2 * BLOCK, BLOCK),
        ],
        out_shape=[
            jax.ShapeDtypeStruct((count, BLOCK, 2 * modes), jnp.float32),
            jax.ShapeDtypeStruct((count, BLOCK, 2 * modes), jnp.bfloat16),
            jax.ShapeDtypeStruct((count, BLOCK, 2 * modes), jnp.bfloat16),
            jax.ShapeDtypeStruct((count, 2 * BLOCK, BLOCK), jnp.bfloat16),
        ],
        compiler_params=pltpu.CompilerParams(vmem_limit_bytes=VMEM),
        cost_estimate=cost(12),
    )(power_re, power_im, read_re[:, None], read_im[:, None], inflow[:, None])


def spread_tokens(ref, scratch):
    sources, count, tokens = ref.shape
    per_source = tokens // BLOCK
    for source in range(sources):
        for part in range(per_source):
            row = (source * per_source + part) * count
            tile = ref[source, :, part * BLOCK : (part + 1) * BLOCK]
            scratch[row : row + count, :] = tile.astype(jnp.float32)


def gather_tokens(scratch, ref):
    sources, count, tokens = ref.shape
    per_source = tokens // BLOCK
    for source in range(sources):
        for part in range(per_source):
            row = (source * per_source + part) * count
            ref[source, :, part * BLOCK : (part + 1) * BLOCK] = scratch[
                row : row + count, :
            ].astype(ref.dtype)


def put_rows(states, rows, value):
    for tile in range(states.shape[0]):
        states[tile, rows, :] = value[:, tile * 128 : (tile + 1) * 128]


def take_rows(states, rows):
    return jnp.concatenate([states[tile, rows, :] for tile in range(states.shape[0])], axis=1)


def run_chain(states, jump_ref, sign, count, blocks, order):
    tiles = states.shape[0] // 2
    jumps = [
        (
            jump_ref[:, t * 128 : (t + 1) * 128],
            sign * jump_ref[:, (tiles + t) * 128 : (tiles + t + 1) * 128],
        )
        for t in range(tiles)
    ]

    def step(turn, state):
        rows = pl.ds(pl.multiple_of(order(turn) * count, count), count)
        following = []
        for t in range(tiles):
            end_re, end_im = states[t, rows, :], states[tiles + t, rows, :]
            states[t, rows, :] = state[t][0]
            states[tiles + t, rows, :] = state[t][1]
            next_re, next_im = cmul(*jumps[t], *state[t])
            following.append((next_re + end_re, next_im + end_im))
        return tuple(following)

    blank = jnp.zeros((count, 128), jnp.float32)
    lax.fori_loop(0, blocks, step, ((blank, blank),) * tiles, unroll=2)


def forward_kernel(
    values_ref,
    skip_ref,
    jump_ref,
    inflow_ref,
    lead_ref,
    out_table_ref,
    in_table_ref,
    toeplitz_ref,
    mixed_ref,
    starts_ref,
    split_ref,
    tokens,
    states,
):
    count = values_ref.shape[1]
    blocks = states.shape[1] // count
    modes = states.shape[0] * 64
    spread_tokens(values_ref, tokens)

    def rows_of(channel):
        return pl.ds(channel, blocks, stride=count)

    def enter(channel, carry):
        own = tokens[rows_of(channel), :].astype(jnp.bfloat16)
        split_ref[channel] = own
        ends = dot(own, in_table_ref[channel], 1, 0)
        put_rows(states, rows_of(channel), ends * inflow_ref[channel])
        return carry

    lax.fori_loop(0, count, enter, 0)
    run_chain(states, jump_ref, 1.0, count, blocks, lambda turn: turn)

    def leave(channel, carry):
        start = take_rows(states, rows_of(channel))
        starts_ref[channel] = start.astype(jnp.bfloat16)
        lead = lead_ref[channel]
        weighted = cmul(lead[:, :modes], lead[:, modes:], start[:, :modes], start[:, modes:])
        weighted = jnp.concatenate(weighted, axis=1).astype(jnp.bfloat16)
        own = tokens[rows_of(channel), :]
        own_low = own.astype(jnp.bfloat16)
        mixed = dot(weighted, out_table_ref[channel], 1, 1)
        mixed += dot(own_low, toeplitz_ref[channel, :BLOCK, :], 1, 0)
        mixed += dot(own_low, toeplitz_ref[channel, BLOCK:, :], 1, 0)
        tokens[rows_of(channel), :] = mixed + skip_ref[channel] * own
        return carry

    lax.fori_loop(0, count, leave, 0)
    gather_tokens(tokens, mixed_ref)


def run_forward(values, skip, jump, inflow, lead, out_table, in_table, toeplitz):
    sources, count, tokens = values.shape
    blocks = sources * tokens // BLOCK
    width = jump.shape[1]
    vmem = pl.BlockSpec(memory_space=pltpu.VMEM)
    return pl.pallas_call(
        forward_kernel,
        in_specs=[vmem, pl.BlockSpec(memory_space=pltpu.SMEM)] + [vmem] * 6,
        out_specs=[vmem] * 3,
        out_shape=[
            jax.ShapeDtypeStruct(values.shape, jnp.bfloat16),
            jax.ShapeDtypeStruct((count, blocks, width), jnp.bfloat16),
            jax.ShapeDtypeStruct((count, blocks, BLOCK), jnp.bfloat16),
        ],
        scratch_shapes=[
            pltpu.VMEM((blocks * count, BLOCK), jnp.float32),
            pltpu.VMEM((width // 128, blocks * count, 128), jnp.float32),
        ],
        compiler_params=pltpu.CompilerParams(vmem_limit_bytes=VMEM),
        cost_estimate=cost(20),
    )(values, skip, jump, inflow, lead, out_table, in_table, toeplitz)


def backward_kernel(
    grads_ref,
    skip_ref,
    jump_ref,
    inflow_ref,
    lead_ref,
    out_table_ref,
    in_table_ref,
    toeplitz_ref,
    values_grad_ref,
    later_ref,
    split_ref,
    grads,
    states,
):
    count = grads_ref.shape[1]
    blocks = states.shape[1] // count
    modes = states.shape[0] * 64
    spread_tokens(grads_ref, grads)

    def rows_of(channel):
        return pl.ds(channel, blocks, stride=count)

    def enter(channel, carry):
        own = grads[rows_of(channel), :].astype(jnp.bfloat16)
        split_ref[channel] = own
        lead = lead_ref[channel]
        back = dot(own, out_table_ref[channel], 1, 0)
        back = cmul(lead[:, :modes], -lead[:, modes:], back[:, :modes], back[:, modes:])
        put_rows(states, rows_of(channel), jnp.concatenate(back, axis=1))
        return carry

    lax.fori_loop(0, count, enter, 0)
    run_chain(states, jump_ref, -1.0, count, blocks, lambda turn: blocks - 1 - turn)

    def leave(channel, carry):
        later = take_rows(states, rows_of(channel))
        later_ref[channel] = later.astype(jnp.bfloat16)
        later = (later * inflow_ref[channel]).astype(jnp.bfloat16)
        grad = grads[rows_of(channel), :]
        grad_low = grad.astype(jnp.bfloat16)
        back = dot(later, in_table_ref[channel], 1, 1)
        back += dot(grad_low, toeplitz_ref[channel, :BLOCK, :], 1, 1)
        back += dot(grad_low, toeplitz_ref[channel, BLOCK:, :], 1, 1)
        grads[rows_of(channel), :] = back + skip_ref[channel] * grad
        return carry

    lax.fori_loop(0, count, leave, 0)
    gather_tokens(grads, values_grad_ref)


def run_backward(grads, skip, jump, inflow, lead, out_table, in_table, toeplitz):
    sources, count, tokens = grads.shape
    blocks = sources * tokens // BLOCK
    width = jump.shape[1]
    vmem = pl.BlockSpec(memory_space=pltpu.VMEM)
    return pl.pallas_call(
        backward_kernel,
        in_specs=[vmem, pl.BlockSpec(memory_space=pltpu.SMEM)] + [vmem] * 6,
        out_specs=[vmem] * 3,
        out_shape=[
            jax.ShapeDtypeStruct(grads.shape, jnp.bfloat16),
            jax.ShapeDtypeStruct((count, blocks, width), jnp.bfloat16),
            jax.ShapeDtypeStruct((count, blocks, BLOCK), jnp.bfloat16),
        ],
        scratch_shapes=[
            pltpu.VMEM((blocks * count, BLOCK), jnp.float32),
            pltpu.VMEM((width // 128, blocks * count, 128), jnp.float32),
        ],
        compiler_params=pltpu.CompilerParams(vmem_limit_bytes=VMEM),
        cost_estimate=cost(20),
    )(grads, skip, jump, inflow, lead, out_table, in_table, toeplitz)


def sums_kernel(grad_ref, value_ref, start_ref, later_ref, power_ref, sums_ref, skip_ref):
    modes = power_ref.shape[2] // 2
    row = lax.broadcasted_iota(jnp.int32, (BLOCK, BLOCK), 0)
    lane = lax.broadcasted_iota(jnp.int32, (BLOCK, BLOCK), 1)
    flip = jnp.where(row + lane == BLOCK - 1, 1.0, 0.0).astype(jnp.bfloat16)

    def fold(part):
        return jnp.sum(part.reshape(part.shape[0] // 8, 8, part.shape[1]), axis=0)

    grad, value = grad_ref[0], value_ref[0]
    start, later = start_ref[0], later_ref[0]
    product = grad.astype(jnp.float32) * value.astype(jnp.float32)
    skip_ref[0] = jnp.sum(product, axis=0, keepdims=True)
    turned = dot(value, flip, 1, 0).astype(jnp.bfloat16)
    out_sum = dot(grad, start, 0, 0)
    in_sum = dot(turned, later, 0, 0)
    cross = dot(grad, turned, 0, 0)
    cross = jnp.where(row + lane >= BLOCK - 1, cross, 0.0)
    lags = jnp.sum(pltpu.roll(cross, 1, 1, stride=1, stride_axis=0), axis=0, keepdims=True)
    lags = jnp.sum(jnp.where(row == lane, lags, 0.0), axis=1, keepdims=True)
    weight = lax.broadcasted_iota(jnp.int32, (BLOCK, modes), 0).astype(jnp.float32)
    power_re, power_im = power_ref[0, :, :modes], power_ref[0, :, modes:]
    terms = []
    for total, sign in ((out_sum, 1.0), (in_sum, -1.0)):
        term_re, term_im = cmul(power_re, power_im, total[:, :modes], sign * total[:, modes:])
        terms += [fold(term_re), fold(term_im), fold(weight * term_re), fold(weight * term_im)]
    later_re, later_im = (later[:, :modes].astype(jnp.float32), later[:, modes:].astype(jnp.float32))
    start_re, start_im = (start[:, :modes].astype(jnp.float32), start[:, modes:].astype(jnp.float32))
    terms += [
        fold(later_re * start_re + later_im * start_im),
        fold(later_re * start_im - later_im * start_re),
    ]
    local_re, local_im = power_re * lags, power_im * lags
    terms += [fold(local_re), fold(local_im), fold(weight * local_re), fold(weight * local_im)]
    for index, term in enumerate(terms):
        sums_ref[0, index : index + 1, :] = jnp.sum(term, axis=0, keepdims=True)


def run_sums(grads, values, starts, later, power):
    count, blocks, width = starts.shape

    def spec(*shape):
        return pl.BlockSpec((1,) + shape, lambda i: (i, 0, 0))

    return pl.pallas_call(
        sums_kernel,
        grid=(count,),
        in_specs=[spec(blocks, BLOCK)] * 2 + [spec(blocks, width)] * 2 + [spec(BLOCK, width)],
        out_specs=[spec(16, width // 2), spec(1, BLOCK)],
        out_shape=[
            jax.ShapeDtypeStruct((count, 16, width // 2), jnp.float32),
            jax.ShapeDtypeStruct((count, 1, BLOCK), jnp.float32),
        ],
        compiler_params=pltpu.CompilerParams(vmem_limit_bytes=VMEM),
        cost_estimate=cost(18),
    )(grads, values, starts, later, power)


def cost(microseconds):
    return pl.CostEstimate(
        flops=int(microseconds * 1e9), bytes_accessed=int(microseconds * 1e6), transcendentals=0
    )


def erf_parts(value):
    half = 0.5 * (1.0 + lax.erf(value * (1.0 / math.sqrt(2.0))))
    density = jnp.exp(-0.5 * value * value) * (1.0 / math.sqrt(2.0 * math.pi))
    return value * half, half + value * density


def norm_kernel(
    place_ref,
    own_ref,
    near_ref,
    far_ref,
    last_ref,
    affine_ref,
    weight_ref,
    bias_ref,
    normed_ref,
    values_ref,
    slope_ref,
    before_ref,
    stats_ref,
    whole,
):
    place = place_ref[0]
    width = own_ref.shape[1]
    for offset, part in enumerate((own_ref, near_ref, far_ref, last_ref)):
        start = pl.multiple_of((place ^ offset) * width, width)
        whole[:, pl.ds(start, width)] = part[...].astype(jnp.float32)
    inputs = whole[...]
    average = jnp.mean(inputs, axis=1, keepdims=True)
    spread = jnp.mean(inputs * inputs, axis=1, keepdims=True) - average * average
    inverse = lax.rsqrt(spread + EPSILON)
    normed = (inputs - average) * inverse * affine_ref[0:1, :] + affine_ref[1:2, :]
    normed = normed.astype(jnp.bfloat16)
    normed_ref[...] = normed
    before = dot(weight_ref[...], normed, 1, 1) + bias_ref[...]
    values, slope = erf_parts(before)
    values_ref[...] = values.astype(jnp.bfloat16)
    slope_ref[...] = slope
    before_ref[...] = before
    lane = lax.broadcasted_iota(jnp.int32, (inputs.shape[0], 128), 1)
    stats_ref[...] = jnp.where(lane < 64, average, inverse)


def run_norm(parts, affine, weight, bias):
    rows, width = parts[0].shape
    channels, full = weight.shape
    step = 256
    place = lax.axis_index("chan").astype(jnp.int32).reshape(1)
    return pl.pallas_call(
        norm_kernel,
        grid_spec=pltpu.PrefetchScalarGridSpec(
            num_scalar_prefetch=1,
            grid=(rows // step,),
            in_specs=[
                pl.BlockSpec((step, width), lambda i, p: (i, 0)),
                pl.BlockSpec((step, width), lambda i, p: (i, 0)),
                pl.BlockSpec((step, width), lambda i, p: (i, 0)),
                pl.BlockSpec((step, width), lambda i, p: (i, 0)),
                pl.BlockSpec((2, full), lambda i, p: (0, 0)),
                pl.BlockSpec((channels, full), lambda i, p: (0, 0)),
                pl.BlockSpec((channels, 1), lambda i, p: (0, 0)),
            ],
            out_specs=[
                pl.BlockSpec((step, full), lambda i, p: (i, 0)),
                pl.BlockSpec((channels, step), lambda i, p: (0, i)),
                pl.BlockSpec((channels, step), lambda i, p: (0, i)),
                pl.BlockSpec((channels, step), lambda i, p: (0, i)),
                pl.BlockSpec((step, 128), lambda i, p: (i, 0)),
            ],
            scratch_shapes=[pltpu.VMEM((step, full), jnp.float32)],
        ),
        out_shape=[
            jax.ShapeDtypeStruct((rows, full), jnp.bfloat16),
            jax.ShapeDtypeStruct((channels, rows), jnp.bfloat16),
            jax.ShapeDtypeStruct((channels, rows), jnp.float32),
            jax.ShapeDtypeStruct((channels, rows), jnp.float32),
            jax.ShapeDtypeStruct((rows, 128), jnp.float32),
        ],
        compiler_params=pltpu.CompilerParams(vmem_limit_bytes=VMEM),
        cost_estimate=cost(8),
    )(place, *parts, affine, weight, bias[:, None])


def gate_kernel(
    place_ref,
    normed_ref,
    grad_ref,
    up_ref,
    down_ref,
    mix_ref,
    bias_ref,
    upper_ref,
    slope_ref,
    lifted_grad_ref,
    keep_ref,
    send_ref,
    bias_grad_ref,
):
    place = place_ref[0]
    size = keep_ref.shape[1]
    before = dot(normed_ref[...], up_ref[...], 1, 0) + bias_ref[...]
    hidden_grad = dot(grad_ref[...], down_ref[...], 1, 0)
    upper, slope = erf_parts(before)
    upper_ref[...] = upper
    slope_ref[...] = hidden_grad * slope
    lifted_grad = (hidden_grad * upper).astype(jnp.bfloat16)
    lifted_grad_ref[...] = lifted_grad

    def piece(offset):
        start = pl.multiple_of((place ^ offset) * size, size)
        return dot(mix_ref[pl.ds(start, size), :], lifted_grad, 1, 1)

    keep_ref[0], keep_ref[1] = piece(0), piece(2)
    send_ref[0], send_ref[1] = piece(1), piece(3)
    part = jnp.sum(lifted_grad.astype(jnp.float32), axis=0, keepdims=True)

    @pl.when(pl.program_id(0) == 0)
    def _():
        bias_grad_ref[...] = jnp.zeros_like(bias_grad_ref)

    bias_grad_ref[...] += part


def run_gate(normed, grad, up, down, mix, bias):
    rows, full = normed.shape
    units = up.shape[1]
    channels = mix.shape[0]
    step = 256

    place = lax.axis_index("chan").astype(jnp.int32).reshape(1)

    def fixed(*shape):
        return pl.BlockSpec(shape, lambda i, p: (0, 0))

    def rowwise(columns):
        return pl.BlockSpec((step, columns), lambda i, p: (i, 0))

    size = channels // 4
    pieces = pl.BlockSpec((2, size, step), lambda i, p: (0, 0, i))
    return pl.pallas_call(
        gate_kernel,
        grid_spec=pltpu.PrefetchScalarGridSpec(
            num_scalar_prefetch=1,
            grid=(rows // step,),
            in_specs=[
                rowwise(full),
                rowwise(full),
                fixed(full, units),
                fixed(full, units),
                fixed(channels, units),
                fixed(1, units),
            ],
            out_specs=[rowwise(units)] * 3 + [pieces] * 2 + [fixed(1, units)],
        ),
        out_shape=[jax.ShapeDtypeStruct((rows, units), jnp.float32)] * 2
        + [jax.ShapeDtypeStruct((rows, units), jnp.bfloat16)]
        + [jax.ShapeDtypeStruct((2, size, rows), jnp.float32)] * 2
        + [jax.ShapeDtypeStruct((1, units), jnp.float32)],
        compiler_params=pltpu.CompilerParams(vmem_limit_bytes=VMEM),
        cost_estimate=cost(15),
    )(place, normed, grad, up, down, mix, bias[None])


def mid_kernel(
    place_ref,
    own_ref,
    near_ref,
    far_ref,
    last_ref,
    upper_ref,
    slope_ref,
    normed_ref,
    mix_ref,
    down_ref,
    up_ref,
    bias_ref,
    affine_ref,
    mixed_ref,
    hidden_ref,
    up_grad_ref,
    out_keep_ref,
    out_send_ref,
    feature_keep_ref,
    feature_send_ref,
    sums_ref,
    bias_grad_ref,
    whole,
):
    place = place_ref[0]
    width = out_keep_ref.shape[2]
    size = own_ref.shape[0]
    for offset, piece in enumerate((own_ref, near_ref, far_ref, last_ref)):
        start = pl.multiple_of((place ^ offset) * size, size)
        mixed_ref[pl.ds(start, size), :] = piece[...]
    lifted = dot(mixed_ref[...], mix_ref[...], 0, 0) + bias_ref[...]
    hidden = (upper_ref[...] * lifted).astype(jnp.bfloat16)
    up_grad = (slope_ref[...] * lifted).astype(jnp.bfloat16)
    hidden_ref[...] = hidden
    up_grad_ref[...] = up_grad

    @pl.when(pl.program_id(0) == 0)
    def _():
        bias_grad_ref[...] = jnp.zeros_like(bias_grad_ref)

    bias_grad_ref[...] += jnp.sum(up_grad.astype(jnp.float32), axis=0, keepdims=True)

    def part(offset):
        start = pl.multiple_of((place ^ offset) * width, width)
        return whole[:, pl.ds(start, width)].astype(jnp.bfloat16)

    whole[...] = dot(hidden, down_ref[...], 1, 1)
    out_keep_ref[0], out_keep_ref[1] = part(0), part(2)
    out_send_ref[0], out_send_ref[1] = part(1), part(3)
    feature = dot(up_grad, up_ref[...], 1, 1)
    whole[...] = feature
    feature_keep_ref[0], feature_keep_ref[1] = part(0), part(2)
    feature_send_ref[0], feature_send_ref[1] = part(1), part(3)
    one = jnp.sum(feature * affine_ref[0:1, :], axis=1, keepdims=True)
    shifted = normed_ref[...].astype(jnp.float32) - affine_ref[1:2, :]
    two = jnp.sum(feature * shifted, axis=1, keepdims=True)
    lane = lax.broadcasted_iota(jnp.int32, (feature.shape[0], 128), 1)
    sums_ref[...] = jnp.where(lane == 0, one, jnp.where(lane == 1, two, 0.0)).T[0:8, :]


def run_mid(parts, upper, slope, normed, mix, down, up, bias, affine):
    rows, full = normed.shape
    units = up.shape[1]
    channels = mix.shape[0]
    width = full // 4
    step = 256
    place = lax.axis_index("chan").astype(jnp.int32).reshape(1)

    def fixed(*shape):
        return pl.BlockSpec(shape, lambda i, p: (0, 0))

    def rowwise(columns):
        return pl.BlockSpec((step, columns), lambda i, p: (i, 0))

    def columns(count):
        return pl.BlockSpec((count, step), lambda i, p: (0, i))

    pieces = pl.BlockSpec((2, step, width), lambda i, p: (0, i, 0))
    piece_shape = jax.ShapeDtypeStruct((2, rows, width), jnp.bfloat16)
    return pl.pallas_call(
        mid_kernel,
        grid_spec=pltpu.PrefetchScalarGridSpec(
            num_scalar_prefetch=1,
            grid=(rows // step,),
            in_specs=[
                columns(channels // 4),
                columns(channels // 4),
                columns(channels // 4),
                columns(channels // 4),
                rowwise(units),
                rowwise(units),
                rowwise(full),
                fixed(channels, units),
                fixed(full, units),
                fixed(full, units),
                fixed(1, units),
                fixed(2, full),
            ],
            out_specs=[columns(channels)]
            + [rowwise(units)] * 2
            + [pieces] * 4
            + [columns(8), fixed(1, units)],
            scratch_shapes=[pltpu.VMEM((step, full), jnp.float32)],
        ),
        out_shape=[jax.ShapeDtypeStruct((channels, rows), jnp.bfloat16)]
        + [jax.ShapeDtypeStruct((rows, units), jnp.bfloat16)] * 2
        + [piece_shape] * 4
        + [
            jax.ShapeDtypeStruct((8, rows), jnp.float32),
            jax.ShapeDtypeStruct((1, units), jnp.float32),
        ],
        compiler_params=pltpu.CompilerParams(vmem_limit_bytes=VMEM),
        cost_estimate=cost(14),
    )(place, *parts, upper, slope, normed, mix, down, up, bias[None], affine)


def payload_kernel(
    grad_ref, slope_ref, before_ref, gain_ref, bias_ref, sums_ref, payload_ref, bias_grad_ref
):
    count = grad_ref.shape[0]
    grad = (grad_ref[...].astype(jnp.float32) * slope_ref[...]).astype(jnp.bfloat16)
    payload_ref[:count, :] = grad
    grad = grad.astype(jnp.float32)
    centred = before_ref[...] - bias_ref[...] - gain_ref[:, 1:2]
    one = jnp.sum(grad * gain_ref[:, 0:1], axis=0, keepdims=True) + sums_ref[0:1, :]
    two = jnp.sum(grad * centred, axis=0, keepdims=True) + sums_ref[1:2, :]
    row = lax.broadcasted_iota(jnp.int32, (16, grad.shape[1]), 0)
    one_high = one.astype(jnp.bfloat16).astype(jnp.float32)
    two_high = two.astype(jnp.bfloat16).astype(jnp.float32)
    tail = jnp.where(row == 0, one_high, jnp.where(row == 1, one - one_high, 0.0))
    tail = jnp.where(row == 2, two_high, jnp.where(row == 3, two - two_high, tail))
    payload_ref[count:, :] = tail.astype(jnp.bfloat16)
    part = jnp.sum(grad, axis=1, keepdims=True)

    @pl.when(pl.program_id(0) == 0)
    def _():
        bias_grad_ref[...] = jnp.zeros_like(bias_grad_ref)

    bias_grad_ref[...] += part


def run_payload(grad, slope, before, gain, bias, sums):
    count, rows = grad.shape
    step = 512

    def columns(lines):
        return pl.BlockSpec((lines, step), lambda i: (0, i))

    def fixed(*shape):
        return pl.BlockSpec(shape, lambda i: (0, 0))

    return pl.pallas_call(
        payload_kernel,
        grid=(rows // step,),
        in_specs=[columns(count)] * 3 + [fixed(count, 2), fixed(count, 1), columns(8)],
        out_specs=[columns(count + 16), fixed(count, 1)],
        out_shape=[
            jax.ShapeDtypeStruct((count + 16, rows), jnp.bfloat16),
            jax.ShapeDtypeStruct((count, 1), jnp.float32),
        ],
        cost_estimate=cost(3),
    )(grad, slope, before, gain, bias[:, None], sums)


def final_kernel(
    place_ref,
    own_ref,
    near_ref,
    far_ref,
    last_ref,
    rows_ref,
    kept_ref,
    sent_ref,
    passed_ref,
    tokens_ref,
    stats_ref,
    grad_ref,
    gain_ref,
    input_grad_ref,
    gain_grad_ref,
    shift_grad_ref,
    down_grad_ref,
):
    place = place_ref[0]
    size = own_ref.shape[0] - 16
    row = lax.broadcasted_iota(jnp.int32, (16, 256), 0)
    lane = lax.broadcasted_iota(jnp.int32, (16, 256), 1)
    pick = jnp.where((row < 2) == (lane < 128), 1.0, 0.0)
    pick = jnp.where(row < 4, pick, 0.0).astype(jnp.bfloat16)
    normed_grad = (
        kept_ref[0].astype(jnp.float32)
        + sent_ref[0].astype(jnp.float32)
        + passed_ref[...].astype(jnp.float32)
    )
    totals = jnp.zeros((normed_grad.shape[0], 256), jnp.float32)
    for offset, piece in enumerate((own_ref, near_ref, far_ref, last_ref)):
        start = pl.multiple_of((place ^ offset) * size, size)
        normed_grad += dot(piece[:size, :], rows_ref[pl.ds(start, size), :], 0, 0)
        totals += dot(piece[size:, :], pick, 0, 0)
    scaled = normed_grad * gain_ref[...]
    centred = (tokens_ref[...].astype(jnp.float32) - stats_ref[:, 0:1]) * stats_ref[:, 64:65]
    grad = grad_ref[...].astype(jnp.float32)
    mean_one = totals[:, 0:1] * (1.0 / D)
    mean_two = totals[:, 128:129] * (1.0 / D)
    input_grad_ref[...] = stats_ref[:, 64:65] * (scaled - mean_one - centred * mean_two) + grad

    @pl.when(pl.program_id(0) == 0)
    def _():
        gain_grad_ref[...] = jnp.zeros_like(gain_grad_ref)
        shift_grad_ref[...] = jnp.zeros_like(shift_grad_ref)
        down_grad_ref[...] = jnp.zeros_like(down_grad_ref)

    gain_grad_ref[...] += jnp.sum(normed_grad * centred, axis=0, keepdims=True)
    shift_grad_ref[...] += jnp.sum(normed_grad, axis=0, keepdims=True)
    down_grad_ref[...] += jnp.sum(grad, axis=0, keepdims=True)


def run_final(parts, input_rows, kept, sent, passed, tokens, stats, grad, gain):
    rows, width = tokens.shape
    lines = parts[0].shape[0]
    step = 256
    place = lax.axis_index("chan").astype(jnp.int32).reshape(1)

    def fixed(*shape):
        return pl.BlockSpec(shape, lambda i, p: (0, 0))

    def rowwise(columns):
        return pl.BlockSpec((step, columns), lambda i, p: (i, 0))

    def columns(count):
        return pl.BlockSpec((count, step), lambda i, p: (0, i))

    piece = pl.BlockSpec((1, step, width), lambda i, p: (0, i, 0))
    return pl.pallas_call(
        final_kernel,
        grid_spec=pltpu.PrefetchScalarGridSpec(
            num_scalar_prefetch=1,
            grid=(rows // step,),
            in_specs=[columns(lines)] * 4
            + [
                fixed(*input_rows.shape),
                piece,
                piece,
                rowwise(width),
                rowwise(width),
                rowwise(128),
                pl.BlockSpec((step, width), lambda i, p: (i, p[0])),
                fixed(1, width),
            ],
            out_specs=[rowwise(width)] + [fixed(1, width)] * 3,
        ),
        out_shape=[jax.ShapeDtypeStruct((rows, width), jnp.float32)]
        + [jax.ShapeDtypeStruct((1, width), jnp.float32)] * 3,
        cost_estimate=cost(6),
    )(place, *parts, input_rows, kept, sent, passed, tokens, stats, grad, gain[None])


def grads_kernel(
    side_ref,
    outer_ref,
    normed_ref,
    mixed_ref,
    hidden_ref,
    up_ref,
    lifted_ref,
    down_send_ref,
    down_keep_ref,
    rest_send_ref,
    rest_keep_ref,
):
    turn = pl.program_id(0)
    half = pl.num_programs(0) // 2
    rows = outer_ref.shape[1]
    down = dot(outer_ref[...], hidden_ref[...], 0, 0).astype(jnp.bfloat16)
    up = dot(normed_ref[...], up_ref[...], 0, 0).astype(jnp.bfloat16)
    mix = dot(mixed_ref[...], lifted_ref[...], 1, 0).astype(jnp.bfloat16)

    def write(down_ref, rest_ref):
        down_ref[0] = down
        rest_ref[0, :rows, :] = up
        rest_ref[0, rows:, :] = mix

    pl.when(turn < half)(lambda: write(down_send_ref, rest_send_ref))
    pl.when(turn >= half)(lambda: write(down_keep_ref, rest_keep_ref))


def run_grads(outer, normed, mixed, hidden, up, lifted):
    rows, full = outer.shape
    channels = mixed.shape[0]
    units = hidden.shape[1]
    devices = lax.axis_size("seq")
    half = devices // 2
    part, mix_part = full // devices, channels // devices
    side = (lax.axis_index("seq") & 1).astype(jnp.int32).reshape(1)

    def target(i, p):
        return 2 * (i % half) + jnp.where(i < half, 1 - p[0], p[0])

    def fixed(*shape):
        return pl.BlockSpec(shape, lambda i, p: (0, 0))

    sent = lambda i, p: (jnp.minimum(i, half - 1), 0, 0)
    kept = lambda i, p: (jnp.maximum(i - half, 0), 0, 0)
    whole = part + mix_part
    return pl.pallas_call(
        grads_kernel,
        grid_spec=pltpu.PrefetchScalarGridSpec(
            num_scalar_prefetch=1,
            grid=(devices,),
            in_specs=[
                pl.BlockSpec((rows, part), lambda i, p: (0, target(i, p))),
                pl.BlockSpec((rows, part), lambda i, p: (0, target(i, p))),
                pl.BlockSpec((mix_part, rows), lambda i, p: (target(i, p), 0)),
                fixed(rows, units),
                fixed(rows, units),
                fixed(rows, units),
            ],
            out_specs=[
                pl.BlockSpec((1, part, units), sent),
                pl.BlockSpec((1, part, units), kept),
                pl.BlockSpec((1, whole, units), sent),
                pl.BlockSpec((1, whole, units), kept),
            ],
        ),
        out_shape=[jax.ShapeDtypeStruct((half, part, units), jnp.bfloat16)] * 2
        + [jax.ShapeDtypeStruct((half, whole, units), jnp.bfloat16)] * 2,
        compiler_params=pltpu.CompilerParams(vmem_limit_bytes=VMEM),
        cost_estimate=cost(14),
    )(side, outer, normed, mixed, hidden, up, lifted)


def swap(value, distance):
    return lax.ppermute(value, "chan", [(i, i ^ distance) for i in range(4)])


def gather_parts(piece):
    far = swap(piece, 2)
    return piece, swap(piece, 1), far, swap(far, 1)


def after(value, *others):
    return lax.optimization_barrier((value,) + others)[0]


def to_channels(value, sequences):
    devices = lax.axis_size("seq")
    channels, tokens = value.shape
    share = channels // devices
    got = lax.all_to_all(value.reshape(devices, share, tokens), "seq", 0, 0, tiled=True)
    got = got.reshape(sequences, devices // sequences, share, tokens)
    return got.transpose(1, 0, 2, 3).reshape(devices // sequences, sequences * share, tokens)


def to_tokens(value, sequences):
    devices = lax.axis_size("seq")
    sources, count, tokens = value.shape
    share = count // sequences
    sent = value.reshape(sources, sequences, share, tokens).transpose(1, 0, 2, 3)
    got = lax.all_to_all(sent.reshape(devices, share, tokens), "seq", 0, 0, tiled=True)
    return got.reshape(devices * share, tokens)


def tile_rows(flat):
    width = flat.shape[-1]
    padded = -(-width // 128) * 128
    flat = jnp.pad(flat, [(0, 0)] * (flat.ndim - 1) + [(0, padded - width)])
    return flat.reshape(flat.shape[:-1] + (padded // 128, 128))


def planes(value, count):
    parts = []
    for _ in range(count):
        part = lax.reduce_precision(value, 8, 7)
        parts.append(part.astype(jnp.bfloat16))
        value = value - part
    return parts


def plain_grads(outer, normed, mixed, hidden, up, lifted):
    devices = lax.axis_size("seq")
    side = lax.axis_index("seq") & 1

    def parts(value):
        value = value.astype(jnp.bfloat16)
        return value.reshape(devices // 2, 2, value.shape[0] // devices, value.shape[1])

    def pick(value, index):
        return lax.dynamic_index_in_dim(value, index, 1, False)

    down = parts(dot(outer, hidden, 0, 0))
    rest = (parts(dot(normed, up, 0, 0)), parts(dot(mixed, lifted, 1, 0)))
    rest = jnp.concatenate(rest, axis=2)
    return (pick(down, 1 - side), pick(down, side), pick(rest, 1 - side), pick(rest, side))


def halve(sent, kept):
    devices = lax.axis_size("seq")
    got = lax.ppermute(sent, "seq", [(i, i ^ 1) for i in range(devices)])
    return (kept.astype(jnp.float32) + got.astype(jnp.float32)).astype(jnp.bfloat16)


def settle(halves):
    devices = lax.axis_size("seq")
    groups = [[i for i in range(devices) if i & 1 == side] for side in (0, 1)]
    got = lax.all_to_all(halves, "seq", 0, 0, axis_index_groups=groups, tiled=True)
    return jnp.sum(got.astype(jnp.float32), axis=0)


def per_device(
    tokens,
    norm_gain,
    norm_shift,
    up_weight,
    up_bias,
    input_weight,
    input_bias,
    mix_weight,
    mix_bias,
    down_weight,
    down_bias,
    decay_rate,
    decay_freq,
    step_log,
    read_real,
    read_imag,
    skip_gain,
    out_grad,
):
    row_count, width = tokens.shape
    devices = lax.axis_size("seq")
    place = lax.axis_index("chan")
    sequences = devices * row_count // LENGTH
    feature_rows, channels = input_weight.shape
    units = up_weight.shape[1]
    share = channels // devices
    modes_here = decay_rate.shape[0]
    modes = modes_here * devices
    token_parts = gather_parts(tokens)

    pair = jnp.stack([norm_gain, norm_shift])
    pairs = jnp.stack([pair, swap(pair, 1), swap(pair, 2), swap(pair, 3)])
    pairs = jnp.stack([pairs[place ^ i] for i in range(4)])
    small = (pairs.reshape(-1), up_bias, input_bias, mix_bias, down_bias, decay_rate, decay_freq)
    sizes = [v.shape[0] for v in small]
    small = tile_rows(jnp.concatenate(small))
    reads = jnp.concatenate([read_real, read_imag], axis=1).reshape(devices, share, 2 * modes_here)
    reads = jnp.pad(reads, ((0, 0), (0, 0), (0, 128 - 2 * modes_here)))
    copies = jnp.broadcast_to(small, (devices,) + small.shape)
    exact = jnp.concatenate([reads, copies], axis=1)
    exact_rows = exact.shape[1]
    weights = jnp.broadcast_to(input_weight, (devices,) + input_weight.shape)
    got = jnp.concatenate(planes(exact, 3) + [weights], axis=1)
    got = lax.all_to_all(got, "seq", 0, 0, tiled=True)
    input_full = got[:, 3 * exact_rows :].reshape(4 * width, channels).T
    got = got.astype(jnp.float32)
    got = got[:, :exact_rows] + (
        got[:, exact_rows : 2 * exact_rows] + got[:, 2 * exact_rows : 3 * exact_rows]
    )
    reads = got[:, :share, : 2 * modes_here].transpose(1, 0, 2)
    read_re = reads[:, :, :modes_here].reshape(share, modes)
    read_im = reads[:, :, modes_here:].reshape(share, modes)
    small = got[:, share:].reshape(devices, -1)
    parts, spot = [], 0
    for size in sizes:
        parts.append(small[:, spot : spot + size])
        spot += size
    affine = parts[0].reshape(devices, 4, 2, -1).transpose(2, 1, 0, 3).reshape(2, 4 * width)
    up_shift, input_shift, mix_shift, down_shift, rate, freq = (p.reshape(-1) for p in parts[1:])
    gain_own = lax.dynamic_slice_in_dim(affine[0], place * width, width)

    mix_rows = mix_weight.shape[0]
    fronts = jnp.concatenate([up_weight, down_weight.T, mix_weight])
    fronts = lax.all_gather(fronts, "seq", axis=0)
    up_full = fronts[:, :feature_rows].reshape(4 * width, units)
    down_full = fronts[:, feature_rows : 2 * feature_rows].reshape(4 * width, units)
    mix_full = fronts[:, 2 * feature_rows :].reshape(devices * mix_rows, units)

    spacing = jnp.exp(step_log)
    damping = spacing[:, None] * rate[None, :]
    rotation = spacing[:, None] * freq[None, :]
    inflow = -jnp.expm1(-damping)
    extents = 2.0 ** jnp.arange(8)[None, :, None]
    length = jnp.exp(-damping[:, None] * extents)
    angle = rotation[:, None] * extents
    power_re, power_im = length * jnp.cos(angle), length * jnp.sin(angle)

    def repeat(value):
        return jnp.tile(value, (sequences,) + (1,) * (value.ndim - 1))

    def rows(value_re, value_im):
        return repeat(jnp.concatenate([value_re, value_im], axis=1)[:, None])

    power, out_table, in_table, toeplitz = make_tables(
        repeat(power_re), repeat(power_im), repeat(read_re), repeat(read_im), repeat(inflow)
    )
    jump = rows(power_re[:, 7], power_im[:, 7])[:, 0]
    flow = rows(inflow, inflow)
    lead = rows(*cmul(read_re, read_im, power_re[:, 0], power_im[:, 0]))
    skip = repeat(skip_gain)

    normed, values_low, in_slope, pre_in, stats = run_norm(
        token_parts, affine, input_full, input_shift
    )
    values = to_channels(values_low, sequences)
    mixed, starts, values_split = run_forward(
        values, skip, jump, flow, lead, out_table, in_table, toeplitz
    )
    mixed_tokens = to_tokens(mixed, sequences)

    upper, up_slope, lifted_grad, channel_keep, channel_send, mix_bias_part = run_gate(
        after(normed, mixed), out_grad, up_full, down_full, mix_full, up_shift
    )
    channel_sent = swap(after(channel_send, mixed_tokens), 1)
    mixed_parts = gather_parts(mixed_tokens)
    channel_passed = (channel_keep[1] + channel_sent[1]).astype(jnp.bfloat16)
    channel_sum = channel_keep[0] + channel_sent[0]
    mixed_grad = (channel_sum + swap(channel_passed, 2).astype(jnp.float32)).astype(jnp.bfloat16)
    grads = to_channels(mixed_grad, sequences)

    (
        mixed_full,
        hidden,
        up_pre_grad,
        out_keep,
        out_send,
        feature_keep,
        feature_send,
        up_sums,
        up_bias_part,
    ) = run_mid(
        (after(mixed_parts[0], channel_passed),) + mixed_parts[1:],
        upper,
        up_slope,
        normed,
        mix_full,
        down_full,
        up_full,
        mix_shift,
        affine,
    )
    out_sent, feature_sent = swap(out_send, 1), swap(feature_send, 1)

    def passed(keep, sent):
        return (keep[1].astype(jnp.float32) + sent[1].astype(jnp.float32)).astype(jnp.bfloat16)

    feature_passed = passed(feature_keep, feature_sent)
    out_passed = passed(out_keep, out_sent)
    make_grads = run_grads if feature_rows % 128 == 0 else plain_grads
    down_send, down_keep, rest_send, rest_keep = make_grads(
        out_grad, normed, mixed_full, hidden, up_pre_grad, lifted_grad
    )
    down_half = halve(down_send, down_keep)
    rest_half = halve(rest_send, rest_keep)

    grads = after(grads, feature_passed, out_passed, down_half, rest_half)
    feature_far, out_far = swap(feature_passed, 2), swap(out_passed, 2)
    down_weight_grad = settle(down_half)
    values_grad, later, grads_split = run_backward(
        grads, skip, jump, flow, lead, out_table, in_table, toeplitz
    )
    later = after(later, down_weight_grad, feature_far, out_far)
    values_back = to_tokens(after(values_grad, down_weight_grad), sequences)
    sums, skip_sums = run_sums(grads_split, values_split, starts, later, power)
    down_weight_grad = down_weight_grad.T
    up_mix = settle(after(rest_half, values_back))
    up_weight_grad, mix_weight_grad = up_mix[:feature_rows], up_mix[feature_rows:]
    inputs = tokens.astype(jnp.float32)
    output = (
        out_keep[0].astype(jnp.float32)
        + out_sent[0].astype(jnp.float32)
        + out_far.astype(jnp.float32)
        + down_shift
        + inputs
    )

    in_gain = jnp.dot(input_full.astype(jnp.float32), affine.T, precision=lax.Precision.HIGHEST)
    payload, input_bias_part = run_payload(
        after(values_back, sums), in_slope, pre_in, in_gain, input_shift, up_sums
    )
    payload_parts = gather_parts(payload)
    input_part = dot(normed, payload[:channels], 0, 1)
    pieces = gather_parts(input_full)
    pieces = [lax.dynamic_slice_in_dim(p, place * width, width, 1) for p in pieces]
    pieces = jnp.stack(pieces)
    input_rows = jnp.concatenate([pieces[place ^ i] for i in range(4)])
    input_grad, gain_part, shift_part, down_bias_part = run_final(
        payload_parts,
        input_rows,
        feature_keep,
        feature_sent,
        feature_far,
        tokens,
        stats,
        out_grad,
        gain_own,
    )

    sums = jnp.concatenate([sums[:, :4], sums[:, 4:8] * flow[:, :, :modes], sums[:, 8:]], axis=1)
    sums = jnp.sum(sums.reshape((sequences, share) + sums.shape[1:]), axis=0)
    skip_grad = jnp.sum(skip_sums.reshape(sequences, share, BLOCK), axis=(0, 2))
    out_zero = cmul(power_re[:, 0], power_im[:, 0], sums[:, 0], sums[:, 1])
    out_one = cmul(
        power_re[:, 0], power_im[:, 0], sums[:, 0] + sums[:, 2], sums[:, 1] + sums[:, 3]
    )
    chained = cmul(power_re[:, 7], power_im[:, 7], sums[:, 8], sums[:, 9])
    local_zero, local_one = (sums[:, 10], sums[:, 11]), (sums[:, 12], sums[:, 13])
    read_re_grad = out_zero[0] + inflow * local_zero[0]
    read_im_grad = -out_zero[1] - inflow * local_zero[1]
    turn = cmul(
        read_re, read_im, out_one[0] + inflow * local_one[0], out_one[1] + inflow * local_one[1]
    )
    turn_re = turn[0] + sums[:, 6] + BLOCK * chained[0]
    turn_im = turn[1] + sums[:, 7] + BLOCK * chained[1]
    inflow_grad = sums[:, 4] / inflow + read_re * local_zero[0] - read_im * local_zero[1]
    damping_grad = jnp.exp(-damping) * inflow_grad - turn_re
    rotation_grad = -turn_im
    step_log_grad = spacing * jnp.sum(
        rate[None, :] * damping_grad + freq[None, :] * rotation_grad, axis=1
    )
    rates = jnp.stack(
        [
            jnp.sum(spacing[:, None] * damping_grad, axis=0),
            jnp.sum(spacing[:, None] * rotation_grad, axis=0),
        ]
    )
    rates = rates + swap(rates, 1)
    rates = rates + swap(rates, 2)

    read_grads = jnp.stack([read_re_grad, read_im_grad], axis=1)
    read_grads = read_grads.reshape(share, 2, devices, modes_here).transpose(2, 0, 1, 3)
    read_grads = read_grads.reshape(devices, share, 2 * modes_here)
    read_grads = jnp.pad(read_grads, ((0, 0), (0, 0), (0, 128 - 2 * modes_here)))
    vectors = (
        gain_part,
        shift_part,
        up_bias_part,
        input_bias_part,
        mix_bias_part,
        down_bias_part,
        rates[0],
        rates[1],
    )
    vectors = [v.reshape(devices, -1) for v in vectors]
    sizes = [v.shape[1] for v in vectors]
    vectors = tile_rows(jnp.concatenate(vectors, axis=1))
    input_part = input_part.reshape(devices, feature_rows, channels)
    parcel = jnp.concatenate([read_grads, vectors], axis=1)
    exact_rows = parcel.shape[1]
    parcel = jnp.concatenate(planes(parcel, 2) + [input_part.astype(jnp.bfloat16)], axis=1)
    late = lax.all_to_all(parcel, "seq", 0, 0, tiled=True).astype(jnp.float32)
    input_weight_grad = jnp.sum(late[:, 2 * exact_rows :], axis=0)
    late = late[:, :exact_rows] + late[:, exact_rows : 2 * exact_rows]
    read_late = late[:, :share, : 2 * modes_here].reshape(channels, 2 * modes_here)
    flat = jnp.sum(late[:, share:], axis=0).reshape(-1)
    parts, spot = [], 0
    for size in sizes:
        parts.append(flat[spot : spot + size])
        spot += size
    gain_grad, shift_grad, up_bias_grad, input_bias_grad = parts[:4]
    mix_bias_grad, down_bias_grad, rate_out, freq_out = parts[4:]
    return (
        output,
        input_grad,
        gain_grad,
        shift_grad,
        up_weight_grad,
        up_bias_grad,
        input_weight_grad,
        input_bias_grad,
        mix_weight_grad,
        mix_bias_grad,
        down_weight_grad,
        down_bias_grad,
        rate_out,
        freq_out,
        step_log_grad,
        read_late[:, :modes_here],
        read_late[:, modes_here:],
        skip_grad,
    )


def solution(mesh):
    return jax.shard_map(
        per_device,
        mesh=mesh,
        in_specs=(
            P("seq", "chan"),
            P(("chan", "seq")),
            P(("chan", "seq")),
            P("seq", "chan"),
            P(("chan", "seq")),
            P("seq", "chan"),
            P(("chan", "seq")),
            P("seq", "chan"),
            P(("chan", "seq")),
            P("chan", "seq"),
            P(("chan", "seq")),
            P("seq"),
            P("seq"),
            P(("chan", "seq")),
            P("chan", "seq"),
            P("chan", "seq"),
            P(("chan", "seq")),
            P("seq", None),
        ),
        out_specs=(
            P("seq", "chan"),
            P("seq", "chan"),
            P(("chan", "seq")),
            P(("chan", "seq")),
            P("seq", "chan"),
            P(("chan", "seq")),
            P("seq", "chan"),
            P(("chan", "seq")),
            P("seq", "chan"),
            P(("chan", "seq")),
            P("chan", "seq"),
            P(("chan", "seq")),
            P("seq"),
            P("seq"),
            P(("chan", "seq")),
            P("chan", "seq"),
            P("chan", "seq"),
            P(("chan", "seq")),
        ),
        check_vma=False,
    )
```

```python
from functools import partial
import math

import jax
import jax.numpy as jnp
from jax import lax
from jax.experimental import pallas as pl
from jax.experimental.pallas import tpu as pltpu
from jax.sharding import PartitionSpec as P

D = 1024
LENGTH = 16384
EPSILON = 1e-05


BLOCK = 128
VMEM = 56 * 1024 * 1024


def dot(left, right, left_dim, right_dim):
    return lax.dot_general(
        left, right, (((left_dim,), (right_dim,)), ((), ())), preferred_element_type=jnp.float32
    )


def cmul(a_re, a_im, b_re, b_im):
    return (a_re * b_re - a_im * b_im, a_re * b_im + a_im * b_re)


def grow(first, reversed_rows, mode_powers, store):
    row = lax.broadcasted_iota(jnp.int32, (8, first[0].shape[1]), 0)
    exponent = 7 - row if reversed_rows else row
    part = (
        jnp.broadcast_to(first[0], row.shape),
        jnp.broadcast_to(first[1], row.shape),
    )
    for level in range(3):
        factor_re, factor_im = mode_powers(level)
        taken = (exponent >> level) & 1 == 1
        part = cmul(*part, jnp.where(taken, factor_re, 1.0), jnp.where(taken, factor_im, 0.0))
    spot = BLOCK - 8 if reversed_rows else 0
    store(spot, part[0], part[1])
    whole = part
    size, level = 8, 3
    while size < BLOCK:
        factor = mode_powers(level)
        fresh = cmul(*whole, *factor)
        spot = BLOCK - 2 * size if reversed_rows else size
        store(spot, *fresh)
        pair = (fresh, whole) if reversed_rows else (whole, fresh)
        whole = tuple(jnp.concatenate([p, q], axis=0) for p, q in zip(*pair))
        size, level = 2 * size, level + 1


def tables_kernel(
    power_re_ref,
    power_im_ref,
    read_re_ref,
    read_im_ref,
    inflow_ref,
    power_ref,
    out_table_ref,
    in_table_ref,
    toeplitz_ref,
):
    modes = power_re_ref.shape[2]
    lower, upper = slice(0, modes), slice(modes, 2 * modes)

    def mode_powers(level):
        return (power_re_ref[0, level : level + 1, :], power_im_ref[0, level : level + 1, :])

    inflow = inflow_ref[0]
    one, none = jnp.ones_like(inflow), jnp.zeros_like(inflow)

    def store_power(spot, part_re, part_im):
        rows = slice(spot, spot + part_re.shape[0])
        power_ref[0, rows, lower] = part_re
        power_ref[0, rows, upper] = part_im

    grow((one, none), False, mode_powers, store_power)
    exact = jnp.concatenate([power_ref[0, :, lower], -power_ref[0, :, upper]], axis=1)
    rounded = exact.astype(jnp.bfloat16)
    out_table_ref[0] = rounded
    rest = (exact - rounded.astype(jnp.float32)).astype(jnp.bfloat16)
    backward = []

    def store_in(spot, part_re, part_im):
        backward.append((spot, part_re, part_im))

    grow((one, none), True, mode_powers, store_in)
    backward.sort(key=lambda entry: entry[0])
    in_table_ref[0, :, lower] = jnp.concatenate([e[1] for e in backward], 0).astype(jnp.bfloat16)
    in_table_ref[0, :, upper] = jnp.concatenate([e[2] for e in backward], 0).astype(jnp.bfloat16)
    weight = jnp.concatenate([read_re_ref[0] * inflow, read_im_ref[0] * inflow], axis=1)
    high = weight.astype(jnp.bfloat16).astype(jnp.float32)
    row = lax.broadcasted_iota(jnp.int32, (16, 2 * modes), 0)
    probe = jnp.where(row == 0, high, jnp.where(row == 1, weight - high, 0.0))
    probe = probe.astype(jnp.bfloat16)
    lags = dot(probe, rounded, 1, 1) + dot(probe, rest, 1, 1)
    kernel_row = jnp.sum(lags, axis=0, keepdims=True)
    skewed = pltpu.roll(
        jnp.broadcast_to(kernel_row, (BLOCK, BLOCK)), 0, 1, stride=1, stride_axis=0
    )
    source = lax.broadcasted_iota(jnp.int32, (BLOCK, BLOCK), 0)
    target = lax.broadcasted_iota(jnp.int32, (BLOCK, BLOCK), 1)
    skewed = jnp.where(target >= source, skewed, 0.0)
    coarse = skewed.astype(jnp.bfloat16)
    toeplitz_ref[0, :BLOCK, :] = coarse
    toeplitz_ref[0, BLOCK:, :] = (skewed - coarse.astype(jnp.float32)).astype(jnp.bfloat16)


def make_tables(power_re, power_im, read_re, read_im, inflow):
    count, levels, modes = power_re.shape

    def spec(*shape):
        return pl.BlockSpec((1,) + shape, lambda i: (i, 0, 0))

    return pl.pallas_call(
        tables_kernel,
        grid=(count,),
        in_specs=[spec(levels, modes)] * 2 + [spec(1, modes)] * 3,
        out_specs=[
            spec(BLOCK, 2 * modes),
            spec(BLOCK, 2 * modes),
            spec(BLOCK, 2 * modes),
            spec(2 * BLOCK, BLOCK),
        ],
        out_shape=[
            jax.ShapeDtypeStruct((count, BLOCK, 2 * modes), jnp.float32),
            jax.ShapeDtypeStruct((count, BLOCK, 2 * modes), jnp.bfloat16),
            jax.ShapeDtypeStruct((count, BLOCK, 2 * modes), jnp.bfloat16),
            jax.ShapeDtypeStruct((count, 2 * BLOCK, BLOCK), jnp.bfloat16),
        ],
        compiler_params=pltpu.CompilerParams(vmem_limit_bytes=VMEM),
        cost_estimate=cost(12),
    )(power_re, power_im, read_re[:, None], read_im[:, None], inflow[:, None])


def spread_tokens(ref, scratch):
    sources, count, tokens = ref.shape
    per_source = tokens // BLOCK
    for source in range(sources):
        for part in range(per_source):
            row = (source * per_source + part) * count
            tile = ref[source, :, part * BLOCK : (part + 1) * BLOCK]
            scratch[row : row + count, :] = tile.astype(jnp.float32)


def gather_tokens(scratch, ref):
    sources, count, tokens = ref.shape
    per_source = tokens // BLOCK
    for source in range(sources):
        for part in range(per_source):
            row = (source * per_source + part) * count
            ref[source, :, part * BLOCK : (part + 1) * BLOCK] = scratch[
                row : row + count, :
            ].astype(ref.dtype)


def put_rows(states, rows, value):
    for tile in range(states.shape[0]):
        states[tile, rows, :] = value[:, tile * 128 : (tile + 1) * 128]


def take_rows(states, rows):
    return jnp.concatenate([states[tile, rows, :] for tile in range(states.shape[0])], axis=1)


def run_chain(states, jump_ref, sign, count, blocks, order):
    tiles = states.shape[0] // 2
    jumps = [
        (
            jump_ref[:, t * 128 : (t + 1) * 128],
            sign * jump_ref[:, (tiles + t) * 128 : (tiles + t + 1) * 128],
        )
        for t in range(tiles)
    ]

    def step(turn, state):
        rows = pl.ds(pl.multiple_of(order(turn) * count, count), count)
        following = []
        for t in range(tiles):
            end_re, end_im = states[t, rows, :], states[tiles + t, rows, :]
            states[t, rows, :] = state[t][0]
            states[tiles + t, rows, :] = state[t][1]
            next_re, next_im = cmul(*jumps[t], *state[t])
            following.append((next_re + end_re, next_im + end_im))
        return tuple(following)

    blank = jnp.zeros((count, 128), jnp.float32)
    lax.fori_loop(0, blocks, step, ((blank, blank),) * tiles, unroll=2)


def forward_kernel(
    values_ref,
    skip_ref,
    jump_ref,
    inflow_ref,
    lead_ref,
    out_table_ref,
    in_table_ref,
    toeplitz_ref,
    mixed_ref,
    starts_ref,
    split_ref,
    tokens,
    states,
):
    count = values_ref.shape[1]
    blocks = states.shape[1] // count
    modes = states.shape[0] * 64
    spread_tokens(values_ref, tokens)

    def rows_of(channel):
        return pl.ds(channel, blocks, stride=count)

    def enter(channel, carry):
        own = tokens[rows_of(channel), :].astype(jnp.bfloat16)
        split_ref[channel] = own
        ends = dot(own, in_table_ref[channel], 1, 0)
        put_rows(states, rows_of(channel), ends * inflow_ref[channel])
        return carry

    lax.fori_loop(0, count, enter, 0)
    run_chain(states, jump_ref, 1.0, count, blocks, lambda turn: turn)

    def leave(channel, carry):
        start = take_rows(states, rows_of(channel))
        starts_ref[channel] = start.astype(jnp.bfloat16)
        lead = lead_ref[channel]
        weighted = cmul(lead[:, :modes], lead[:, modes:], start[:, :modes], start[:, modes:])
        weighted = jnp.concatenate(weighted, axis=1).astype(jnp.bfloat16)
        own = tokens[rows_of(channel), :]
        own_low = own.astype(jnp.bfloat16)
        mixed = dot(weighted, out_table_ref[channel], 1, 1)
        mixed += dot(own_low, toeplitz_ref[channel, :BLOCK, :], 1, 0)
        mixed += dot(own_low, toeplitz_ref[channel, BLOCK:, :], 1, 0)
        tokens[rows_of(channel), :] = mixed + skip_ref[channel] * own
        return carry

    lax.fori_loop(0, count, leave, 0)
    gather_tokens(tokens, mixed_ref)


def run_forward(values, skip, jump, inflow, lead, out_table, in_table, toeplitz):
    sources, count, tokens = values.shape
    blocks = sources * tokens // BLOCK
    width = jump.shape[1]
    vmem = pl.BlockSpec(memory_space=pltpu.VMEM)
    return pl.pallas_call(
        forward_kernel,
        in_specs=[vmem, pl.BlockSpec(memory_space=pltpu.SMEM)] + [vmem] * 6,
        out_specs=[vmem] * 3,
        out_shape=[
            jax.ShapeDtypeStruct(values.shape, jnp.bfloat16),
            jax.ShapeDtypeStruct((count, blocks, width), jnp.bfloat16),
            jax.ShapeDtypeStruct((count, blocks, BLOCK), jnp.bfloat16),
        ],
        scratch_shapes=[
            pltpu.VMEM((blocks * count, BLOCK), jnp.float32),
            pltpu.VMEM((width // 128, blocks * count, 128), jnp.float32),
        ],
        compiler_params=pltpu.CompilerParams(vmem_limit_bytes=VMEM),
        cost_estimate=cost(20),
    )(values, skip, jump, inflow, lead, out_table, in_table, toeplitz)


def backward_kernel(
    grads_ref,
    skip_ref,
    jump_ref,
    inflow_ref,
    lead_ref,
    out_table_ref,
    in_table_ref,
    toeplitz_ref,
    values_grad_ref,
    later_ref,
    split_ref,
    grads,
    states,
):
    count = grads_ref.shape[1]
    blocks = states.shape[1] // count
    modes = states.shape[0] * 64
    spread_tokens(grads_ref, grads)

    def rows_of(channel):
        return pl.ds(channel, blocks, stride=count)

    def enter(channel, carry):
        own = grads[rows_of(channel), :].astype(jnp.bfloat16)
        split_ref[channel] = own
        lead = lead_ref[channel]
        back = dot(own, out_table_ref[channel], 1, 0)
        back = cmul(lead[:, :modes], -lead[:, modes:], back[:, :modes], back[:, modes:])
        put_rows(states, rows_of(channel), jnp.concatenate(back, axis=1))
        return carry

    lax.fori_loop(0, count, enter, 0)
    run_chain(states, jump_ref, -1.0, count, blocks, lambda turn: blocks - 1 - turn)

    def leave(channel, carry):
        later = take_rows(states, rows_of(channel))
        later_ref[channel] = later.astype(jnp.bfloat16)
        later = (later * inflow_ref[channel]).astype(jnp.bfloat16)
        grad = grads[rows_of(channel), :]
        grad_low = grad.astype(jnp.bfloat16)
        back = dot(later, in_table_ref[channel], 1, 1)
        back += dot(grad_low, toeplitz_ref[channel, :BLOCK, :], 1, 1)
        back += dot(grad_low, toeplitz_ref[channel, BLOCK:, :], 1, 1)
        grads[rows_of(channel), :] = back + skip_ref[channel] * grad
        return carry

    lax.fori_loop(0, count, leave, 0)
    gather_tokens(grads, values_grad_ref)


def run_backward(grads, skip, jump, inflow, lead, out_table, in_table, toeplitz):
    sources, count, tokens = grads.shape
    blocks = sources * tokens // BLOCK
    width = jump.shape[1]
    vmem = pl.BlockSpec(memory_space=pltpu.VMEM)
    return pl.pallas_call(
        backward_kernel,
        in_specs=[vmem, pl.BlockSpec(memory_space=pltpu.SMEM)] + [vmem] * 6,
        out_specs=[vmem] * 3,
        out_shape=[
            jax.ShapeDtypeStruct(grads.shape, jnp.bfloat16),
            jax.ShapeDtypeStruct((count, blocks, width), jnp.bfloat16),
            jax.ShapeDtypeStruct((count, blocks, BLOCK), jnp.bfloat16),
        ],
        scratch_shapes=[
            pltpu.VMEM((blocks * count, BLOCK), jnp.float32),
            pltpu.VMEM((width // 128, blocks * count, 128), jnp.float32),
        ],
        compiler_params=pltpu.CompilerParams(vmem_limit_bytes=VMEM),
        cost_estimate=cost(20),
    )(grads, skip, jump, inflow, lead, out_table, in_table, toeplitz)


def sums_kernel(grad_ref, value_ref, start_ref, later_ref, power_ref, sums_ref, skip_ref):
    modes = power_ref.shape[2] // 2
    row = lax.broadcasted_iota(jnp.int32, (BLOCK, BLOCK), 0)
    lane = lax.broadcasted_iota(jnp.int32, (BLOCK, BLOCK), 1)
    flip = jnp.where(row + lane == BLOCK - 1, 1.0, 0.0).astype(jnp.bfloat16)

    def fold(part):
        return jnp.sum(part.reshape(part.shape[0] // 8, 8, part.shape[1]), axis=0)

    grad, value = grad_ref[0], value_ref[0]
    start, later = start_ref[0], later_ref[0]
    product = grad.astype(jnp.float32) * value.astype(jnp.float32)
    skip_ref[0] = jnp.sum(product, axis=0, keepdims=True)
    turned = dot(value, flip, 1, 0).astype(jnp.bfloat16)
    out_sum = dot(grad, start, 0, 0)
    in_sum = dot(turned, later, 0, 0)
    cross = dot(grad, turned, 0, 0)
    cross = jnp.where(row + lane >= BLOCK - 1, cross, 0.0)
    lags = jnp.sum(pltpu.roll(cross, 1, 1, stride=1, stride_axis=0), axis=0, keepdims=True)
    lags = jnp.sum(jnp.where(row == lane, lags, 0.0), axis=1, keepdims=True)
    weight = lax.broadcasted_iota(jnp.int32, (BLOCK, modes), 0).astype(jnp.float32)
    power_re, power_im = power_ref[0, :, :modes], power_ref[0, :, modes:]
    terms = []
    for total, sign in ((out_sum, 1.0), (in_sum, -1.0)):
        term_re, term_im = cmul(power_re, power_im, total[:, :modes], sign * total[:, modes:])
        terms += [fold(term_re), fold(term_im), fold(weight * term_re), fold(weight * term_im)]
    later_re, later_im = (later[:, :modes].astype(jnp.float32), later[:, modes:].astype(jnp.float32))
    start_re, start_im = (start[:, :modes].astype(jnp.float32), start[:, modes:].astype(jnp.float32))
    terms += [
        fold(later_re * start_re + later_im * start_im),
        fold(later_re * start_im - later_im * start_re),
    ]
    local_re, local_im = power_re * lags, power_im * lags
    terms += [fold(local_re), fold(local_im), fold(weight * local_re), fold(weight * local_im)]
    for index, term in enumerate(terms):
        sums_ref[0, index : index + 1, :] = jnp.sum(term, axis=0, keepdims=True)


def run_sums(grads, values, starts, later, power):
    count, blocks, width = starts.shape

    def spec(*shape):
        return pl.BlockSpec((1,) + shape, lambda i: (i, 0, 0))

    return pl.pallas_call(
        sums_kernel,
        grid=(count,),
        in_specs=[spec(blocks, BLOCK)] * 2 + [spec(blocks, width)] * 2 + [spec(BLOCK, width)],
        out_specs=[spec(16, width // 2), spec(1, BLOCK)],
        out_shape=[
            jax.ShapeDtypeStruct((count, 16, width // 2), jnp.float32),
            jax.ShapeDtypeStruct((count, 1, BLOCK), jnp.float32),
        ],
        compiler_params=pltpu.CompilerParams(vmem_limit_bytes=VMEM),
        cost_estimate=cost(18),
    )(grads, values, starts, later, power)


def cost(microseconds):
    return pl.CostEstimate(
        flops=int(microseconds * 1e9), bytes_accessed=int(microseconds * 1e6), transcendentals=0
    )


def erf_parts(value):
    half = 0.5 * (1.0 + lax.erf(value * (1.0 / math.sqrt(2.0))))
    density = jnp.exp(-0.5 * value * value) * (1.0 / math.sqrt(2.0 * math.pi))
    return value * half, half + value * density


def norm_kernel(
    early_steps,
    place_ref,
    own_ref,
    near_ref,
    far_ref,
    far_late_ref,
    last_ref,
    last_late_ref,
    affine_ref,
    weight_ref,
    bias_ref,
    normed_ref,
    values_ref,
    slope_ref,
    before_ref,
    stats_ref,
    whole,
):
    place = place_ref[0]
    width = own_ref.shape[1]
    early = pl.program_id(0) < early_steps
    parts = (
        own_ref[...],
        near_ref[...],
        jnp.where(early, far_ref[...], far_late_ref[...]),
        jnp.where(early, last_ref[...], last_late_ref[...]),
    )
    for offset, part in enumerate(parts):
        start = pl.multiple_of((place ^ offset) * width, width)
        whole[:, pl.ds(start, width)] = part.astype(jnp.float32)
    inputs = whole[...]
    average = jnp.mean(inputs, axis=1, keepdims=True)
    spread = jnp.mean(inputs * inputs, axis=1, keepdims=True) - average * average
    inverse = lax.rsqrt(spread + EPSILON)
    normed = (inputs - average) * inverse * affine_ref[0:1, :] + affine_ref[1:2, :]
    normed = normed.astype(jnp.bfloat16)
    normed_ref[...] = normed
    before = dot(weight_ref[...], normed, 0, 1) + bias_ref[...]
    values, slope = erf_parts(before)
    values_ref[...] = values.astype(jnp.bfloat16)
    slope_ref[...] = slope
    before_ref[...] = before
    lane = lax.broadcasted_iota(jnp.int32, (inputs.shape[0], 128), 1)
    stats_ref[...] = jnp.where(lane < 64, average, inverse)


def run_norm(parts, affine, weight, bias):
    rows, width = parts[0].shape
    full, channels = weight.shape
    step = 256
    place = lax.axis_index("chan").astype(jnp.int32).reshape(1)
    half = parts[2].shape[0] // step
    full_rows = pl.BlockSpec((step, width), lambda i, p: (i, 0))
    first_rows = pl.BlockSpec((step, width), lambda i, p: (jnp.minimum(i, half - 1), 0))
    later_rows = pl.BlockSpec((step, width), lambda i, p: (jnp.maximum(i - half, 0), 0))
    return pl.pallas_call(
        partial(norm_kernel, half),
        grid_spec=pltpu.PrefetchScalarGridSpec(
            num_scalar_prefetch=1,
            grid=(rows // step,),
            in_specs=[
                full_rows,
                full_rows,
                first_rows,
                later_rows,
                first_rows,
                later_rows,
                pl.BlockSpec((2, full), lambda i, p: (0, 0)),
                pl.BlockSpec((full, channels), lambda i, p: (0, 0)),
                pl.BlockSpec((channels, 1), lambda i, p: (0, 0)),
            ],
            out_specs=[
                pl.BlockSpec((step, full), lambda i, p: (i, 0)),
                pl.BlockSpec((channels, step), lambda i, p: (0, i)),
                pl.BlockSpec((channels, step), lambda i, p: (0, i)),
                pl.BlockSpec((channels, step), lambda i, p: (0, i)),
                pl.BlockSpec((step, 128), lambda i, p: (i, 0)),
            ],
            scratch_shapes=[pltpu.VMEM((step, full), jnp.float32)],
        ),
        out_shape=[
            jax.ShapeDtypeStruct((rows, full), jnp.bfloat16),
            jax.ShapeDtypeStruct((channels, rows), jnp.bfloat16),
            jax.ShapeDtypeStruct((channels, rows), jnp.float32),
            jax.ShapeDtypeStruct((channels, rows), jnp.float32),
            jax.ShapeDtypeStruct((rows, 128), jnp.float32),
        ],
        compiler_params=pltpu.CompilerParams(vmem_limit_bytes=VMEM),
        cost_estimate=cost(8),
    )(place, *parts, affine, weight, bias[:, None])


def gate_kernel(
    place_ref,
    normed_ref,
    grad_ref,
    fronts_ref,
    bias_ref,
    upper_ref,
    slope_ref,
    lifted_grad_ref,
    keep_ref,
    send_ref,
    bias_grad_ref,
    up_ref,
    down_ref,
    mix_ref,
):
    place = place_ref[0]
    size = keep_ref.shape[1]
    unpack_fronts(fronts_ref, up_ref, down_ref, mix_ref)
    before = dot(normed_ref[...], up_ref[...], 1, 0) + bias_ref[...]
    hidden_grad = dot(grad_ref[...], down_ref[...], 1, 0)
    upper, slope = erf_parts(before)
    upper_ref[...] = upper
    slope_ref[...] = hidden_grad * slope
    lifted_grad = (hidden_grad * upper).astype(jnp.bfloat16)
    lifted_grad_ref[...] = lifted_grad

    def piece(offset):
        start = pl.multiple_of((place ^ offset) * size, size)
        return dot(mix_ref[pl.ds(start, size), :], lifted_grad, 1, 1)

    keep_ref[0], keep_ref[1] = piece(0), piece(2)
    send_ref[0], send_ref[1] = piece(1), piece(3)
    part = jnp.sum(lifted_grad.astype(jnp.float32), axis=0, keepdims=True)

    @pl.when(pl.program_id(0) == 0)
    def _():
        bias_grad_ref[...] = jnp.zeros_like(bias_grad_ref)

    bias_grad_ref[...] += part


def unpack_fronts(fronts_ref, up_ref, down_ref, mix_ref):
    devices = fronts_ref.shape[0]
    part, mix_part = up_ref.shape[0] // devices, mix_ref.shape[0] // devices

    @pl.when(pl.program_id(0) == 0)
    def _():
        for source in range(devices):
            up_ref[source * part : (source + 1) * part, :] = fronts_ref[source, :part, :]
            down_ref[source * part : (source + 1) * part, :] = fronts_ref[source, part : 2 * part, :]
            mix_ref[source * mix_part : (source + 1) * mix_part, :] = fronts_ref[
                source, 2 * part :, :
            ]


def front_scratch(full, channels, units):
    return [
        pltpu.VMEM((full, units), jnp.bfloat16),
        pltpu.VMEM((full, units), jnp.bfloat16),
        pltpu.VMEM((channels, units), jnp.bfloat16),
    ]


def run_gate(normed, grad, fronts, channels, bias):
    rows, full = normed.shape
    units = fronts.shape[2]
    step = 256

    place = lax.axis_index("chan").astype(jnp.int32).reshape(1)

    def fixed(*shape):
        return pl.BlockSpec(shape, lambda i, p: (0, 0))

    def rowwise(columns):
        return pl.BlockSpec((step, columns), lambda i, p: (i, 0))

    size = channels // 4
    pieces = pl.BlockSpec((2, size, step), lambda i, p: (0, 0, i))
    return pl.pallas_call(
        gate_kernel,
        grid_spec=pltpu.PrefetchScalarGridSpec(
            num_scalar_prefetch=1,
            grid=(rows // step,),
            in_specs=[
                rowwise(full),
                rowwise(full),
                pl.BlockSpec(fronts.shape, lambda i, p: (0, 0, 0)),
                fixed(1, units),
            ],
            out_specs=[rowwise(units)] * 3 + [pieces] * 2 + [fixed(1, units)],
            scratch_shapes=front_scratch(full, channels, units),
        ),
        out_shape=[jax.ShapeDtypeStruct((rows, units), jnp.float32)] * 2
        + [jax.ShapeDtypeStruct((rows, units), jnp.bfloat16)]
        + [jax.ShapeDtypeStruct((2, size, rows), jnp.float32)] * 2
        + [jax.ShapeDtypeStruct((1, units), jnp.float32)],
        compiler_params=pltpu.CompilerParams(vmem_limit_bytes=VMEM),
        cost_estimate=cost(15),
    )(place, normed, grad, fronts, bias[None])


def mid_kernel(
    place_ref,
    own_ref,
    near_ref,
    far_ref,
    last_ref,
    upper_ref,
    slope_ref,
    normed_ref,
    fronts_ref,
    bias_ref,
    affine_ref,
    mixed_ref,
    hidden_ref,
    up_grad_ref,
    out_keep_ref,
    out_send_ref,
    feature_keep_ref,
    feature_send_ref,
    sums_ref,
    bias_grad_ref,
    up_ref,
    down_ref,
    mix_ref,
    whole,
):
    place = place_ref[0]
    width = out_keep_ref.shape[2]
    unpack_fronts(fronts_ref, up_ref, down_ref, mix_ref)
    size = own_ref.shape[0]
    for offset, piece in enumerate((own_ref, near_ref, far_ref, last_ref)):
        start = pl.multiple_of((place ^ offset) * size, size)
        mixed_ref[pl.ds(start, size), :] = piece[...]
    lifted = dot(mixed_ref[...], mix_ref[...], 0, 0) + bias_ref[...]
    hidden = (upper_ref[...] * lifted).astype(jnp.bfloat16)
    up_grad = (slope_ref[...] * lifted).astype(jnp.bfloat16)
    hidden_ref[...] = hidden
    up_grad_ref[...] = up_grad

    @pl.when(pl.program_id(0) == 0)
    def _():
        bias_grad_ref[...] = jnp.zeros_like(bias_grad_ref)

    bias_grad_ref[...] += jnp.sum(up_grad.astype(jnp.float32), axis=0, keepdims=True)

    def part(offset):
        start = pl.multiple_of((place ^ offset) * width, width)
        return whole[:, pl.ds(start, width)].astype(jnp.bfloat16)

    whole[...] = dot(hidden, down_ref[...], 1, 1)
    out_keep_ref[0], out_keep_ref[1] = part(0), part(2)
    out_send_ref[0], out_send_ref[1] = part(1), part(3)
    feature = dot(up_grad, up_ref[...], 1, 1)
    whole[...] = feature
    feature_keep_ref[0], feature_keep_ref[1] = part(0), part(2)
    feature_send_ref[0], feature_send_ref[1] = part(1), part(3)
    one = jnp.sum(feature * affine_ref[0:1, :], axis=1, keepdims=True)
    shifted = normed_ref[...].astype(jnp.float32) - affine_ref[1:2, :]
    two = jnp.sum(feature * shifted, axis=1, keepdims=True)
    lane = lax.broadcasted_iota(jnp.int32, (feature.shape[0], 128), 1)
    sums_ref[...] = jnp.where(lane == 0, one, jnp.where(lane == 1, two, 0.0)).T[0:8, :]


def run_mid(parts, upper, slope, normed, fronts, bias, affine):
    rows, full = normed.shape
    units = fronts.shape[2]
    channels = 4 * parts[0].shape[0]
    width = full // 4
    step = 256
    place = lax.axis_index("chan").astype(jnp.int32).reshape(1)

    def fixed(*shape):
        return pl.BlockSpec(shape, lambda i, p: (0, 0))

    def rowwise(columns):
        return pl.BlockSpec((step, columns), lambda i, p: (i, 0))

    def columns(count):
        return pl.BlockSpec((count, step), lambda i, p: (0, i))

    pieces = pl.BlockSpec((2, step, width), lambda i, p: (0, i, 0))
    piece_shape = jax.ShapeDtypeStruct((2, rows, width), jnp.bfloat16)
    return pl.pallas_call(
        mid_kernel,
        grid_spec=pltpu.PrefetchScalarGridSpec(
            num_scalar_prefetch=1,
            grid=(rows // step,),
            in_specs=[
                columns(channels // 4),
                columns(channels // 4),
                columns(channels // 4),
                columns(channels // 4),
                rowwise(units),
                rowwise(units),
                rowwise(full),
                pl.BlockSpec(fronts.shape, lambda i, p: (0, 0, 0)),
                fixed(1, units),
                fixed(2, full),
            ],
            out_specs=[columns(channels)]
            + [rowwise(units)] * 2
            + [pieces] * 4
            + [columns(8), fixed(1, units)],
            scratch_shapes=front_scratch(full, channels, units)
            + [pltpu.VMEM((step, full), jnp.float32)],
        ),
        out_shape=[jax.ShapeDtypeStruct((channels, rows), jnp.bfloat16)]
        + [jax.ShapeDtypeStruct((rows, units), jnp.bfloat16)] * 2
        + [piece_shape] * 4
        + [
            jax.ShapeDtypeStruct((8, rows), jnp.float32),
            jax.ShapeDtypeStruct((1, units), jnp.float32),
        ],
        compiler_params=pltpu.CompilerParams(vmem_limit_bytes=VMEM),
        cost_estimate=cost(14),
    )(place, *parts, upper, slope, normed, fronts, bias[None], affine)


def payload_kernel(
    grad_ref, slope_ref, before_ref, gain_ref, bias_ref, sums_ref, payload_ref, bias_grad_ref
):
    count = grad_ref.shape[0]
    grad = (grad_ref[...].astype(jnp.float32) * slope_ref[...]).astype(jnp.bfloat16)
    payload_ref[:count, :] = grad
    grad = grad.astype(jnp.float32)
    centred = before_ref[...] - bias_ref[...] - gain_ref[:, 1:2]
    one = jnp.sum(grad * gain_ref[:, 0:1], axis=0, keepdims=True) + sums_ref[0:1, :]
    two = jnp.sum(grad * centred, axis=0, keepdims=True) + sums_ref[1:2, :]
    row = lax.broadcasted_iota(jnp.int32, (16, grad.shape[1]), 0)
    one_high = one.astype(jnp.bfloat16).astype(jnp.float32)
    two_high = two.astype(jnp.bfloat16).astype(jnp.float32)
    tail = jnp.where(row == 0, one_high, jnp.where(row == 1, one - one_high, 0.0))
    tail = jnp.where(row == 2, two_high, jnp.where(row == 3, two - two_high, tail))
    payload_ref[count:, :] = tail.astype(jnp.bfloat16)
    part = jnp.sum(grad, axis=1, keepdims=True)

    @pl.when(pl.program_id(0) == 0)
    def _():
        bias_grad_ref[...] = jnp.zeros_like(bias_grad_ref)

    bias_grad_ref[...] += part


def run_payload(grad, slope, before, gain, bias, sums):
    count, rows = grad.shape
    step = 512

    def columns(lines):
        return pl.BlockSpec((lines, step), lambda i: (0, i))

    def fixed(*shape):
        return pl.BlockSpec(shape, lambda i: (0, 0))

    return pl.pallas_call(
        payload_kernel,
        grid=(rows // step,),
        in_specs=[columns(count)] * 3 + [fixed(count, 2), fixed(count, 1), columns(8)],
        out_specs=[columns(count + 16), fixed(count, 1)],
        out_shape=[
            jax.ShapeDtypeStruct((count + 16, rows), jnp.bfloat16),
            jax.ShapeDtypeStruct((count, 1), jnp.float32),
        ],
        cost_estimate=cost(3),
    )(grad, slope, before, gain, bias[:, None], sums)


def final_kernel(
    _,
    own_ref,
    near_ref,
    far_ref,
    last_ref,
    rows_ref,
    kept_ref,
    sent_ref,
    passed_ref,
    tokens_ref,
    stats_ref,
    grad_ref,
    gain_ref,
    input_grad_ref,
    gain_grad_ref,
    shift_grad_ref,
    down_grad_ref,
):
    size = own_ref.shape[0] - 16
    row = lax.broadcasted_iota(jnp.int32, (16, 256), 0)
    lane = lax.broadcasted_iota(jnp.int32, (16, 256), 1)
    pick = jnp.where((row < 2) == (lane < 128), 1.0, 0.0)
    pick = jnp.where(row < 4, pick, 0.0).astype(jnp.bfloat16)
    normed_grad = (
        kept_ref[0].astype(jnp.float32)
        + sent_ref[0].astype(jnp.float32)
        + passed_ref[...].astype(jnp.float32)
    )
    totals = jnp.zeros((normed_grad.shape[0], 256), jnp.float32)
    for offset, piece in enumerate((own_ref, near_ref, far_ref, last_ref)):
        weights = rows_ref[:, offset * size : (offset + 1) * size]
        normed_grad += dot(piece[:size, :], weights, 0, 1)
        totals += dot(piece[size:, :], pick, 0, 0)
    scaled = normed_grad * gain_ref[...]
    centred = (tokens_ref[...].astype(jnp.float32) - stats_ref[:, 0:1]) * stats_ref[:, 64:65]
    grad = grad_ref[...].astype(jnp.float32)
    mean_one = totals[:, 0:1] * (1.0 / D)
    mean_two = totals[:, 128:129] * (1.0 / D)
    input_grad_ref[...] = stats_ref[:, 64:65] * (scaled - mean_one - centred * mean_two) + grad

    @pl.when(pl.program_id(0) == 0)
    def _():
        gain_grad_ref[...] = jnp.zeros_like(gain_grad_ref)
        shift_grad_ref[...] = jnp.zeros_like(shift_grad_ref)
        down_grad_ref[...] = jnp.zeros_like(down_grad_ref)

    gain_grad_ref[...] += jnp.sum(normed_grad * centred, axis=0, keepdims=True)
    shift_grad_ref[...] += jnp.sum(normed_grad, axis=0, keepdims=True)
    down_grad_ref[...] += jnp.sum(grad, axis=0, keepdims=True)


def run_final(parts, input_rows, kept, sent, passed, tokens, stats, grad, gain):
    rows, width = tokens.shape
    lines = parts[0].shape[0]
    step = 256
    place = lax.axis_index("chan").astype(jnp.int32).reshape(1)

    def fixed(*shape):
        return pl.BlockSpec(shape, lambda i, p: (0, 0))

    def rowwise(columns):
        return pl.BlockSpec((step, columns), lambda i, p: (i, 0))

    def columns(count):
        return pl.BlockSpec((count, step), lambda i, p: (0, i))

    piece = pl.BlockSpec((1, step, width), lambda i, p: (0, i, 0))
    return pl.pallas_call(
        final_kernel,
        grid_spec=pltpu.PrefetchScalarGridSpec(
            num_scalar_prefetch=1,
            grid=(rows // step,),
            in_specs=[columns(lines)] * 4
            + [
                fixed(*input_rows.shape),
                piece,
                piece,
                rowwise(width),
                rowwise(width),
                rowwise(128),
                pl.BlockSpec((step, width), lambda i, p: (i, p[0])),
                fixed(1, width),
            ],
            out_specs=[rowwise(width)] + [fixed(1, width)] * 3,
        ),
        out_shape=[jax.ShapeDtypeStruct((rows, width), jnp.float32)]
        + [jax.ShapeDtypeStruct((1, width), jnp.float32)] * 3,
        cost_estimate=cost(6),
    )(place, *parts, input_rows, kept, sent, passed, tokens, stats, grad, gain[None])


def grads_kernel(
    side_ref,
    outer_ref,
    normed_ref,
    mixed_ref,
    hidden_ref,
    up_ref,
    lifted_ref,
    down_send_ref,
    down_keep_ref,
    rest_send_ref,
    rest_keep_ref,
):
    turn = pl.program_id(0)
    half = pl.num_programs(0) // 2
    rows = outer_ref.shape[1]
    down = dot(outer_ref[...], hidden_ref[...], 0, 0).astype(jnp.bfloat16)
    up = dot(normed_ref[...], up_ref[...], 0, 0).astype(jnp.bfloat16)
    mix = dot(mixed_ref[...], lifted_ref[...], 1, 0).astype(jnp.bfloat16)

    def write(down_ref, rest_ref):
        down_ref[0] = down
        rest_ref[0, :rows, :] = up
        rest_ref[0, rows:, :] = mix

    pl.when(turn < half)(lambda: write(down_send_ref, rest_send_ref))
    pl.when(turn >= half)(lambda: write(down_keep_ref, rest_keep_ref))


def run_grads(outer, normed, mixed, hidden, up, lifted):
    rows, full = outer.shape
    channels = mixed.shape[0]
    units = hidden.shape[1]
    devices = lax.axis_size("seq")
    half = devices // 2
    part, mix_part = full // devices, channels // devices
    side = (lax.axis_index("seq") & 1).astype(jnp.int32).reshape(1)

    def target(i, p):
        return 2 * (i % half) + jnp.where(i < half, 1 - p[0], p[0])

    def fixed(*shape):
        return pl.BlockSpec(shape, lambda i, p: (0, 0))

    sent = lambda i, p: (jnp.minimum(i, half - 1), 0, 0)
    kept = lambda i, p: (jnp.maximum(i - half, 0), 0, 0)
    whole = part + mix_part
    return pl.pallas_call(
        grads_kernel,
        grid_spec=pltpu.PrefetchScalarGridSpec(
            num_scalar_prefetch=1,
            grid=(devices,),
            in_specs=[
                pl.BlockSpec((rows, part), lambda i, p: (0, target(i, p))),
                pl.BlockSpec((rows, part), lambda i, p: (0, target(i, p))),
                pl.BlockSpec((mix_part, rows), lambda i, p: (target(i, p), 0)),
                fixed(rows, units),
                fixed(rows, units),
                fixed(rows, units),
            ],
            out_specs=[
                pl.BlockSpec((1, part, units), sent),
                pl.BlockSpec((1, part, units), kept),
                pl.BlockSpec((1, whole, units), sent),
                pl.BlockSpec((1, whole, units), kept),
            ],
        ),
        out_shape=[jax.ShapeDtypeStruct((half, part, units), jnp.bfloat16)] * 2
        + [jax.ShapeDtypeStruct((half, whole, units), jnp.bfloat16)] * 2,
        compiler_params=pltpu.CompilerParams(vmem_limit_bytes=VMEM),
        cost_estimate=cost(14),
    )(side, outer, normed, mixed, hidden, up, lifted)


def swap(value, distance):
    return lax.ppermute(value, "chan", [(i, i ^ distance) for i in range(4)])


def gather_parts(piece):
    far = swap(piece, 2)
    return piece, swap(piece, 1), far, swap(far, 1)


def after(value, *others):
    return lax.optimization_barrier((value,) + others)[0]


def to_channels(value, sequences):
    devices = lax.axis_size("seq")
    channels, tokens = value.shape
    share = channels // devices
    got = lax.all_to_all(value.reshape(devices, share, tokens), "seq", 0, 0, tiled=True)
    got = got.reshape(sequences, devices // sequences, share, tokens)
    return got.transpose(1, 0, 2, 3).reshape(devices // sequences, sequences * share, tokens)


def to_tokens(value, sequences):
    devices = lax.axis_size("seq")
    sources, count, tokens = value.shape
    share = count // sequences
    sent = value.reshape(sources, sequences, share, tokens).transpose(1, 0, 2, 3)
    got = lax.all_to_all(sent.reshape(devices, share, tokens), "seq", 0, 0, tiled=True)
    return got.reshape(devices * share, tokens)


def tile_rows(flat):
    width = flat.shape[-1]
    padded = -(-width // 128) * 128
    flat = jnp.pad(flat, [(0, 0)] * (flat.ndim - 1) + [(0, padded - width)])
    return flat.reshape(flat.shape[:-1] + (padded // 128, 128))


def planes(value, count):
    parts = []
    for _ in range(count):
        part = lax.reduce_precision(value, 8, 7)
        parts.append(part.astype(jnp.bfloat16))
        value = value - part
    return parts


def plain_grads(outer, normed, mixed, hidden, up, lifted):
    devices = lax.axis_size("seq")
    side = lax.axis_index("seq") & 1

    def parts(value):
        value = value.astype(jnp.bfloat16)
        return value.reshape(devices // 2, 2, value.shape[0] // devices, value.shape[1])

    def pick(value, index):
        return lax.dynamic_index_in_dim(value, index, 1, False)

    down = parts(dot(outer, hidden, 0, 0))
    rest = (parts(dot(normed, up, 0, 0)), parts(dot(mixed, lifted, 1, 0)))
    rest = jnp.concatenate(rest, axis=2)
    return (pick(down, 1 - side), pick(down, side), pick(rest, 1 - side), pick(rest, side))


def halve(sent, kept):
    devices = lax.axis_size("seq")
    got = lax.ppermute(sent, "seq", [(i, i ^ 1) for i in range(devices)])
    return (kept.astype(jnp.float32) + got.astype(jnp.float32)).astype(jnp.bfloat16)


def settle(halves):
    devices = lax.axis_size("seq")
    groups = [[i for i in range(devices) if i & 1 == side] for side in (0, 1)]
    got = lax.all_to_all(halves, "seq", 0, 0, axis_index_groups=groups, tiled=True)
    return jnp.sum(got.astype(jnp.float32), axis=0)


def per_device(
    tokens,
    norm_gain,
    norm_shift,
    up_weight,
    up_bias,
    input_weight,
    input_bias,
    mix_weight,
    mix_bias,
    down_weight,
    down_bias,
    decay_rate,
    decay_freq,
    step_log,
    read_real,
    read_imag,
    skip_gain,
    out_grad,
):
    row_count, width = tokens.shape
    devices = lax.axis_size("seq")
    place = lax.axis_index("chan")
    sequences = devices * row_count // LENGTH
    feature_rows, channels = input_weight.shape
    units = up_weight.shape[1]
    share = channels // devices
    modes_here = decay_rate.shape[0]
    modes = modes_here * devices
    near = swap(tokens, 1)
    early_rows = row_count // 4
    far, far_late = swap(tokens[:early_rows], 2), swap(tokens[early_rows:], 2)
    token_parts = (tokens, near, far, far_late, swap(far, 1), swap(far_late, 1))

    pair = jnp.stack([norm_gain, norm_shift])
    pairs = jnp.stack([pair, swap(pair, 1), swap(pair, 2), swap(pair, 3)])
    pairs = jnp.stack([pairs[place ^ i] for i in range(4)])
    fronts = jnp.concatenate([up_weight, down_weight.T, mix_weight])
    pairs = after(pairs, far, fronts)
    fronts = lax.all_gather(fronts, "seq", axis=0)
    small = (pairs.reshape(-1), up_bias, input_bias, mix_bias, down_bias, decay_rate, decay_freq)
    sizes = [v.shape[0] for v in small]
    small = tile_rows(jnp.concatenate(small))
    reads = jnp.concatenate([read_real, read_imag], axis=1).reshape(devices, share, 2 * modes_here)
    reads = jnp.pad(reads, ((0, 0), (0, 0), (0, 128 - 2 * modes_here)))
    copies = jnp.broadcast_to(small, (devices,) + small.shape)
    exact = jnp.concatenate([reads, copies], axis=1)
    exact_rows = exact.shape[1]
    weights = jnp.broadcast_to(input_weight, (devices,) + input_weight.shape)
    got = jnp.concatenate(planes(exact, 3) + [weights], axis=1)
    got = lax.all_to_all(got, "seq", 0, 0, tiled=True)
    input_full = got[:, 3 * exact_rows :].reshape(4 * width, channels)

    def exact_part(start, stop):
        rows = [got[:, i * exact_rows + start : i * exact_rows + stop] for i in range(3)]
        rows = [r.astype(jnp.float32) for r in rows]
        return rows[0] + (rows[1] + rows[2])

    small = exact_part(share, exact_rows).reshape(devices, -1)
    parts, spot = [], 0
    for size in sizes:
        parts.append(small[:, spot : spot + size])
        spot += size
    affine = parts[0].reshape(devices, 4, 2, -1).transpose(2, 1, 0, 3).reshape(2, 4 * width)
    input_shift = parts[2].reshape(-1)

    normed, values_low, in_slope, pre_in, stats = run_norm(
        token_parts, affine, input_full, input_shift
    )
    values = to_channels(values_low, sequences)

    got = after(got, normed)
    parts = lax.optimization_barrier(tuple(parts) + (normed,))[:-1]
    reads = exact_part(0, share)[:, :, : 2 * modes_here].transpose(1, 0, 2)
    read_re = reads[:, :, :modes_here].reshape(share, modes)
    read_im = reads[:, :, modes_here:].reshape(share, modes)
    up_shift, _, mix_shift, down_shift, rate, freq = (p.reshape(-1) for p in parts[1:])
    gain_own = lax.dynamic_slice_in_dim(affine[0], place * width, width)

    spacing = jnp.exp(step_log)
    damping = spacing[:, None] * rate[None, :]
    rotation = spacing[:, None] * freq[None, :]
    inflow = -jnp.expm1(-damping)
    extents = 2.0 ** jnp.arange(8)[None, :, None]
    length = jnp.exp(-damping[:, None] * extents)
    angle = rotation[:, None] * extents
    power_re, power_im = length * jnp.cos(angle), length * jnp.sin(angle)

    def repeat(value):
        return jnp.tile(value, (sequences,) + (1,) * (value.ndim - 1))

    def rows(value_re, value_im):
        return repeat(jnp.concatenate([value_re, value_im], axis=1)[:, None])

    power, out_table, in_table, toeplitz = make_tables(
        repeat(power_re), repeat(power_im), repeat(read_re), repeat(read_im), repeat(inflow)
    )
    jump = rows(power_re[:, 7], power_im[:, 7])[:, 0]
    flow = rows(inflow, inflow)
    lead = rows(*cmul(read_re, read_im, power_re[:, 0], power_im[:, 0]))
    skip = repeat(skip_gain)

    mixed, starts, values_split = run_forward(
        values, skip, jump, flow, lead, out_table, in_table, toeplitz
    )
    mixed_tokens = to_tokens(mixed, sequences)

    upper, up_slope, lifted_grad, channel_keep, channel_send, mix_bias_part = run_gate(
        after(normed, mixed), out_grad, fronts, 4 * channels, up_shift
    )
    channel_sent = swap(after(channel_send, mixed_tokens), 1)
    mixed_parts = gather_parts(mixed_tokens)
    channel_passed = (channel_keep[1] + channel_sent[1]).astype(jnp.bfloat16)
    channel_sum = channel_keep[0] + channel_sent[0]
    channel_far = swap(channel_passed, 2)
    mixed_grad = (channel_sum + channel_far.astype(jnp.float32)).astype(jnp.bfloat16)
    grads = to_channels(mixed_grad, sequences)

    (
        mixed_full,
        hidden,
        up_pre_grad,
        out_keep,
        out_send,
        feature_keep,
        feature_send,
        up_sums,
        up_bias_part,
    ) = run_mid(
        (after(mixed_parts[0], channel_passed),) + mixed_parts[1:],
        upper,
        up_slope,
        normed,
        fronts,
        mix_shift,
        affine,
    )
    out_sent, feature_sent = swap(out_send, 1), swap(feature_send, 1)

    def passed(keep, sent):
        return (keep[1].astype(jnp.float32) + sent[1].astype(jnp.float32)).astype(jnp.bfloat16)

    feature_passed = passed(feature_keep, feature_sent)
    out_passed = passed(out_keep, out_sent)
    make_grads = run_grads if feature_rows % 128 == 0 else plain_grads
    down_send, down_keep, rest_send, rest_keep = make_grads(
        out_grad, normed, mixed_full, after(hidden, mixed_grad), up_pre_grad, lifted_grad
    )
    feature_far, out_far = swap(feature_passed, 2), swap(out_passed, 2)
    down_half = halve(after(down_send, grads), down_keep)
    rest_half = halve(after(rest_send, grads), rest_keep)
    grads = after(grads, down_send, feature_passed, out_passed)
    values_grad, later, grads_split = run_backward(
        grads, skip, jump, flow, lead, out_table, in_table, toeplitz
    )
    values_back = to_tokens(after(values_grad, feature_far), sequences)
    sums, skip_sums = run_sums(grads_split, values_split, starts, later, power)
    halves = jnp.concatenate([down_half, rest_half], axis=1)
    large = settle(after(halves, values_back))
    down_weight_grad = large[:feature_rows].T
    up_weight_grad, mix_weight_grad = large[feature_rows : 2 * feature_rows], large[2 * feature_rows :]
    inputs = tokens.astype(jnp.float32)
    output = (
        out_keep[0].astype(jnp.float32)
        + out_sent[0].astype(jnp.float32)
        + out_far.astype(jnp.float32)
        + down_shift
        + inputs
    )

    in_gain = jnp.dot(
        input_full.T.astype(jnp.float32), affine.T, precision=lax.Precision.HIGHEST
    )
    payload, input_bias_part = run_payload(
        after(values_back, sums, out_far, halves), in_slope, pre_in, in_gain, input_shift, up_sums
    )
    payload_parts = gather_parts(payload)
    input_part = dot(normed, payload[:channels], 0, 1)
    pieces = gather_parts(after(input_full, hidden))
    pieces = [lax.dynamic_slice_in_dim(p, place * width, width, 0) for p in pieces]
    input_rows = jnp.concatenate(pieces, axis=1)
    input_grad, gain_part, shift_part, down_bias_part = run_final(
        payload_parts,
        input_rows,
        feature_keep,
        feature_sent,
        feature_far,
        tokens,
        stats,
        out_grad,
        gain_own,
    )

    sums = jnp.concatenate([sums[:, :4], sums[:, 4:8] * flow[:, :, :modes], sums[:, 8:]], axis=1)
    sums = jnp.sum(sums.reshape((sequences, share) + sums.shape[1:]), axis=0)
    skip_grad = jnp.sum(skip_sums.reshape(sequences, share, BLOCK), axis=(0, 2))
    out_zero = cmul(power_re[:, 0], power_im[:, 0], sums[:, 0], sums[:, 1])
    out_one = cmul(
        power_re[:, 0], power_im[:, 0], sums[:, 0] + sums[:, 2], sums[:, 1] + sums[:, 3]
    )
    chained = cmul(power_re[:, 7], power_im[:, 7], sums[:, 8], sums[:, 9])
    local_zero, local_one = (sums[:, 10], sums[:, 11]), (sums[:, 12], sums[:, 13])
    read_re_grad = out_zero[0] + inflow * local_zero[0]
    read_im_grad = -out_zero[1] - inflow * local_zero[1]
    turn = cmul(
        read_re, read_im, out_one[0] + inflow * local_one[0], out_one[1] + inflow * local_one[1]
    )
    turn_re = turn[0] + sums[:, 6] + BLOCK * chained[0]
    turn_im = turn[1] + sums[:, 7] + BLOCK * chained[1]
    inflow_grad = sums[:, 4] / inflow + read_re * local_zero[0] - read_im * local_zero[1]
    damping_grad = jnp.exp(-damping) * inflow_grad - turn_re
    rotation_grad = -turn_im
    step_log_grad = spacing * jnp.sum(
        rate[None, :] * damping_grad + freq[None, :] * rotation_grad, axis=1
    )
    rates = jnp.stack(
        [
            jnp.sum(spacing[:, None] * damping_grad, axis=0),
            jnp.sum(spacing[:, None] * rotation_grad, axis=0),
        ]
    )
    rates = rates + swap(rates, 1)
    rates = rates + swap(rates, 2)

    read_grads = jnp.stack([read_re_grad, read_im_grad], axis=1)
    read_grads = read_grads.reshape(share, 2, devices, modes_here).transpose(2, 0, 1, 3)
    read_grads = read_grads.reshape(devices, share, 2 * modes_here)
    read_grads = jnp.pad(read_grads, ((0, 0), (0, 0), (0, 128 - 2 * modes_here)))

    def line_up(vectors):
        vectors = [v.reshape(devices, -1) for v in vectors]
        sizes = [v.shape[1] for v in vectors]
        return tile_rows(jnp.concatenate(vectors, axis=1)), sizes

    def take_apart(flat, sizes):
        parts, spot = [], 0
        for size in sizes:
            parts.append(flat[spot : spot + size])
            spot += size
        return parts

    vectors, sizes = line_up(
        (
            up_bias_part,
            input_bias_part,
            mix_bias_part,
            rates[0],
            rates[1],
            gain_part,
            shift_part,
            down_bias_part,
        )
    )
    input_part = input_part.reshape(devices, feature_rows, channels)
    parcel = after(jnp.concatenate([read_grads, vectors], axis=1), large)
    exact_rows = parcel.shape[1]
    parcel = jnp.concatenate(planes(parcel, 2) + [input_part.astype(jnp.bfloat16)], axis=1)
    late = lax.all_to_all(parcel, "seq", 0, 0, tiled=True).astype(jnp.float32)
    input_weight_grad = jnp.sum(late[:, 2 * exact_rows :], axis=0)
    late = late[:, :exact_rows] + late[:, exact_rows : 2 * exact_rows]
    read_late = late[:, :share, : 2 * modes_here].reshape(channels, 2 * modes_here)
    late = take_apart(jnp.sum(late[:, share:], axis=0).reshape(-1), sizes)
    up_bias_grad, input_bias_grad, mix_bias_grad, rate_out, freq_out = late[:5]
    gain_grad, shift_grad, down_bias_grad = late[5:]
    return (
        output,
        input_grad,
        gain_grad,
        shift_grad,
        up_weight_grad,
        up_bias_grad,
        input_weight_grad,
        input_bias_grad,
        mix_weight_grad,
        mix_bias_grad,
        down_weight_grad,
        down_bias_grad,
        rate_out,
        freq_out,
        step_log_grad,
        read_late[:, :modes_here],
        read_late[:, modes_here:],
        skip_grad,
    )


def solution(mesh):
    return jax.shard_map(
        per_device,
        mesh=mesh,
        in_specs=(
            P("seq", "chan"),
            P(("chan", "seq")),
            P(("chan", "seq")),
            P("seq", "chan"),
            P(("chan", "seq")),
            P("seq", "chan"),
            P(("chan", "seq")),
            P("seq", "chan"),
            P(("chan", "seq")),
            P("chan", "seq"),
            P(("chan", "seq")),
            P("seq"),
            P("seq"),
            P(("chan", "seq")),
            P("chan", "seq"),
            P("chan", "seq"),
            P(("chan", "seq")),
            P("seq", None),
        ),
        out_specs=(
            P("seq", "chan"),
            P("seq", "chan"),
            P(("chan", "seq")),
            P(("chan", "seq")),
            P("seq", "chan"),
            P(("chan", "seq")),
            P("seq", "chan"),
            P(("chan", "seq")),
            P("seq", "chan"),
            P(("chan", "seq")),
            P("chan", "seq"),
            P(("chan", "seq")),
            P("seq"),
            P("seq"),
            P(("chan", "seq")),
            P("chan", "seq"),
            P("chan", "seq"),
            P(("chan", "seq")),
        ),
        check_vma=False,
    )
```

```python
from functools import partial
import math

import jax
import jax.numpy as jnp
from jax import lax
from jax.experimental import pallas as pl
from jax.experimental.pallas import tpu as pltpu
from jax.sharding import PartitionSpec as P

D = 1024
LENGTH = 16384
EPSILON = 1e-05


BLOCK = 128
MEGA = 1024 * 1024
VMEM = 56 * MEGA


def dot(left, right, left_dim, right_dim):
    return lax.dot_general(
        left, right, (((left_dim,), (right_dim,)), ((), ())), preferred_element_type=jnp.float32
    )


def cmul(a_re, a_im, b_re, b_im):
    return (a_re * b_re - a_im * b_im, a_re * b_im + a_im * b_re)


def grow(first, reversed_rows, mode_powers, store):
    row = lax.broadcasted_iota(jnp.int32, (8, first[0].shape[1]), 0)
    exponent = 7 - row if reversed_rows else row
    part = (
        jnp.broadcast_to(first[0], row.shape),
        jnp.broadcast_to(first[1], row.shape),
    )
    for level in range(3):
        factor_re, factor_im = mode_powers(level)
        taken = (exponent >> level) & 1 == 1
        part = cmul(*part, jnp.where(taken, factor_re, 1.0), jnp.where(taken, factor_im, 0.0))
    spot = BLOCK - 8 if reversed_rows else 0
    store(spot, part[0], part[1])
    whole = part
    size, level = 8, 3
    while size < BLOCK:
        factor = mode_powers(level)
        fresh = cmul(*whole, *factor)
        spot = BLOCK - 2 * size if reversed_rows else size
        store(spot, *fresh)
        pair = (fresh, whole) if reversed_rows else (whole, fresh)
        whole = tuple(jnp.concatenate([p, q], axis=0) for p, q in zip(*pair))
        size, level = 2 * size, level + 1


def tables_kernel(
    power_re_ref,
    power_im_ref,
    read_re_ref,
    read_im_ref,
    inflow_ref,
    power_ref,
    out_table_ref,
    in_table_ref,
    toeplitz_ref,
):
    modes = power_re_ref.shape[2]
    lower, upper = slice(0, modes), slice(modes, 2 * modes)

    def mode_powers(level):
        return (power_re_ref[0, level : level + 1, :], power_im_ref[0, level : level + 1, :])

    inflow = inflow_ref[0]
    one, none = jnp.ones_like(inflow), jnp.zeros_like(inflow)

    def store_power(spot, part_re, part_im):
        rows = slice(spot, spot + part_re.shape[0])
        power_ref[0, rows, lower] = part_re
        power_ref[0, rows, upper] = part_im

    grow((one, none), False, mode_powers, store_power)
    exact = jnp.concatenate([power_ref[0, :, lower], -power_ref[0, :, upper]], axis=1)
    rounded = exact.astype(jnp.bfloat16)
    out_table_ref[0] = rounded
    rest = (exact - rounded.astype(jnp.float32)).astype(jnp.bfloat16)
    backward = []

    def store_in(spot, part_re, part_im):
        backward.append((spot, part_re, part_im))

    grow((one, none), True, mode_powers, store_in)
    backward.sort(key=lambda entry: entry[0])
    in_table_ref[0, :, lower] = jnp.concatenate([e[1] for e in backward], 0).astype(jnp.bfloat16)
    in_table_ref[0, :, upper] = jnp.concatenate([e[2] for e in backward], 0).astype(jnp.bfloat16)
    weight = jnp.concatenate([read_re_ref[0] * inflow, read_im_ref[0] * inflow], axis=1)
    high = weight.astype(jnp.bfloat16).astype(jnp.float32)
    row = lax.broadcasted_iota(jnp.int32, (16, 2 * modes), 0)
    probe = jnp.where(row == 0, high, jnp.where(row == 1, weight - high, 0.0))
    probe = probe.astype(jnp.bfloat16)
    lags = dot(probe, rounded, 1, 1) + dot(probe, rest, 1, 1)
    kernel_row = jnp.sum(lags, axis=0, keepdims=True)
    skewed = pltpu.roll(
        jnp.broadcast_to(kernel_row, (BLOCK, BLOCK)), 0, 1, stride=1, stride_axis=0
    )
    source = lax.broadcasted_iota(jnp.int32, (BLOCK, BLOCK), 0)
    target = lax.broadcasted_iota(jnp.int32, (BLOCK, BLOCK), 1)
    skewed = jnp.where(target >= source, skewed, 0.0)
    coarse = skewed.astype(jnp.bfloat16)
    toeplitz_ref[0, :BLOCK, :] = coarse
    toeplitz_ref[0, BLOCK:, :] = (skewed - coarse.astype(jnp.float32)).astype(jnp.bfloat16)


def make_tables(power_re, power_im, read_re, read_im, inflow):
    count, levels, modes = power_re.shape

    def spec(*shape):
        return pl.BlockSpec((1,) + shape, lambda i: (i, 0, 0))

    return pl.pallas_call(
        tables_kernel,
        grid=(count,),
        in_specs=[spec(levels, modes)] * 2 + [spec(1, modes)] * 3,
        out_specs=[
            spec(BLOCK, 2 * modes),
            spec(BLOCK, 2 * modes),
            spec(BLOCK, 2 * modes),
            spec(2 * BLOCK, BLOCK),
        ],
        out_shape=[
            jax.ShapeDtypeStruct((count, BLOCK, 2 * modes), jnp.float32),
            jax.ShapeDtypeStruct((count, BLOCK, 2 * modes), jnp.bfloat16),
            jax.ShapeDtypeStruct((count, BLOCK, 2 * modes), jnp.bfloat16),
            jax.ShapeDtypeStruct((count, 2 * BLOCK, BLOCK), jnp.bfloat16),
        ],
        compiler_params=pltpu.CompilerParams(vmem_limit_bytes=VMEM),
        cost_estimate=cost(12),
    )(power_re, power_im, read_re[:, None], read_im[:, None], inflow[:, None])


def spread_tokens(ref, scratch):
    sources, count, tokens = ref.shape
    per_source = tokens // BLOCK
    for source in range(sources):
        for part in range(per_source):
            row = (source * per_source + part) * count
            tile = ref[source, :, part * BLOCK : (part + 1) * BLOCK]
            scratch[row : row + count, :] = tile.astype(jnp.float32)


def gather_tokens(scratch, ref):
    sources, count, tokens = ref.shape
    per_source = tokens // BLOCK
    for source in range(sources):
        for part in range(per_source):
            row = (source * per_source + part) * count
            ref[source, :, part * BLOCK : (part + 1) * BLOCK] = scratch[
                row : row + count, :
            ].astype(ref.dtype)


def put_rows(states, rows, value):
    for tile in range(states.shape[0]):
        states[tile, rows, :] = value[:, tile * 128 : (tile + 1) * 128]


def take_rows(states, rows):
    return jnp.concatenate([states[tile, rows, :] for tile in range(states.shape[0])], axis=1)


def run_chain(states, jump_ref, sign, count, blocks, order):
    tiles = states.shape[0] // 2
    jumps = [
        (
            jump_ref[:, t * 128 : (t + 1) * 128],
            sign * jump_ref[:, (tiles + t) * 128 : (tiles + t + 1) * 128],
        )
        for t in range(tiles)
    ]

    def step(turn, state):
        rows = pl.ds(pl.multiple_of(order(turn) * count, count), count)
        following = []
        for t in range(tiles):
            end_re, end_im = states[t, rows, :], states[tiles + t, rows, :]
            states[t, rows, :] = state[t][0]
            states[tiles + t, rows, :] = state[t][1]
            next_re, next_im = cmul(*jumps[t], *state[t])
            following.append((next_re + end_re, next_im + end_im))
        return tuple(following)

    blank = jnp.zeros((count, 128), jnp.float32)
    lax.fori_loop(0, blocks, step, ((blank, blank),) * tiles, unroll=2)


def forward_kernel(
    values_ref,
    skip_ref,
    jump_ref,
    inflow_ref,
    lead_ref,
    out_table_ref,
    in_table_ref,
    toeplitz_ref,
    mixed_ref,
    starts_ref,
    split_ref,
    tokens,
    states,
):
    count = values_ref.shape[1]
    blocks = states.shape[1] // count
    modes = states.shape[0] * 64
    spread_tokens(values_ref, tokens)

    def rows_of(channel):
        return pl.ds(channel, blocks, stride=count)

    def enter(channel, carry):
        own = tokens[rows_of(channel), :].astype(jnp.bfloat16)
        split_ref[channel] = own
        ends = dot(own, in_table_ref[channel], 1, 0)
        put_rows(states, rows_of(channel), ends * inflow_ref[channel])
        return carry

    lax.fori_loop(0, count, enter, 0, unroll=4)
    run_chain(states, jump_ref, 1.0, count, blocks, lambda turn: turn)

    def leave(channel, carry):
        start = take_rows(states, rows_of(channel))
        starts_ref[channel] = start.astype(jnp.bfloat16)
        lead = lead_ref[channel]
        weighted = cmul(lead[:, :modes], lead[:, modes:], start[:, :modes], start[:, modes:])
        weighted = jnp.concatenate(weighted, axis=1).astype(jnp.bfloat16)
        own = tokens[rows_of(channel), :]
        own_low = own.astype(jnp.bfloat16)
        mixed = dot(weighted, out_table_ref[channel], 1, 1)
        mixed += dot(own_low, toeplitz_ref[channel, :BLOCK, :], 1, 0)
        mixed += dot(own_low, toeplitz_ref[channel, BLOCK:, :], 1, 0)
        tokens[rows_of(channel), :] = mixed + skip_ref[channel] * own
        return carry

    lax.fori_loop(0, count, leave, 0, unroll=4)
    gather_tokens(tokens, mixed_ref)


def run_forward(values, skip, jump, inflow, lead, out_table, in_table, toeplitz):
    sources, count, tokens = values.shape
    blocks = sources * tokens // BLOCK
    width = jump.shape[1]
    vmem = pl.BlockSpec(memory_space=pltpu.VMEM)
    return pl.pallas_call(
        forward_kernel,
        in_specs=[vmem, pl.BlockSpec(memory_space=pltpu.SMEM)] + [vmem] * 6,
        out_specs=[vmem] * 3,
        out_shape=[
            jax.ShapeDtypeStruct(values.shape, jnp.bfloat16),
            jax.ShapeDtypeStruct((count, blocks, width), jnp.bfloat16),
            jax.ShapeDtypeStruct((count, blocks, BLOCK), jnp.bfloat16),
        ],
        scratch_shapes=[
            pltpu.VMEM((blocks * count, BLOCK), jnp.float32),
            pltpu.VMEM((width // 128, blocks * count, 128), jnp.float32),
        ],
        compiler_params=pltpu.CompilerParams(vmem_limit_bytes=VMEM),
        cost_estimate=cost(20),
    )(values, skip, jump, inflow, lead, out_table, in_table, toeplitz)


def backward_kernel(
    grads_ref,
    skip_ref,
    jump_ref,
    inflow_ref,
    lead_ref,
    out_table_ref,
    in_table_ref,
    toeplitz_ref,
    values_grad_ref,
    later_ref,
    split_ref,
    grads,
    states,
):
    count = grads_ref.shape[1]
    blocks = states.shape[1] // count
    modes = states.shape[0] * 64
    spread_tokens(grads_ref, grads)

    def rows_of(channel):
        return pl.ds(channel, blocks, stride=count)

    def enter(channel, carry):
        own = grads[rows_of(channel), :].astype(jnp.bfloat16)
        split_ref[channel] = own
        lead = lead_ref[channel]
        back = dot(own, out_table_ref[channel], 1, 0)
        back = cmul(lead[:, :modes], -lead[:, modes:], back[:, :modes], back[:, modes:])
        put_rows(states, rows_of(channel), jnp.concatenate(back, axis=1))
        return carry

    lax.fori_loop(0, count, enter, 0, unroll=4)
    run_chain(states, jump_ref, -1.0, count, blocks, lambda turn: blocks - 1 - turn)

    def leave(channel, carry):
        later = take_rows(states, rows_of(channel))
        later_ref[channel] = later.astype(jnp.bfloat16)
        later = (later * inflow_ref[channel]).astype(jnp.bfloat16)
        grad = grads[rows_of(channel), :]
        grad_low = grad.astype(jnp.bfloat16)
        back = dot(later, in_table_ref[channel], 1, 1)
        back += dot(grad_low, toeplitz_ref[channel, :BLOCK, :], 1, 1)
        back += dot(grad_low, toeplitz_ref[channel, BLOCK:, :], 1, 1)
        grads[rows_of(channel), :] = back + skip_ref[channel] * grad
        return carry

    lax.fori_loop(0, count, leave, 0, unroll=4)
    gather_tokens(grads, values_grad_ref)


def run_backward(grads, skip, jump, inflow, lead, out_table, in_table, toeplitz):
    sources, count, tokens = grads.shape
    blocks = sources * tokens // BLOCK
    width = jump.shape[1]
    vmem = pl.BlockSpec(memory_space=pltpu.VMEM)
    return pl.pallas_call(
        backward_kernel,
        in_specs=[vmem, pl.BlockSpec(memory_space=pltpu.SMEM)] + [vmem] * 6,
        out_specs=[vmem] * 3,
        out_shape=[
            jax.ShapeDtypeStruct(grads.shape, jnp.bfloat16),
            jax.ShapeDtypeStruct((count, blocks, width), jnp.bfloat16),
            jax.ShapeDtypeStruct((count, blocks, BLOCK), jnp.bfloat16),
        ],
        scratch_shapes=[
            pltpu.VMEM((blocks * count, BLOCK), jnp.float32),
            pltpu.VMEM((width // 128, blocks * count, 128), jnp.float32),
        ],
        compiler_params=pltpu.CompilerParams(vmem_limit_bytes=VMEM),
        cost_estimate=cost(20),
    )(grads, skip, jump, inflow, lead, out_table, in_table, toeplitz)


def sums_kernel(grad_ref, value_ref, start_ref, later_ref, power_ref, sums_ref, skip_ref):
    for index in range(grad_ref.shape[0]):
        channel_sums(
            *(r.at[index] for r in (grad_ref, value_ref, start_ref, later_ref, power_ref)),
            sums_ref.at[index],
            skip_ref.at[index],
        )


def channel_sums(grad_ref, value_ref, start_ref, later_ref, power_ref, sums_ref, skip_ref):
    modes = power_ref.shape[1] // 2
    row = lax.broadcasted_iota(jnp.int32, (BLOCK, BLOCK), 0)
    lane = lax.broadcasted_iota(jnp.int32, (BLOCK, BLOCK), 1)
    flip = jnp.where(row + lane == BLOCK - 1, 1.0, 0.0).astype(jnp.bfloat16)

    def fold(part):
        return jnp.sum(part.reshape(part.shape[0] // 8, 8, part.shape[1]), axis=0)

    grad, value = grad_ref[...], value_ref[...]
    start, later = start_ref[...], later_ref[...]
    product = grad.astype(jnp.float32) * value.astype(jnp.float32)
    skip_ref[...] = jnp.sum(product, axis=0, keepdims=True)
    turned = dot(value, flip, 1, 0).astype(jnp.bfloat16)
    out_sum = dot(grad, start, 0, 0)
    in_sum = dot(turned, later, 0, 0)
    cross = dot(grad, turned, 0, 0)
    cross = jnp.where(row + lane >= BLOCK - 1, cross, 0.0)
    lags = jnp.sum(pltpu.roll(cross, 1, 1, stride=1, stride_axis=0), axis=0, keepdims=True)
    lags = jnp.sum(jnp.where(row == lane, lags, 0.0), axis=1, keepdims=True)
    weight = lax.broadcasted_iota(jnp.int32, (BLOCK, modes), 0).astype(jnp.float32)
    power_re, power_im = power_ref[:, :modes], power_ref[:, modes:]
    terms = []
    for total, sign in ((out_sum, 1.0), (in_sum, -1.0)):
        term_re, term_im = cmul(power_re, power_im, total[:, :modes], sign * total[:, modes:])
        terms += [fold(term_re), fold(term_im), fold(weight * term_re), fold(weight * term_im)]
    later_re, later_im = (later[:, :modes].astype(jnp.float32), later[:, modes:].astype(jnp.float32))
    start_re, start_im = (start[:, :modes].astype(jnp.float32), start[:, modes:].astype(jnp.float32))
    terms += [
        fold(later_re * start_re + later_im * start_im),
        fold(later_re * start_im - later_im * start_re),
    ]
    local_re, local_im = power_re * lags, power_im * lags
    terms += [fold(local_re), fold(local_im), fold(weight * local_re), fold(weight * local_im)]
    for index, term in enumerate(terms):
        sums_ref[index : index + 1, :] = jnp.sum(term, axis=0, keepdims=True)


def run_sums(grads, values, starts, later, power):
    count, blocks, width = starts.shape
    group = 4

    def spec(*shape):
        return pl.BlockSpec((group,) + shape, lambda i: (i, 0, 0))

    return pl.pallas_call(
        sums_kernel,
        grid=(count // group,),
        in_specs=[spec(blocks, BLOCK)] * 2 + [spec(blocks, width)] * 2 + [spec(BLOCK, width)],
        out_specs=[spec(16, width // 2), spec(1, BLOCK)],
        out_shape=[
            jax.ShapeDtypeStruct((count, 16, width // 2), jnp.float32),
            jax.ShapeDtypeStruct((count, 1, BLOCK), jnp.float32),
        ],
        compiler_params=pltpu.CompilerParams(vmem_limit_bytes=VMEM),
        cost_estimate=cost(18),
    )(grads, values, starts, later, power)


def cost(microseconds):
    return pl.CostEstimate(
        flops=int(microseconds * 1e9), bytes_accessed=int(microseconds * 1e6), transcendentals=0
    )


def erf_parts(value):
    half = 0.5 * (1.0 + lax.erf(value * (1.0 / math.sqrt(2.0))))
    density = jnp.exp(-0.5 * value * value) * (1.0 / math.sqrt(2.0 * math.pi))
    return value * half, half + value * density


def norm_kernel(
    early_steps,
    place_ref,
    own_ref,
    near_ref,
    far_ref,
    far_late_ref,
    last_ref,
    last_late_ref,
    affine_ref,
    weight_ref,
    bias_ref,
    normed_ref,
    values_ref,
    slope_ref,
    before_ref,
    stats_ref,
    whole,
):
    place = place_ref[0]
    width = own_ref.shape[1]
    early = pl.program_id(0) < early_steps
    parts = (
        own_ref[...],
        near_ref[...],
        jnp.where(early, far_ref[...], far_late_ref[...]),
        jnp.where(early, last_ref[...], last_late_ref[...]),
    )
    for offset, part in enumerate(parts):
        start = pl.multiple_of((place ^ offset) * width, width)
        whole[:, pl.ds(start, width)] = part.astype(jnp.float32)
    inputs = whole[...]
    average = jnp.mean(inputs, axis=1, keepdims=True)
    spread = jnp.mean(inputs * inputs, axis=1, keepdims=True) - average * average
    inverse = lax.rsqrt(spread + EPSILON)
    normed = (inputs - average) * inverse * affine_ref[0:1, :] + affine_ref[1:2, :]
    normed = normed.astype(jnp.bfloat16)
    normed_ref[...] = normed
    before = dot(weight_ref[...], normed, 0, 1) + bias_ref[...]
    values, slope = erf_parts(before)
    values_ref[...] = values.astype(jnp.bfloat16)
    slope_ref[...] = slope
    before_ref[...] = before
    lane = lax.broadcasted_iota(jnp.int32, (inputs.shape[0], 128), 1)
    stats_ref[...] = jnp.where(lane < 64, average, inverse)


def run_norm(parts, affine, weight, bias):
    rows, width = parts[0].shape
    full, channels = weight.shape
    step = 512
    place = lax.axis_index("chan").astype(jnp.int32).reshape(1)
    half = parts[2].shape[0] // step
    full_rows = pl.BlockSpec((step, width), lambda i, p: (i, 0))
    first_rows = pl.BlockSpec((step, width), lambda i, p: (jnp.minimum(i, half - 1), 0))
    later_rows = pl.BlockSpec((step, width), lambda i, p: (jnp.maximum(i - half, 0), 0))
    return pl.pallas_call(
        partial(norm_kernel, half),
        grid_spec=pltpu.PrefetchScalarGridSpec(
            num_scalar_prefetch=1,
            grid=(rows // step,),
            in_specs=[
                full_rows,
                full_rows,
                first_rows,
                later_rows,
                first_rows,
                later_rows,
                pl.BlockSpec((2, full), lambda i, p: (0, 0)),
                pl.BlockSpec((full, channels), lambda i, p: (0, 0)),
                pl.BlockSpec((channels, 1), lambda i, p: (0, 0)),
            ],
            out_specs=[
                pl.BlockSpec((step, full), lambda i, p: (i, 0)),
                pl.BlockSpec((channels, step), lambda i, p: (0, i)),
                pl.BlockSpec((channels, step), lambda i, p: (0, i)),
                pl.BlockSpec((channels, step), lambda i, p: (0, i)),
                pl.BlockSpec((step, 128), lambda i, p: (i, 0)),
            ],
            scratch_shapes=[pltpu.VMEM((step, full), jnp.float32)],
        ),
        out_shape=[
            jax.ShapeDtypeStruct((rows, full), jnp.bfloat16),
            jax.ShapeDtypeStruct((channels, rows), jnp.bfloat16),
            jax.ShapeDtypeStruct((channels, rows), jnp.float32),
            jax.ShapeDtypeStruct((channels, rows), jnp.float32),
            jax.ShapeDtypeStruct((rows, 128), jnp.float32),
        ],
        compiler_params=pltpu.CompilerParams(vmem_limit_bytes=VMEM),
        cost_estimate=cost(8),
    )(place, *parts, affine, weight, bias[:, None])


def gate_kernel(
    place_ref,
    normed_ref,
    grad_ref,
    fronts_ref,
    bias_ref,
    upper_ref,
    slope_ref,
    lifted_grad_ref,
    keep_ref,
    send_ref,
    bias_grad_ref,
    up_ref,
    down_ref,
    mix_ref,
):
    place = place_ref[0]
    size = keep_ref.shape[1]
    unpack_fronts(fronts_ref, up_ref, down_ref, mix_ref)
    before = dot(normed_ref[...], up_ref[...], 1, 0) + bias_ref[...]
    hidden_grad = dot(grad_ref[...], down_ref[...], 1, 0)
    upper, slope = erf_parts(before)
    upper_ref[...] = upper.astype(jnp.bfloat16)
    slope_ref[...] = (hidden_grad * slope).astype(jnp.bfloat16)
    lifted_grad = (hidden_grad * upper).astype(jnp.bfloat16)
    lifted_grad_ref[...] = lifted_grad

    def piece(offset):
        start = pl.multiple_of((place ^ offset) * size, size)
        return dot(mix_ref[pl.ds(start, size), :], lifted_grad, 1, 1)

    keep_ref[0], keep_ref[1] = piece(0), piece(2)
    send_ref[0], send_ref[1] = piece(1), piece(3)
    part = jnp.sum(lifted_grad.astype(jnp.float32), axis=0, keepdims=True)

    @pl.when(pl.program_id(0) == 0)
    def _():
        bias_grad_ref[...] = jnp.zeros_like(bias_grad_ref)

    bias_grad_ref[...] += part


def unpack_fronts(fronts_ref, up_ref, down_ref, mix_ref):
    devices = fronts_ref.shape[0]
    part, mix_part = up_ref.shape[0] // devices, mix_ref.shape[0] // devices

    @pl.when(pl.program_id(0) == 0)
    def _():
        for source in range(devices):
            up_ref[source * part : (source + 1) * part, :] = fronts_ref[source, :part, :]
            down_ref[source * part : (source + 1) * part, :] = fronts_ref[source, part : 2 * part, :]
            mix_ref[source * mix_part : (source + 1) * mix_part, :] = fronts_ref[
                source, 2 * part :, :
            ]


def front_scratch(full, channels, units):
    return [
        pltpu.VMEM((full, units), jnp.bfloat16),
        pltpu.VMEM((full, units), jnp.bfloat16),
        pltpu.VMEM((channels, units), jnp.bfloat16),
    ]


def run_gate(normed, grad, fronts, channels, bias):
    rows, full = normed.shape
    units = fronts.shape[2]
    step = 256

    place = lax.axis_index("chan").astype(jnp.int32).reshape(1)

    def fixed(*shape):
        return pl.BlockSpec(shape, lambda i, p: (0, 0))

    def rowwise(columns):
        return pl.BlockSpec((step, columns), lambda i, p: (i, 0))

    size = channels // 4
    pieces = pl.BlockSpec((2, size, step), lambda i, p: (0, 0, i))
    return pl.pallas_call(
        gate_kernel,
        grid_spec=pltpu.PrefetchScalarGridSpec(
            num_scalar_prefetch=1,
            grid=(rows // step,),
            in_specs=[
                rowwise(full),
                rowwise(full),
                pl.BlockSpec(fronts.shape, lambda i, p: (0, 0, 0), pipeline_mode=pl.Buffered(1)),
                fixed(1, units),
            ],
            out_specs=[rowwise(units)] * 3 + [pieces] * 2 + [fixed(1, units)],
            scratch_shapes=front_scratch(full, channels, units),
        ),
        out_shape=[jax.ShapeDtypeStruct((rows, units), jnp.bfloat16)] * 3
        + [jax.ShapeDtypeStruct((2, size, rows), jnp.float32)] * 2
        + [jax.ShapeDtypeStruct((1, units), jnp.float32)],
        compiler_params=pltpu.CompilerParams(vmem_limit_bytes=VMEM),
        cost_estimate=cost(15),
    )(place, normed, grad, fronts, bias[None])


def mid_kernel(
    place_ref,
    own_ref,
    near_ref,
    far_ref,
    last_ref,
    upper_ref,
    slope_ref,
    normed_ref,
    fronts_ref,
    bias_ref,
    affine_ref,
    mixed_ref,
    hidden_ref,
    up_grad_ref,
    out_keep_ref,
    out_send_ref,
    feature_keep_ref,
    feature_send_ref,
    sums_ref,
    bias_grad_ref,
    up_ref,
    down_ref,
    mix_ref,
    whole,
):
    place = place_ref[0]
    width = out_keep_ref.shape[2]
    unpack_fronts(fronts_ref, up_ref, down_ref, mix_ref)
    size = own_ref.shape[0]
    for offset, piece in enumerate((own_ref, near_ref, far_ref, last_ref)):
        start = pl.multiple_of((place ^ offset) * size, size)
        mixed_ref[pl.ds(start, size), :] = piece[...]
    lifted = dot(mixed_ref[...], mix_ref[...], 0, 0) + bias_ref[...]
    hidden = (upper_ref[...].astype(jnp.float32) * lifted).astype(jnp.bfloat16)
    up_grad = (slope_ref[...].astype(jnp.float32) * lifted).astype(jnp.bfloat16)
    hidden_ref[...] = hidden
    up_grad_ref[...] = up_grad

    @pl.when(pl.program_id(0) == 0)
    def _():
        bias_grad_ref[...] = jnp.zeros_like(bias_grad_ref)

    bias_grad_ref[...] += jnp.sum(up_grad.astype(jnp.float32), axis=0, keepdims=True)

    def part(offset):
        start = pl.multiple_of((place ^ offset) * width, width)
        return whole[:, pl.ds(start, width)].astype(jnp.bfloat16)

    whole[...] = dot(hidden, down_ref[...], 1, 1)
    out_keep_ref[0], out_keep_ref[1] = part(0), part(2)
    out_send_ref[0], out_send_ref[1] = part(1), part(3)
    feature = dot(up_grad, up_ref[...], 1, 1)
    whole[...] = feature
    feature_keep_ref[0], feature_keep_ref[1] = part(0), part(2)
    feature_send_ref[0], feature_send_ref[1] = part(1), part(3)
    one = jnp.sum(feature * affine_ref[0:1, :], axis=1, keepdims=True)
    shifted = normed_ref[...].astype(jnp.float32) - affine_ref[1:2, :]
    two = jnp.sum(feature * shifted, axis=1, keepdims=True)
    lane = lax.broadcasted_iota(jnp.int32, (feature.shape[0], 128), 1)
    sums_ref[...] = jnp.where(lane == 0, one, jnp.where(lane == 1, two, 0.0)).T[0:8, :]


def run_mid(parts, upper, slope, normed, fronts, bias, affine):
    rows, full = normed.shape
    units = fronts.shape[2]
    channels = 4 * parts[0].shape[0]
    width = full // 4
    step = 512
    place = lax.axis_index("chan").astype(jnp.int32).reshape(1)

    def fixed(*shape):
        return pl.BlockSpec(shape, lambda i, p: (0, 0))

    def rowwise(columns):
        return pl.BlockSpec((step, columns), lambda i, p: (i, 0))

    def columns(count):
        return pl.BlockSpec((count, step), lambda i, p: (0, i))

    pieces = pl.BlockSpec((2, step, width), lambda i, p: (0, i, 0))
    piece_shape = jax.ShapeDtypeStruct((2, rows, width), jnp.bfloat16)
    return pl.pallas_call(
        mid_kernel,
        grid_spec=pltpu.PrefetchScalarGridSpec(
            num_scalar_prefetch=1,
            grid=(rows // step,),
            in_specs=[
                columns(channels // 4),
                columns(channels // 4),
                columns(channels // 4),
                columns(channels // 4),
                rowwise(units),
                rowwise(units),
                rowwise(full),
                pl.BlockSpec(fronts.shape, lambda i, p: (0, 0, 0), pipeline_mode=pl.Buffered(1)),
                fixed(1, units),
                fixed(2, full),
            ],
            out_specs=[columns(channels)]
            + [rowwise(units)] * 2
            + [pieces] * 4
            + [columns(8), fixed(1, units)],
            scratch_shapes=front_scratch(full, channels, units)
            + [pltpu.VMEM((step, full), jnp.float32)],
        ),
        out_shape=[jax.ShapeDtypeStruct((channels, rows), jnp.bfloat16)]
        + [jax.ShapeDtypeStruct((rows, units), jnp.bfloat16)] * 2
        + [piece_shape] * 4
        + [
            jax.ShapeDtypeStruct((8, rows), jnp.float32),
            jax.ShapeDtypeStruct((1, units), jnp.float32),
        ],
        compiler_params=pltpu.CompilerParams(vmem_limit_bytes=VMEM),
        cost_estimate=cost(14),
    )(place, *parts, upper, slope, normed, fronts, bias[None], affine)


def payload_kernel(
    grad_ref, slope_ref, before_ref, gain_ref, bias_ref, sums_ref, payload_ref, bias_grad_ref
):
    count = grad_ref.shape[0]
    grad = (grad_ref[...].astype(jnp.float32) * slope_ref[...]).astype(jnp.bfloat16)
    payload_ref[:count, :] = grad
    grad = grad.astype(jnp.float32)
    centred = before_ref[...] - bias_ref[...] - gain_ref[:, 1:2]
    one = jnp.sum(grad * gain_ref[:, 0:1], axis=0, keepdims=True) + sums_ref[0:1, :]
    two = jnp.sum(grad * centred, axis=0, keepdims=True) + sums_ref[1:2, :]
    row = lax.broadcasted_iota(jnp.int32, (16, grad.shape[1]), 0)
    one_high = one.astype(jnp.bfloat16).astype(jnp.float32)
    two_high = two.astype(jnp.bfloat16).astype(jnp.float32)
    tail = jnp.where(row == 0, one_high, jnp.where(row == 1, one - one_high, 0.0))
    tail = jnp.where(row == 2, two_high, jnp.where(row == 3, two - two_high, tail))
    payload_ref[count:, :] = tail.astype(jnp.bfloat16)
    part = jnp.sum(grad, axis=1, keepdims=True)

    @pl.when(pl.program_id(0) == 0)
    def _():
        bias_grad_ref[...] = jnp.zeros_like(bias_grad_ref)

    bias_grad_ref[...] += part


def run_payload(grad, slope, before, gain, bias, sums):
    count, rows = grad.shape
    step = 512

    def columns(lines):
        return pl.BlockSpec((lines, step), lambda i: (0, i))

    def fixed(*shape):
        return pl.BlockSpec(shape, lambda i: (0, 0))

    return pl.pallas_call(
        payload_kernel,
        grid=(rows // step,),
        in_specs=[columns(count)] * 3 + [fixed(count, 2), fixed(count, 1), columns(8)],
        out_specs=[columns(count + 16), fixed(count, 1)],
        out_shape=[
            jax.ShapeDtypeStruct((count + 16, rows), jnp.bfloat16),
            jax.ShapeDtypeStruct((count, 1), jnp.float32),
        ],
        cost_estimate=cost(3),
    )(grad, slope, before, gain, bias[:, None], sums)


def final_kernel(
    _,
    own_ref,
    near_ref,
    far_ref,
    last_ref,
    rows_ref,
    kept_ref,
    sent_ref,
    passed_ref,
    tokens_ref,
    stats_ref,
    grad_ref,
    gain_ref,
    input_grad_ref,
    gain_grad_ref,
    shift_grad_ref,
    down_grad_ref,
):
    size = own_ref.shape[0] - 16
    row = lax.broadcasted_iota(jnp.int32, (16, 256), 0)
    lane = lax.broadcasted_iota(jnp.int32, (16, 256), 1)
    pick = jnp.where((row < 2) == (lane < 128), 1.0, 0.0)
    pick = jnp.where(row < 4, pick, 0.0).astype(jnp.bfloat16)
    normed_grad = (
        kept_ref[0].astype(jnp.float32)
        + sent_ref[0].astype(jnp.float32)
        + passed_ref[...].astype(jnp.float32)
    )
    totals = jnp.zeros((normed_grad.shape[0], 256), jnp.float32)
    for offset, piece in enumerate((own_ref, near_ref, far_ref, last_ref)):
        weights = rows_ref[:, offset * size : (offset + 1) * size]
        normed_grad += dot(piece[:size, :], weights, 0, 1)
        totals += dot(piece[size:, :], pick, 0, 0)
    scaled = normed_grad * gain_ref[...]
    centred = (tokens_ref[...].astype(jnp.float32) - stats_ref[:, 0:1]) * stats_ref[:, 64:65]
    grad = grad_ref[...].astype(jnp.float32)
    mean_one = totals[:, 0:1] * (1.0 / D)
    mean_two = totals[:, 128:129] * (1.0 / D)
    input_grad_ref[...] = stats_ref[:, 64:65] * (scaled - mean_one - centred * mean_two) + grad

    @pl.when(pl.program_id(0) == 0)
    def _():
        gain_grad_ref[...] = jnp.zeros_like(gain_grad_ref)
        shift_grad_ref[...] = jnp.zeros_like(shift_grad_ref)
        down_grad_ref[...] = jnp.zeros_like(down_grad_ref)

    gain_grad_ref[...] += jnp.sum(normed_grad * centred, axis=0, keepdims=True)
    shift_grad_ref[...] += jnp.sum(normed_grad, axis=0, keepdims=True)
    down_grad_ref[...] += jnp.sum(grad, axis=0, keepdims=True)


def run_final(parts, input_rows, kept, sent, passed, tokens, stats, grad, gain):
    rows, width = tokens.shape
    lines = parts[0].shape[0]
    step = 512
    place = lax.axis_index("chan").astype(jnp.int32).reshape(1)

    def fixed(*shape):
        return pl.BlockSpec(shape, lambda i, p: (0, 0))

    def rowwise(columns):
        return pl.BlockSpec((step, columns), lambda i, p: (i, 0))

    def columns(count):
        return pl.BlockSpec((count, step), lambda i, p: (0, i))

    piece = pl.BlockSpec((1, step, width), lambda i, p: (0, i, 0))
    return pl.pallas_call(
        final_kernel,
        grid_spec=pltpu.PrefetchScalarGridSpec(
            num_scalar_prefetch=1,
            grid=(rows // step,),
            in_specs=[columns(lines)] * 4
            + [
                fixed(*input_rows.shape),
                piece,
                piece,
                rowwise(width),
                rowwise(width),
                rowwise(128),
                pl.BlockSpec((step, width), lambda i, p: (i, p[0])),
                fixed(1, width),
            ],
            out_specs=[rowwise(width)] + [fixed(1, width)] * 3,
        ),
        out_shape=[jax.ShapeDtypeStruct((rows, width), jnp.float32)]
        + [jax.ShapeDtypeStruct((1, width), jnp.float32)] * 3,
        cost_estimate=cost(6),
    )(place, *parts, input_rows, kept, sent, passed, tokens, stats, grad, gain[None])


def grads_kernel(
    side_ref,
    outer_ref,
    normed_ref,
    mixed_ref,
    hidden_ref,
    up_ref,
    lifted_ref,
    down_send_ref,
    down_keep_ref,
    rest_send_ref,
    rest_keep_ref,
    whole,
    mix_whole,
):
    kept = side_ref[0]
    part = outer_ref.shape[1] // 2
    mix_part = mixed_ref.shape[0] // 2

    def half(scratch, size, side):
        return scratch[pl.ds(pl.multiple_of(side * size, size), size), :].astype(jnp.bfloat16)

    whole[...] = dot(outer_ref[...], hidden_ref[...], 0, 0)
    down_send_ref[0] = half(whole, part, 1 - kept)
    down_keep_ref[0] = half(whole, part, kept)
    whole[...] = dot(normed_ref[...], up_ref[...], 0, 0)
    rest_send_ref[0, :part, :] = half(whole, part, 1 - kept)
    rest_keep_ref[0, :part, :] = half(whole, part, kept)
    mix_whole[...] = dot(mixed_ref[...], lifted_ref[...], 1, 0)
    rest_send_ref[0, part:, :] = half(mix_whole, mix_part, 1 - kept)
    rest_keep_ref[0, part:, :] = half(mix_whole, mix_part, kept)


def run_grads(outer, normed, mixed, hidden, up, lifted):
    rows, full = outer.shape
    channels = mixed.shape[0]
    units = hidden.shape[1]
    devices = lax.axis_size("seq")
    half = devices // 2
    part, mix_part = full // devices, channels // devices
    side = (lax.axis_index("seq") & 1).astype(jnp.int32).reshape(1)

    def fixed(*shape):
        return pl.BlockSpec(shape, lambda i, p: (0, 0), pipeline_mode=pl.Buffered(1))

    whole = part + mix_part
    return pl.pallas_call(
        grads_kernel,
        grid_spec=pltpu.PrefetchScalarGridSpec(
            num_scalar_prefetch=1,
            grid=(half,),
            in_specs=[
                pl.BlockSpec((rows, 2 * part), lambda i, p: (0, i)),
                pl.BlockSpec((rows, 2 * part), lambda i, p: (0, i)),
                pl.BlockSpec((2 * mix_part, rows), lambda i, p: (i, 0)),
                fixed(rows, units),
                fixed(rows, units),
                fixed(rows, units),
            ],
            out_specs=[pl.BlockSpec((1, part, units), lambda i, p: (i, 0, 0))] * 2
            + [pl.BlockSpec((1, whole, units), lambda i, p: (i, 0, 0))] * 2,
            scratch_shapes=[
                pltpu.VMEM((2 * part, units), jnp.float32),
                pltpu.VMEM((2 * mix_part, units), jnp.float32),
            ],
        ),
        out_shape=[jax.ShapeDtypeStruct((half, part, units), jnp.bfloat16)] * 2
        + [jax.ShapeDtypeStruct((half, whole, units), jnp.bfloat16)] * 2,
        compiler_params=pltpu.CompilerParams(vmem_limit_bytes=VMEM),
        cost_estimate=cost(14),
    )(side, outer, normed, mixed, hidden, up, lifted)


def swap(value, distance):
    return lax.ppermute(value, "chan", [(i, i ^ distance) for i in range(4)])


def gather_parts(piece):
    far = swap(piece, 2)
    return piece, swap(piece, 1), far, swap(far, 1)


def after(value, *others):
    return lax.optimization_barrier((value,) + others)[0]


def to_channels(value, sequences):
    devices = lax.axis_size("seq")
    channels, tokens = value.shape
    share = channels // devices
    got = lax.all_to_all(value.reshape(devices, share, tokens), "seq", 0, 0, tiled=True)
    got = got.reshape(sequences, devices // sequences, share, tokens)
    return got.transpose(1, 0, 2, 3).reshape(devices // sequences, sequences * share, tokens)


def to_tokens(value, sequences):
    devices = lax.axis_size("seq")
    sources, count, tokens = value.shape
    share = count // sequences
    sent = value.reshape(sources, sequences, share, tokens).transpose(1, 0, 2, 3)
    got = lax.all_to_all(sent.reshape(devices, share, tokens), "seq", 0, 0, tiled=True)
    return got.reshape(devices * share, tokens)


def tile_rows(flat):
    width = flat.shape[-1]
    padded = -(-width // 128) * 128
    flat = jnp.pad(flat, [(0, 0)] * (flat.ndim - 1) + [(0, padded - width)])
    return flat.reshape(flat.shape[:-1] + (padded // 128, 128))


def planes(value, count):
    parts = []
    for _ in range(count):
        part = lax.reduce_precision(value, 8, 7)
        parts.append(part.astype(jnp.bfloat16))
        value = value - part
    return parts


def plain_grads(outer, normed, mixed, hidden, up, lifted):
    devices = lax.axis_size("seq")
    side = lax.axis_index("seq") & 1

    def parts(value):
        value = value.astype(jnp.bfloat16)
        return value.reshape(devices // 2, 2, value.shape[0] // devices, value.shape[1])

    def pick(value, index):
        return lax.dynamic_index_in_dim(value, index, 1, False)

    down = parts(dot(outer, hidden, 0, 0))
    rest = (parts(dot(normed, up, 0, 0)), parts(dot(mixed, lifted, 1, 0)))
    rest = jnp.concatenate(rest, axis=2)
    return (pick(down, 1 - side), pick(down, side), pick(rest, 1 - side), pick(rest, side))


def halve(sent, kept):
    devices = lax.axis_size("seq")
    got = lax.ppermute(sent, "seq", [(i, i ^ 1) for i in range(devices)])
    return (kept.astype(jnp.float32) + got.astype(jnp.float32)).astype(jnp.bfloat16)


def settle(halves):
    devices = lax.axis_size("seq")
    groups = [[i for i in range(devices) if i & 1 == side] for side in (0, 1)]
    got = lax.all_to_all(halves, "seq", 0, 0, axis_index_groups=groups, tiled=True)
    return jnp.sum(got.astype(jnp.float32), axis=0)


def per_device(
    tokens,
    norm_gain,
    norm_shift,
    up_weight,
    up_bias,
    input_weight,
    input_bias,
    mix_weight,
    mix_bias,
    down_weight,
    down_bias,
    decay_rate,
    decay_freq,
    step_log,
    read_real,
    read_imag,
    skip_gain,
    out_grad,
):
    row_count, width = tokens.shape
    devices = lax.axis_size("seq")
    place = lax.axis_index("chan")
    sequences = devices * row_count // LENGTH
    feature_rows, channels = input_weight.shape
    units = up_weight.shape[1]
    share = channels // devices
    modes_here = decay_rate.shape[0]
    modes = modes_here * devices
    near = swap(tokens, 1)
    early_rows = row_count // 4
    far, far_late = swap(tokens[:early_rows], 2), swap(tokens[early_rows:], 2)
    token_parts = (tokens, near, far, far_late, swap(far, 1), swap(far_late, 1))

    pair = jnp.stack([norm_gain, norm_shift])
    pairs = jnp.stack([pair, swap(pair, 1), swap(pair, 2), swap(pair, 3)])
    pairs = jnp.stack([pairs[place ^ i] for i in range(4)])
    fronts = jnp.concatenate([up_weight, down_weight.T, mix_weight])
    pairs = after(pairs, far, fronts)
    fronts = lax.all_gather(fronts, "seq", axis=0)
    small = (pairs.reshape(-1), up_bias, input_bias, mix_bias, down_bias, decay_rate, decay_freq)
    sizes = [v.shape[0] for v in small]
    small = tile_rows(jnp.concatenate(small))
    reads = jnp.concatenate([read_real, read_imag], axis=1).reshape(devices, share, 2 * modes_here)
    reads = jnp.pad(reads, ((0, 0), (0, 0), (0, 128 - 2 * modes_here)))
    copies = jnp.broadcast_to(small, (devices,) + small.shape)
    exact = jnp.concatenate([reads, copies], axis=1)
    exact_rows = exact.shape[1]
    weights = jnp.broadcast_to(input_weight, (devices,) + input_weight.shape)
    got = jnp.concatenate(planes(exact, 3) + [weights], axis=1)
    got = lax.all_to_all(got, "seq", 0, 0, tiled=True)
    input_full = got[:, 3 * exact_rows :].reshape(4 * width, channels)

    def exact_part(start, stop):
        rows = [got[:, i * exact_rows + start : i * exact_rows + stop] for i in range(3)]
        rows = [r.astype(jnp.float32) for r in rows]
        return rows[0] + (rows[1] + rows[2])

    small = exact_part(share, exact_rows).reshape(devices, -1)
    parts, spot = [], 0
    for size in sizes:
        parts.append(small[:, spot : spot + size])
        spot += size
    affine = parts[0].reshape(devices, 4, 2, -1).transpose(2, 1, 0, 3).reshape(2, 4 * width)
    input_shift = parts[2].reshape(-1)

    normed, values_low, in_slope, pre_in, stats = run_norm(
        token_parts, affine, input_full, input_shift
    )
    values = to_channels(values_low, sequences)

    got = after(got, normed)
    parts = lax.optimization_barrier(tuple(parts) + (normed,))[:-1]
    reads = exact_part(0, share)[:, :, : 2 * modes_here].transpose(1, 0, 2)
    read_re = reads[:, :, :modes_here].reshape(share, modes)
    read_im = reads[:, :, modes_here:].reshape(share, modes)
    up_shift, _, mix_shift, down_shift, rate, freq = (p.reshape(-1) for p in parts[1:])
    gain_own = lax.dynamic_slice_in_dim(affine[0], place * width, width)

    spacing = jnp.exp(step_log)
    damping = spacing[:, None] * rate[None, :]
    rotation = spacing[:, None] * freq[None, :]
    inflow = -jnp.expm1(-damping)
    extents = 2.0 ** jnp.arange(8)[None, :, None]
    length = jnp.exp(-damping[:, None] * extents)
    angle = rotation[:, None] * extents
    power_re, power_im = length * jnp.cos(angle), length * jnp.sin(angle)

    def repeat(value):
        return jnp.tile(value, (sequences,) + (1,) * (value.ndim - 1))

    def rows(value_re, value_im):
        return repeat(jnp.concatenate([value_re, value_im], axis=1)[:, None])

    power, out_table, in_table, toeplitz = make_tables(
        repeat(power_re), repeat(power_im), repeat(read_re), repeat(read_im), repeat(inflow)
    )
    jump = rows(power_re[:, 7], power_im[:, 7])[:, 0]
    flow = rows(inflow, inflow)
    lead = rows(*cmul(read_re, read_im, power_re[:, 0], power_im[:, 0]))
    skip = repeat(skip_gain)

    pieces = gather_parts(after(input_full, normed))
    pieces = [lax.dynamic_slice_in_dim(p, place * width, width, 0) for p in pieces]
    input_rows = jnp.concatenate(pieces, axis=1)
    in_gain = jnp.dot(
        input_full.T.astype(jnp.float32), affine.T, precision=lax.Precision.HIGHEST
    )
    mixed, starts, values_split = run_forward(
        after(values, input_rows, in_gain), skip, jump, flow, lead, out_table, in_table, toeplitz
    )
    mixed_tokens = to_tokens(mixed, sequences)

    upper, up_slope, lifted_grad, channel_keep, channel_send, mix_bias_part = run_gate(
        after(normed, mixed), out_grad, fronts, 4 * channels, up_shift
    )
    channel_sent = swap(after(channel_send, mixed_tokens), 1)
    mixed_parts = gather_parts(mixed_tokens)
    channel_passed = (channel_keep[1] + channel_sent[1]).astype(jnp.bfloat16)
    channel_sum = channel_keep[0] + channel_sent[0]
    channel_far = swap(channel_passed, 2)
    mixed_grad = (channel_sum + channel_far.astype(jnp.float32)).astype(jnp.bfloat16)
    grads = to_channels(mixed_grad, sequences)

    (
        mixed_full,
        hidden,
        up_pre_grad,
        out_keep,
        out_send,
        feature_keep,
        feature_send,
        up_sums,
        up_bias_part,
    ) = run_mid(
        (after(mixed_parts[0], channel_passed),) + mixed_parts[1:],
        upper,
        up_slope,
        normed,
        fronts,
        mix_shift,
        affine,
    )
    out_sent, feature_sent = swap(out_send, 1), swap(feature_send, 1)

    def passed(keep, sent):
        return (keep[1].astype(jnp.float32) + sent[1].astype(jnp.float32)).astype(jnp.bfloat16)

    feature_passed = passed(feature_keep, feature_sent)
    out_passed = passed(out_keep, out_sent)
    make_grads = run_grads if feature_rows % 128 == 0 else plain_grads
    down_send, down_keep, rest_send, rest_keep = make_grads(
        out_grad, normed, mixed_full, after(hidden, mixed_grad), up_pre_grad, lifted_grad
    )
    feature_far = swap(feature_passed, 2)
    down_sent, rest_sent = after(down_send, grads), after(rest_send, grads)
    grads = after(grads, down_send, feature_passed, out_passed)
    values_grad, later, grads_split = run_backward(
        grads, skip, jump, flow, lead, out_table, in_table, toeplitz
    )
    values_back = to_tokens(after(values_grad, feature_far), sequences)
    out_far = swap(after(out_passed, values_grad), 2)
    sums, skip_sums = run_sums(grads_split, values_split, starts, later, power)
    down_half = halve(down_sent, after(down_keep, values_grad))
    rest_half = halve(rest_sent, after(rest_keep, values_grad))
    down_total = settle(after(down_half, values_back))
    rest_total = settle(after(rest_half, values_back, down_total))
    down_weight_grad = down_total.T
    up_weight_grad, mix_weight_grad = rest_total[:feature_rows], rest_total[feature_rows:]
    inputs = tokens.astype(jnp.float32)
    output = (
        out_keep[0].astype(jnp.float32)
        + out_sent[0].astype(jnp.float32)
        + out_far.astype(jnp.float32)
        + down_shift
        + inputs
    )

    payload, input_bias_part = run_payload(
        after(values_back, sums, out_far, down_half), in_slope, pre_in, in_gain, input_shift, up_sums
    )
    payload_parts = gather_parts(payload)
    input_part = dot(normed, payload[:channels], 0, 1)
    input_grad, gain_part, shift_part, down_bias_part = run_final(
        payload_parts,
        input_rows,
        feature_keep,
        feature_sent,
        feature_far,
        tokens,
        stats,
        out_grad,
        gain_own,
    )

    sums = jnp.concatenate([sums[:, :4], sums[:, 4:8] * flow[:, :, :modes], sums[:, 8:]], axis=1)
    sums = jnp.sum(sums.reshape((sequences, share) + sums.shape[1:]), axis=0)
    skip_grad = jnp.sum(skip_sums.reshape(sequences, share, BLOCK), axis=(0, 2))
    out_zero = cmul(power_re[:, 0], power_im[:, 0], sums[:, 0], sums[:, 1])
    out_one = cmul(
        power_re[:, 0], power_im[:, 0], sums[:, 0] + sums[:, 2], sums[:, 1] + sums[:, 3]
    )
    chained = cmul(power_re[:, 7], power_im[:, 7], sums[:, 8], sums[:, 9])
    local_zero, local_one = (sums[:, 10], sums[:, 11]), (sums[:, 12], sums[:, 13])
    read_re_grad = out_zero[0] + inflow * local_zero[0]
    read_im_grad = -out_zero[1] - inflow * local_zero[1]
    turn = cmul(
        read_re, read_im, out_one[0] + inflow * local_one[0], out_one[1] + inflow * local_one[1]
    )
    turn_re = turn[0] + sums[:, 6] + BLOCK * chained[0]
    turn_im = turn[1] + sums[:, 7] + BLOCK * chained[1]
    inflow_grad = sums[:, 4] / inflow + read_re * local_zero[0] - read_im * local_zero[1]
    damping_grad = jnp.exp(-damping) * inflow_grad - turn_re
    rotation_grad = -turn_im
    step_log_grad = spacing * jnp.sum(
        rate[None, :] * damping_grad + freq[None, :] * rotation_grad, axis=1
    )
    rates = jnp.stack(
        [
            jnp.sum(spacing[:, None] * damping_grad, axis=0),
            jnp.sum(spacing[:, None] * rotation_grad, axis=0),
        ]
    )
    rates = rates + swap(rates, 1)
    rates = rates + swap(rates, 2)

    read_grads = jnp.stack([read_re_grad, read_im_grad], axis=1)
    read_grads = read_grads.reshape(share, 2, devices, modes_here).transpose(2, 0, 1, 3)
    read_grads = read_grads.reshape(devices, share, 2 * modes_here)
    read_grads = jnp.pad(read_grads, ((0, 0), (0, 0), (0, 128 - 2 * modes_here)))

    def line_up(vectors):
        vectors = [v.reshape(devices, -1) for v in vectors]
        sizes = [v.shape[1] for v in vectors]
        return tile_rows(jnp.concatenate(vectors, axis=1)), sizes

    def take_apart(flat, sizes):
        parts, spot = [], 0
        for size in sizes:
            parts.append(flat[spot : spot + size])
            spot += size
        return parts

    vectors, sizes = line_up(
        (
            up_bias_part,
            input_bias_part,
            mix_bias_part,
            rates[0],
            rates[1],
            gain_part,
            shift_part,
            down_bias_part,
        )
    )
    input_part = input_part.reshape(devices, feature_rows, channels)
    parcel = after(jnp.concatenate([read_grads, vectors], axis=1), rest_total)
    exact_rows = parcel.shape[1]
    parcel = jnp.concatenate(planes(parcel, 2) + [input_part.astype(jnp.bfloat16)], axis=1)
    late = lax.all_to_all(parcel, "seq", 0, 0, tiled=True).astype(jnp.float32)
    input_weight_grad = jnp.sum(late[:, 2 * exact_rows :], axis=0)
    late = late[:, :exact_rows] + late[:, exact_rows : 2 * exact_rows]
    read_late = late[:, :share, : 2 * modes_here].reshape(channels, 2 * modes_here)
    late = take_apart(jnp.sum(late[:, share:], axis=0).reshape(-1), sizes)
    up_bias_grad, input_bias_grad, mix_bias_grad, rate_out, freq_out = late[:5]
    gain_grad, shift_grad, down_bias_grad = late[5:]
    return (
        output,
        input_grad,
        gain_grad,
        shift_grad,
        up_weight_grad,
        up_bias_grad,
        input_weight_grad,
        input_bias_grad,
        mix_weight_grad,
        mix_bias_grad,
        down_weight_grad,
        down_bias_grad,
        rate_out,
        freq_out,
        step_log_grad,
        read_late[:, :modes_here],
        read_late[:, modes_here:],
        skip_grad,
    )


def solution(mesh):
    return jax.shard_map(
        per_device,
        mesh=mesh,
        in_specs=(
            P("seq", "chan"),
            P(("chan", "seq")),
            P(("chan", "seq")),
            P("seq", "chan"),
            P(("chan", "seq")),
            P("seq", "chan"),
            P(("chan", "seq")),
            P("seq", "chan"),
            P(("chan", "seq")),
            P("chan", "seq"),
            P(("chan", "seq")),
            P("seq"),
            P("seq"),
            P(("chan", "seq")),
            P("chan", "seq"),
            P("chan", "seq"),
            P(("chan", "seq")),
            P("seq", None),
        ),
        out_specs=(
            P("seq", "chan"),
            P("seq", "chan"),
            P(("chan", "seq")),
            P(("chan", "seq")),
            P("seq", "chan"),
            P(("chan", "seq")),
            P("seq", "chan"),
            P(("chan", "seq")),
            P("seq", "chan"),
            P(("chan", "seq")),
            P("chan", "seq"),
            P(("chan", "seq")),
            P("seq"),
            P("seq"),
            P(("chan", "seq")),
            P("chan", "seq"),
            P("chan", "seq"),
            P(("chan", "seq")),
        ),
        check_vma=False,
    )
```

```python
from functools import partial
import math

import jax
import jax.numpy as jnp
from jax import lax
from jax.experimental import pallas as pl
from jax.experimental.pallas import tpu as pltpu
from jax.sharding import PartitionSpec as P

D = 1024
LENGTH = 16384
EPSILON = 1e-05


BLOCK = 128
MEGA = 1024 * 1024
VMEM = 56 * MEGA


def dot(left, right, left_dim, right_dim):
    return lax.dot_general(
        left, right, (((left_dim,), (right_dim,)), ((), ())), preferred_element_type=jnp.float32
    )


def cmul(a_re, a_im, b_re, b_im):
    return (a_re * b_re - a_im * b_im, a_re * b_im + a_im * b_re)


def grow(first, reversed_rows, mode_powers, store):
    row = lax.broadcasted_iota(jnp.int32, (8, first[0].shape[1]), 0)
    exponent = 7 - row if reversed_rows else row
    part = (
        jnp.broadcast_to(first[0], row.shape),
        jnp.broadcast_to(first[1], row.shape),
    )
    for level in range(3):
        factor_re, factor_im = mode_powers(level)
        taken = (exponent >> level) & 1 == 1
        part = cmul(*part, jnp.where(taken, factor_re, 1.0), jnp.where(taken, factor_im, 0.0))
    spot = BLOCK - 8 if reversed_rows else 0
    store(spot, part[0], part[1])
    whole = part
    size, level = 8, 3
    while size < BLOCK:
        factor = mode_powers(level)
        fresh = cmul(*whole, *factor)
        spot = BLOCK - 2 * size if reversed_rows else size
        store(spot, *fresh)
        pair = (fresh, whole) if reversed_rows else (whole, fresh)
        whole = tuple(jnp.concatenate([p, q], axis=0) for p, q in zip(*pair))
        size, level = 2 * size, level + 1


def tables_kernel(
    power_re_ref,
    power_im_ref,
    read_re_ref,
    read_im_ref,
    inflow_ref,
    power_ref,
    out_table_ref,
    in_table_ref,
    toeplitz_ref,
):
    modes = power_re_ref.shape[2]
    lower, upper = slice(0, modes), slice(modes, 2 * modes)

    def mode_powers(level):
        return (power_re_ref[0, level : level + 1, :], power_im_ref[0, level : level + 1, :])

    inflow = inflow_ref[0]
    one, none = jnp.ones_like(inflow), jnp.zeros_like(inflow)

    def store_power(spot, part_re, part_im):
        rows = slice(spot, spot + part_re.shape[0])
        power_ref[0, rows, lower] = part_re
        power_ref[0, rows, upper] = part_im

    grow((one, none), False, mode_powers, store_power)
    exact = jnp.concatenate([power_ref[0, :, lower], -power_ref[0, :, upper]], axis=1)
    rounded = exact.astype(jnp.bfloat16)
    out_table_ref[0] = rounded
    rest = (exact - rounded.astype(jnp.float32)).astype(jnp.bfloat16)
    backward = []

    def store_in(spot, part_re, part_im):
        backward.append((spot, part_re, part_im))

    grow((one, none), True, mode_powers, store_in)
    backward.sort(key=lambda entry: entry[0])
    in_table_ref[0, :, lower] = jnp.concatenate([e[1] for e in backward], 0).astype(jnp.bfloat16)
    in_table_ref[0, :, upper] = jnp.concatenate([e[2] for e in backward], 0).astype(jnp.bfloat16)
    weight = jnp.concatenate([read_re_ref[0] * inflow, read_im_ref[0] * inflow], axis=1)
    high = weight.astype(jnp.bfloat16).astype(jnp.float32)
    row = lax.broadcasted_iota(jnp.int32, (16, 2 * modes), 0)
    probe = jnp.where(row == 0, high, jnp.where(row == 1, weight - high, 0.0))
    probe = probe.astype(jnp.bfloat16)
    lags = dot(probe, rounded, 1, 1) + dot(probe, rest, 1, 1)
    kernel_row = jnp.sum(lags, axis=0, keepdims=True)
    skewed = pltpu.roll(
        jnp.broadcast_to(kernel_row, (BLOCK, BLOCK)), 0, 1, stride=1, stride_axis=0
    )
    source = lax.broadcasted_iota(jnp.int32, (BLOCK, BLOCK), 0)
    target = lax.broadcasted_iota(jnp.int32, (BLOCK, BLOCK), 1)
    skewed = jnp.where(target >= source, skewed, 0.0)
    coarse = skewed.astype(jnp.bfloat16)
    toeplitz_ref[0, :BLOCK, :] = coarse
    toeplitz_ref[0, BLOCK:, :] = (skewed - coarse.astype(jnp.float32)).astype(jnp.bfloat16)


def make_tables(power_re, power_im, read_re, read_im, inflow):
    count, levels, modes = power_re.shape

    def spec(*shape):
        return pl.BlockSpec((1,) + shape, lambda i: (i, 0, 0))

    return pl.pallas_call(
        tables_kernel,
        grid=(count,),
        in_specs=[spec(levels, modes)] * 2 + [spec(1, modes)] * 3,
        out_specs=[
            spec(BLOCK, 2 * modes),
            spec(BLOCK, 2 * modes),
            spec(BLOCK, 2 * modes),
            spec(2 * BLOCK, BLOCK),
        ],
        out_shape=[
            jax.ShapeDtypeStruct((count, BLOCK, 2 * modes), jnp.float32),
            jax.ShapeDtypeStruct((count, BLOCK, 2 * modes), jnp.bfloat16),
            jax.ShapeDtypeStruct((count, BLOCK, 2 * modes), jnp.bfloat16),
            jax.ShapeDtypeStruct((count, 2 * BLOCK, BLOCK), jnp.bfloat16),
        ],
        compiler_params=pltpu.CompilerParams(vmem_limit_bytes=VMEM),
        cost_estimate=cost(12),
    )(power_re, power_im, read_re[:, None], read_im[:, None], inflow[:, None])


def spread_tokens(ref, scratch):
    sources, count, tokens = ref.shape
    per_source = tokens // BLOCK
    for source in range(sources):
        for part in range(per_source):
            row = (source * per_source + part) * count
            tile = ref[source, :, part * BLOCK : (part + 1) * BLOCK]
            scratch[row : row + count, :] = tile.astype(jnp.float32)


def gather_tokens(scratch, ref):
    sources, count, tokens = ref.shape
    per_source = tokens // BLOCK
    for source in range(sources):
        for part in range(per_source):
            row = (source * per_source + part) * count
            ref[source, :, part * BLOCK : (part + 1) * BLOCK] = scratch[
                row : row + count, :
            ].astype(ref.dtype)


def put_rows(states, rows, value):
    for tile in range(states.shape[0]):
        states[tile, rows, :] = value[:, tile * 128 : (tile + 1) * 128]


def take_rows(states, rows):
    return jnp.concatenate([states[tile, rows, :] for tile in range(states.shape[0])], axis=1)


def run_chain(states, jump_ref, sign, count, blocks, order):
    tiles = states.shape[0] // 2
    jumps = [
        (
            jump_ref[:, t * 128 : (t + 1) * 128],
            sign * jump_ref[:, (tiles + t) * 128 : (tiles + t + 1) * 128],
        )
        for t in range(tiles)
    ]

    def step(turn, state):
        rows = pl.ds(pl.multiple_of(order(turn) * count, count), count)
        following = []
        for t in range(tiles):
            end_re, end_im = states[t, rows, :], states[tiles + t, rows, :]
            states[t, rows, :] = state[t][0]
            states[tiles + t, rows, :] = state[t][1]
            next_re, next_im = cmul(*jumps[t], *state[t])
            following.append((next_re + end_re, next_im + end_im))
        return tuple(following)

    blank = jnp.zeros((count, 128), jnp.float32)
    lax.fori_loop(0, blocks, step, ((blank, blank),) * tiles, unroll=2)


GROUP = 4


def halves(total):
    first = lambda i: (jnp.minimum(i, total - 1), 0, 0)
    second = lambda i: (jnp.maximum(i - total, 0), 0, 0)
    return first, second


def two_passes(states, total, begin, enter, middle, leave, end):
    turn = pl.program_id(0)
    blocks = states.shape[1] // (total * GROUP)

    def channel_rows(first):
        channels = [(turn - first) * GROUP + index for index in range(GROUP)]
        return [pl.ds(c, blocks, stride=total * GROUP) for c in channels]

    pl.when(turn == 0)(begin)

    @pl.when(turn < total)
    def _():
        for index, rows in enumerate(channel_rows(0)):
            enter(index, rows)

    pl.when(turn == total)(middle)

    @pl.when(turn >= total)
    def _():
        for index, rows in enumerate(channel_rows(total)):
            leave(index, rows, (turn - total) * GROUP + index)

    pl.when(turn == 2 * total - 1)(end)


def forward_kernel(
    values_ref,
    skip_ref,
    jump_ref,
    inflow_ref,
    lead_ref,
    out_table_ref,
    in_table_ref,
    toeplitz_ref,
    mixed_ref,
    starts_ref,
    split_ref,
    tokens,
    states,
):
    count = values_ref.shape[1]
    blocks = states.shape[1] // count
    modes = states.shape[0] * 64

    def enter(index, rows):
        own = tokens[rows, :].astype(jnp.bfloat16)
        split_ref[index] = own
        put_rows(states, rows, dot(own, in_table_ref[index], 1, 0) * inflow_ref[index])

    def leave(index, rows, channel):
        start = take_rows(states, rows)
        starts_ref[index] = start.astype(jnp.bfloat16)
        lead = lead_ref[index]
        weighted = cmul(lead[:, :modes], lead[:, modes:], start[:, :modes], start[:, modes:])
        weighted = jnp.concatenate(weighted, axis=1).astype(jnp.bfloat16)
        own = tokens[rows, :]
        own_low = own.astype(jnp.bfloat16)
        mixed = dot(weighted, out_table_ref[index], 1, 1)
        mixed += dot(own_low, toeplitz_ref[index, :BLOCK, :], 1, 0)
        mixed += dot(own_low, toeplitz_ref[index, BLOCK:, :], 1, 0)
        tokens[rows, :] = mixed + skip_ref[channel] * own

    two_passes(
        states,
        count // GROUP,
        lambda: spread_tokens(values_ref, tokens),
        enter,
        lambda: run_chain(states, jump_ref, 1.0, count, blocks, lambda turn: turn),
        leave,
        lambda: gather_tokens(tokens, mixed_ref),
    )


def run_forward(values, skip, jump, inflow, lead, out_table, in_table, toeplitz):
    sources, count, tokens = values.shape
    blocks = sources * tokens // BLOCK
    width = jump.shape[1]
    total = count // GROUP
    first, second = halves(total)
    whole = pl.BlockSpec(values.shape, lambda i: (0, 0, 0), pipeline_mode=pl.Buffered(1))
    return pl.pallas_call(
        forward_kernel,
        grid=(2 * total,),
        in_specs=[
            whole,
            pl.BlockSpec(memory_space=pltpu.SMEM),
            pl.BlockSpec(jump.shape, lambda i: (0, 0), pipeline_mode=pl.Buffered(1)),
            pl.BlockSpec((GROUP, 1, width), first),
            pl.BlockSpec((GROUP, 1, width), second),
            pl.BlockSpec((GROUP, BLOCK, width), second),
            pl.BlockSpec((GROUP, BLOCK, width), first),
            pl.BlockSpec((GROUP, 2 * BLOCK, BLOCK), second),
        ],
        out_specs=[
            whole,
            pl.BlockSpec((GROUP, blocks, width), second),
            pl.BlockSpec((GROUP, blocks, BLOCK), first),
        ],
        out_shape=[
            jax.ShapeDtypeStruct(values.shape, jnp.bfloat16),
            jax.ShapeDtypeStruct((count, blocks, width), jnp.bfloat16),
            jax.ShapeDtypeStruct((count, blocks, BLOCK), jnp.bfloat16),
        ],
        scratch_shapes=[
            pltpu.VMEM((blocks * count, BLOCK), jnp.float32),
            pltpu.VMEM((width // 128, blocks * count, 128), jnp.float32),
        ],
        compiler_params=pltpu.CompilerParams(vmem_limit_bytes=VMEM),
        cost_estimate=cost(20),
    )(values, skip, jump, inflow, lead, out_table, in_table, toeplitz)


def backward_kernel(
    grads_ref,
    skip_ref,
    jump_ref,
    inflow_ref,
    lead_ref,
    out_table_ref,
    in_table_ref,
    toeplitz_ref,
    values_grad_ref,
    later_ref,
    split_ref,
    grads,
    states,
):
    count = grads_ref.shape[1]
    blocks = states.shape[1] // count
    modes = states.shape[0] * 64

    def enter(index, rows):
        own = grads[rows, :].astype(jnp.bfloat16)
        split_ref[index] = own
        lead = lead_ref[index]
        back = dot(own, out_table_ref[index], 1, 0)
        back = cmul(lead[:, :modes], -lead[:, modes:], back[:, :modes], back[:, modes:])
        put_rows(states, rows, jnp.concatenate(back, axis=1))

    def leave(index, rows, channel):
        later = take_rows(states, rows)
        later_ref[index] = later.astype(jnp.bfloat16)
        later = (later * inflow_ref[index]).astype(jnp.bfloat16)
        grad = grads[rows, :]
        grad_low = grad.astype(jnp.bfloat16)
        back = dot(later, in_table_ref[index], 1, 1)
        back += dot(grad_low, toeplitz_ref[index, :BLOCK, :], 1, 1)
        back += dot(grad_low, toeplitz_ref[index, BLOCK:, :], 1, 1)
        grads[rows, :] = back + skip_ref[channel] * grad

    two_passes(
        states,
        count // GROUP,
        lambda: spread_tokens(grads_ref, grads),
        enter,
        lambda: run_chain(states, jump_ref, -1.0, count, blocks, lambda turn: blocks - 1 - turn),
        leave,
        lambda: gather_tokens(grads, values_grad_ref),
    )


def run_backward(grads, skip, jump, inflow, lead, out_table, in_table, toeplitz):
    sources, count, tokens = grads.shape
    blocks = sources * tokens // BLOCK
    width = jump.shape[1]
    total = count // GROUP
    first, second = halves(total)
    whole = pl.BlockSpec(grads.shape, lambda i: (0, 0, 0), pipeline_mode=pl.Buffered(1))
    return pl.pallas_call(
        backward_kernel,
        grid=(2 * total,),
        in_specs=[
            whole,
            pl.BlockSpec(memory_space=pltpu.SMEM),
            pl.BlockSpec(jump.shape, lambda i: (0, 0), pipeline_mode=pl.Buffered(1)),
            pl.BlockSpec((GROUP, 1, width), second),
            pl.BlockSpec((GROUP, 1, width), first),
            pl.BlockSpec((GROUP, BLOCK, width), first),
            pl.BlockSpec((GROUP, BLOCK, width), second),
            pl.BlockSpec((GROUP, 2 * BLOCK, BLOCK), second),
        ],
        out_specs=[
            whole,
            pl.BlockSpec((GROUP, blocks, width), second),
            pl.BlockSpec((GROUP, blocks, BLOCK), first),
        ],
        out_shape=[
            jax.ShapeDtypeStruct(grads.shape, jnp.bfloat16),
            jax.ShapeDtypeStruct((count, blocks, width), jnp.bfloat16),
            jax.ShapeDtypeStruct((count, blocks, BLOCK), jnp.bfloat16),
        ],
        scratch_shapes=[
            pltpu.VMEM((blocks * count, BLOCK), jnp.float32),
            pltpu.VMEM((width // 128, blocks * count, 128), jnp.float32),
        ],
        compiler_params=pltpu.CompilerParams(vmem_limit_bytes=VMEM),
        cost_estimate=cost(20),
    )(grads, skip, jump, inflow, lead, out_table, in_table, toeplitz)


def sums_kernel(grad_ref, value_ref, start_ref, later_ref, power_ref, sums_ref, skip_ref):
    for index in range(grad_ref.shape[0]):
        channel_sums(
            *(r.at[index] for r in (grad_ref, value_ref, start_ref, later_ref, power_ref)),
            sums_ref.at[index],
            skip_ref.at[index],
        )


def channel_sums(grad_ref, value_ref, start_ref, later_ref, power_ref, sums_ref, skip_ref):
    modes = power_ref.shape[1] // 2
    row = lax.broadcasted_iota(jnp.int32, (BLOCK, BLOCK), 0)
    lane = lax.broadcasted_iota(jnp.int32, (BLOCK, BLOCK), 1)
    flip = jnp.where(row + lane == BLOCK - 1, 1.0, 0.0).astype(jnp.bfloat16)

    def fold(part):
        return jnp.sum(part.reshape(part.shape[0] // 8, 8, part.shape[1]), axis=0)

    grad, value = grad_ref[...], value_ref[...]
    start, later = start_ref[...], later_ref[...]
    product = grad.astype(jnp.float32) * value.astype(jnp.float32)
    skip_ref[...] = jnp.sum(product, axis=0, keepdims=True)
    turned = dot(value, flip, 1, 0).astype(jnp.bfloat16)
    out_sum = dot(grad, start, 0, 0)
    in_sum = dot(turned, later, 0, 0)
    cross = dot(grad, turned, 0, 0)
    cross = jnp.where(row + lane >= BLOCK - 1, cross, 0.0)
    lags = jnp.sum(pltpu.roll(cross, 1, 1, stride=1, stride_axis=0), axis=0, keepdims=True)
    lags = jnp.sum(jnp.where(row == lane, lags, 0.0), axis=1, keepdims=True)
    weight = lax.broadcasted_iota(jnp.int32, (BLOCK, modes), 0).astype(jnp.float32)
    power_re, power_im = power_ref[:, :modes], power_ref[:, modes:]
    terms = []
    for total, sign in ((out_sum, 1.0), (in_sum, -1.0)):
        term_re, term_im = cmul(power_re, power_im, total[:, :modes], sign * total[:, modes:])
        terms += [fold(term_re), fold(term_im), fold(weight * term_re), fold(weight * term_im)]
    later_re, later_im = (later[:, :modes].astype(jnp.float32), later[:, modes:].astype(jnp.float32))
    start_re, start_im = (start[:, :modes].astype(jnp.float32), start[:, modes:].astype(jnp.float32))
    terms += [
        fold(later_re * start_re + later_im * start_im),
        fold(later_re * start_im - later_im * start_re),
    ]
    local_re, local_im = power_re * lags, power_im * lags
    terms += [fold(local_re), fold(local_im), fold(weight * local_re), fold(weight * local_im)]
    for index, term in enumerate(terms):
        sums_ref[index : index + 1, :] = jnp.sum(term, axis=0, keepdims=True)


def run_sums(grads, values, starts, later, power):
    count, blocks, width = starts.shape
    group = 4

    def spec(*shape):
        return pl.BlockSpec((group,) + shape, lambda i: (i, 0, 0))

    return pl.pallas_call(
        sums_kernel,
        grid=(count // group,),
        in_specs=[spec(blocks, BLOCK)] * 2 + [spec(blocks, width)] * 2 + [spec(BLOCK, width)],
        out_specs=[spec(16, width // 2), spec(1, BLOCK)],
        out_shape=[
            jax.ShapeDtypeStruct((count, 16, width // 2), jnp.float32),
            jax.ShapeDtypeStruct((count, 1, BLOCK), jnp.float32),
        ],
        compiler_params=pltpu.CompilerParams(vmem_limit_bytes=VMEM),
        cost_estimate=cost(18),
    )(grads, values, starts, later, power)


def cost(microseconds):
    return pl.CostEstimate(
        flops=int(microseconds * 1e9), bytes_accessed=int(microseconds * 1e6), transcendentals=0
    )


def erf_parts(value):
    half = 0.5 * (1.0 + lax.erf(value * (1.0 / math.sqrt(2.0))))
    density = jnp.exp(-0.5 * value * value) * (1.0 / math.sqrt(2.0 * math.pi))
    return value * half, half + value * density


def norm_kernel(
    early_steps,
    place_ref,
    own_ref,
    near_ref,
    far_ref,
    far_late_ref,
    last_ref,
    last_late_ref,
    affine_ref,
    weight_ref,
    bias_ref,
    normed_ref,
    values_ref,
    slope_ref,
    before_ref,
    stats_ref,
    whole,
):
    place = place_ref[0]
    width = own_ref.shape[1]
    early = pl.program_id(0) < early_steps
    parts = (
        own_ref[...],
        near_ref[...],
        jnp.where(early, far_ref[...], far_late_ref[...]),
        jnp.where(early, last_ref[...], last_late_ref[...]),
    )
    for offset, part in enumerate(parts):
        start = pl.multiple_of((place ^ offset) * width, width)
        whole[:, pl.ds(start, width)] = part.astype(jnp.float32)
    inputs = whole[...]
    average = jnp.mean(inputs, axis=1, keepdims=True)
    spread = jnp.mean(inputs * inputs, axis=1, keepdims=True) - average * average
    inverse = lax.rsqrt(spread + EPSILON)
    normed = (inputs - average) * inverse * affine_ref[0:1, :] + affine_ref[1:2, :]
    normed = normed.astype(jnp.bfloat16)
    normed_ref[...] = normed
    before = dot(weight_ref[...], normed, 0, 1) + bias_ref[...]
    values, slope = erf_parts(before)
    values_ref[...] = values.astype(jnp.bfloat16)
    slope_ref[...] = slope
    before_ref[...] = before
    lane = lax.broadcasted_iota(jnp.int32, (inputs.shape[0], 128), 1)
    stats_ref[...] = jnp.where(lane < 64, average, inverse)


def run_norm(parts, affine, weight, bias):
    rows, width = parts[0].shape
    full, channels = weight.shape
    step = 512
    place = lax.axis_index("chan").astype(jnp.int32).reshape(1)
    half = parts[2].shape[0] // step
    full_rows = pl.BlockSpec((step, width), lambda i, p: (i, 0))
    first_rows = pl.BlockSpec((step, width), lambda i, p: (jnp.minimum(i, half - 1), 0))
    later_rows = pl.BlockSpec((step, width), lambda i, p: (jnp.maximum(i - half, 0), 0))
    return pl.pallas_call(
        partial(norm_kernel, half),
        grid_spec=pltpu.PrefetchScalarGridSpec(
            num_scalar_prefetch=1,
            grid=(rows // step,),
            in_specs=[
                full_rows,
                full_rows,
                first_rows,
                later_rows,
                first_rows,
                later_rows,
                pl.BlockSpec((2, full), lambda i, p: (0, 0)),
                pl.BlockSpec((full, channels), lambda i, p: (0, 0)),
                pl.BlockSpec((channels, 1), lambda i, p: (0, 0)),
            ],
            out_specs=[
                pl.BlockSpec((step, full), lambda i, p: (i, 0)),
                pl.BlockSpec((channels, step), lambda i, p: (0, i)),
                pl.BlockSpec((channels, step), lambda i, p: (0, i)),
                pl.BlockSpec((channels, step), lambda i, p: (0, i)),
                pl.BlockSpec((step, 128), lambda i, p: (i, 0)),
            ],
            scratch_shapes=[pltpu.VMEM((step, full), jnp.float32)],
        ),
        out_shape=[
            jax.ShapeDtypeStruct((rows, full), jnp.bfloat16),
            jax.ShapeDtypeStruct((channels, rows), jnp.bfloat16),
            jax.ShapeDtypeStruct((channels, rows), jnp.float32),
            jax.ShapeDtypeStruct((channels, rows), jnp.float32),
            jax.ShapeDtypeStruct((rows, 128), jnp.float32),
        ],
        compiler_params=pltpu.CompilerParams(vmem_limit_bytes=VMEM),
        cost_estimate=cost(8),
    )(place, *parts, affine, weight, bias[:, None])


def gate_kernel(
    place_ref,
    normed_ref,
    grad_ref,
    fronts_ref,
    bias_ref,
    upper_ref,
    slope_ref,
    lifted_grad_ref,
    keep_ref,
    send_ref,
    bias_grad_ref,
    up_ref,
    down_ref,
    mix_ref,
):
    place = place_ref[0]
    size = keep_ref.shape[1]
    unpack_fronts(fronts_ref, up_ref, down_ref, mix_ref)
    before = dot(normed_ref[...], up_ref[...], 1, 0) + bias_ref[...]
    hidden_grad = dot(grad_ref[...], down_ref[...], 1, 0)
    upper, slope = erf_parts(before)
    upper_ref[...] = upper.astype(jnp.bfloat16)
    slope_ref[...] = (hidden_grad * slope).astype(jnp.bfloat16)
    lifted_grad = (hidden_grad * upper).astype(jnp.bfloat16)
    lifted_grad_ref[...] = lifted_grad

    def piece(offset):
        start = pl.multiple_of((place ^ offset) * size, size)
        return dot(mix_ref[pl.ds(start, size), :], lifted_grad, 1, 1)

    keep_ref[0], keep_ref[1] = piece(0), piece(2)
    send_ref[0], send_ref[1] = piece(1), piece(3)
    part = jnp.sum(lifted_grad.astype(jnp.float32), axis=0, keepdims=True)

    @pl.when(pl.program_id(0) == 0)
    def _():
        bias_grad_ref[...] = jnp.zeros_like(bias_grad_ref)

    bias_grad_ref[...] += part


def unpack_fronts(fronts_ref, up_ref, down_ref, mix_ref):
    devices = fronts_ref.shape[0]
    part, mix_part = up_ref.shape[0] // devices, mix_ref.shape[0] // devices

    @pl.when(pl.program_id(0) == 0)
    def _():
        for source in range(devices):
            up_ref[source * part : (source + 1) * part, :] = fronts_ref[source, :part, :]
            down_ref[source * part : (source + 1) * part, :] = fronts_ref[source, part : 2 * part, :]
            mix_ref[source * mix_part : (source + 1) * mix_part, :] = fronts_ref[
                source, 2 * part :, :
            ]


def front_scratch(full, channels, units):
    return [
        pltpu.VMEM((full, units), jnp.bfloat16),
        pltpu.VMEM((full, units), jnp.bfloat16),
        pltpu.VMEM((channels, units), jnp.bfloat16),
    ]


def run_gate(normed, grad, fronts, channels, bias):
    rows, full = normed.shape
    units = fronts.shape[2]
    step = 256

    place = lax.axis_index("chan").astype(jnp.int32).reshape(1)

    def fixed(*shape):
        return pl.BlockSpec(shape, lambda i, p: (0, 0))

    def rowwise(columns):
        return pl.BlockSpec((step, columns), lambda i, p: (i, 0))

    size = channels // 4
    pieces = pl.BlockSpec((2, size, step), lambda i, p: (0, 0, i))
    return pl.pallas_call(
        gate_kernel,
        grid_spec=pltpu.PrefetchScalarGridSpec(
            num_scalar_prefetch=1,
            grid=(rows // step,),
            in_specs=[
                rowwise(full),
                rowwise(full),
                pl.BlockSpec(fronts.shape, lambda i, p: (0, 0, 0), pipeline_mode=pl.Buffered(1)),
                fixed(1, units),
            ],
            out_specs=[rowwise(units)] * 3 + [pieces] * 2 + [fixed(1, units)],
            scratch_shapes=front_scratch(full, channels, units),
        ),
        out_shape=[jax.ShapeDtypeStruct((rows, units), jnp.bfloat16)] * 3
        + [jax.ShapeDtypeStruct((2, size, rows), jnp.float32)] * 2
        + [jax.ShapeDtypeStruct((1, units), jnp.float32)],
        compiler_params=pltpu.CompilerParams(vmem_limit_bytes=VMEM),
        cost_estimate=cost(15),
    )(place, normed, grad, fronts, bias[None])


def mid_kernel(
    place_ref,
    own_ref,
    near_ref,
    far_ref,
    last_ref,
    upper_ref,
    slope_ref,
    normed_ref,
    fronts_ref,
    bias_ref,
    affine_ref,
    mixed_ref,
    hidden_ref,
    up_grad_ref,
    out_keep_ref,
    out_send_ref,
    feature_keep_ref,
    feature_send_ref,
    sums_ref,
    bias_grad_ref,
    up_ref,
    down_ref,
    mix_ref,
    whole,
):
    place = place_ref[0]
    width = out_keep_ref.shape[2]
    unpack_fronts(fronts_ref, up_ref, down_ref, mix_ref)
    size = own_ref.shape[0]
    for offset, piece in enumerate((own_ref, near_ref, far_ref, last_ref)):
        start = pl.multiple_of((place ^ offset) * size, size)
        mixed_ref[pl.ds(start, size), :] = piece[...]
    lifted = dot(mixed_ref[...], mix_ref[...], 0, 0) + bias_ref[...]
    hidden = (upper_ref[...].astype(jnp.float32) * lifted).astype(jnp.bfloat16)
    up_grad = (slope_ref[...].astype(jnp.float32) * lifted).astype(jnp.bfloat16)
    hidden_ref[...] = hidden
    up_grad_ref[...] = up_grad

    @pl.when(pl.program_id(0) == 0)
    def _():
        bias_grad_ref[...] = jnp.zeros_like(bias_grad_ref)

    bias_grad_ref[...] += jnp.sum(up_grad.astype(jnp.float32), axis=0, keepdims=True)

    def part(offset):
        start = pl.multiple_of((place ^ offset) * width, width)
        return whole[:, pl.ds(start, width)].astype(jnp.bfloat16)

    whole[...] = dot(hidden, down_ref[...], 1, 1)
    out_keep_ref[0], out_keep_ref[1] = part(0), part(2)
    out_send_ref[0], out_send_ref[1] = part(1), part(3)
    feature = dot(up_grad, up_ref[...], 1, 1)
    whole[...] = feature
    feature_keep_ref[0], feature_keep_ref[1] = part(0), part(2)
    feature_send_ref[0], feature_send_ref[1] = part(1), part(3)
    one = jnp.sum(feature * affine_ref[0:1, :], axis=1, keepdims=True)
    shifted = normed_ref[...].astype(jnp.float32) - affine_ref[1:2, :]
    two = jnp.sum(feature * shifted, axis=1, keepdims=True)
    lane = lax.broadcasted_iota(jnp.int32, (feature.shape[0], 128), 1)
    sums_ref[...] = jnp.where(lane == 0, one, jnp.where(lane == 1, two, 0.0)).T[0:8, :]


def run_mid(parts, upper, slope, normed, fronts, bias, affine):
    rows, full = normed.shape
    units = fronts.shape[2]
    channels = 4 * parts[0].shape[0]
    width = full // 4
    step = 512
    place = lax.axis_index("chan").astype(jnp.int32).reshape(1)

    def fixed(*shape):
        return pl.BlockSpec(shape, lambda i, p: (0, 0))

    def rowwise(columns):
        return pl.BlockSpec((step, columns), lambda i, p: (i, 0))

    def columns(count):
        return pl.BlockSpec((count, step), lambda i, p: (0, i))

    pieces = pl.BlockSpec((2, step, width), lambda i, p: (0, i, 0))
    piece_shape = jax.ShapeDtypeStruct((2, rows, width), jnp.bfloat16)
    return pl.pallas_call(
        mid_kernel,
        grid_spec=pltpu.PrefetchScalarGridSpec(
            num_scalar_prefetch=1,
            grid=(rows // step,),
            in_specs=[
                columns(channels // 4),
                columns(channels // 4),
                columns(channels // 4),
                columns(channels // 4),
                rowwise(units),
                rowwise(units),
                rowwise(full),
                pl.BlockSpec(fronts.shape, lambda i, p: (0, 0, 0), pipeline_mode=pl.Buffered(1)),
                fixed(1, units),
                fixed(2, full),
            ],
            out_specs=[columns(channels)]
            + [rowwise(units)] * 2
            + [pieces] * 4
            + [columns(8), fixed(1, units)],
            scratch_shapes=front_scratch(full, channels, units)
            + [pltpu.VMEM((step, full), jnp.float32)],
        ),
        out_shape=[jax.ShapeDtypeStruct((channels, rows), jnp.bfloat16)]
        + [jax.ShapeDtypeStruct((rows, units), jnp.bfloat16)] * 2
        + [piece_shape] * 4
        + [
            jax.ShapeDtypeStruct((8, rows), jnp.float32),
            jax.ShapeDtypeStruct((1, units), jnp.float32),
        ],
        compiler_params=pltpu.CompilerParams(vmem_limit_bytes=VMEM),
        cost_estimate=cost(14),
    )(place, *parts, upper, slope, normed, fronts, bias[None], affine)


def payload_kernel(
    grad_ref, slope_ref, before_ref, gain_ref, bias_ref, sums_ref, payload_ref, bias_grad_ref
):
    count = grad_ref.shape[0]
    grad = (grad_ref[...].astype(jnp.float32) * slope_ref[...]).astype(jnp.bfloat16)
    payload_ref[:count, :] = grad
    grad = grad.astype(jnp.float32)
    centred = before_ref[...] - bias_ref[...] - gain_ref[:, 1:2]
    one = jnp.sum(grad * gain_ref[:, 0:1], axis=0, keepdims=True) + sums_ref[0:1, :]
    two = jnp.sum(grad * centred, axis=0, keepdims=True) + sums_ref[1:2, :]
    row = lax.broadcasted_iota(jnp.int32, (16, grad.shape[1]), 0)
    one_high = one.astype(jnp.bfloat16).astype(jnp.float32)
    two_high = two.astype(jnp.bfloat16).astype(jnp.float32)
    tail = jnp.where(row == 0, one_high, jnp.where(row == 1, one - one_high, 0.0))
    tail = jnp.where(row == 2, two_high, jnp.where(row == 3, two - two_high, tail))
    payload_ref[count:, :] = tail.astype(jnp.bfloat16)
    part = jnp.sum(grad, axis=1, keepdims=True)

    @pl.when(pl.program_id(0) == 0)
    def _():
        bias_grad_ref[...] = jnp.zeros_like(bias_grad_ref)

    bias_grad_ref[...] += part


def run_payload(grad, slope, before, gain, bias, sums):
    count, rows = grad.shape
    step = 512

    def columns(lines):
        return pl.BlockSpec((lines, step), lambda i: (0, i))

    def fixed(*shape):
        return pl.BlockSpec(shape, lambda i: (0, 0))

    return pl.pallas_call(
        payload_kernel,
        grid=(rows // step,),
        in_specs=[columns(count)] * 3 + [fixed(count, 2), fixed(count, 1), columns(8)],
        out_specs=[columns(count + 16), fixed(count, 1)],
        out_shape=[
            jax.ShapeDtypeStruct((count + 16, rows), jnp.bfloat16),
            jax.ShapeDtypeStruct((count, 1), jnp.float32),
        ],
        cost_estimate=cost(3),
    )(grad, slope, before, gain, bias[:, None], sums)


def final_kernel(
    _,
    own_ref,
    near_ref,
    far_ref,
    last_ref,
    rows_ref,
    kept_ref,
    sent_ref,
    passed_ref,
    tokens_ref,
    stats_ref,
    grad_ref,
    gain_ref,
    input_grad_ref,
    vectors_ref,
    gain_grad_ref,
    shift_grad_ref,
    down_grad_ref,
    total,
):
    size = own_ref.shape[0] - 16
    row = lax.broadcasted_iota(jnp.int32, (16, 256), 0)
    lane = lax.broadcasted_iota(jnp.int32, (16, 256), 1)
    pick = jnp.where((row < 2) == (lane < 128), 1.0, 0.0)
    pick = jnp.where(row < 4, pick, 0.0).astype(jnp.bfloat16)
    normed_grad = (
        kept_ref[0].astype(jnp.float32)
        + sent_ref[0].astype(jnp.float32)
        + passed_ref[...].astype(jnp.float32)
    )
    totals = jnp.zeros((normed_grad.shape[0], 256), jnp.float32)
    for offset, piece in enumerate((own_ref, near_ref, far_ref, last_ref)):
        weights = rows_ref[:, offset * size : (offset + 1) * size]
        normed_grad += dot(piece[:size, :], weights, 0, 1)
        totals += dot(piece[size:, :], pick, 0, 0)
    scaled = normed_grad * gain_ref[...]
    centred = (tokens_ref[...].astype(jnp.float32) - stats_ref[:, 0:1]) * stats_ref[:, 64:65]
    grad = grad_ref[...].astype(jnp.float32)
    mean_one = totals[:, 0:1] * (1.0 / D)
    mean_two = totals[:, 128:129] * (1.0 / D)
    input_grad_ref[...] = stats_ref[:, 64:65] * (scaled - mean_one - centred * mean_two) + grad

    @pl.when(pl.program_id(0) == 0)
    def _():
        gain_grad_ref[...] = jnp.zeros_like(gain_grad_ref)
        shift_grad_ref[...] = jnp.zeros_like(shift_grad_ref)
        down_grad_ref[...] = jnp.zeros_like(down_grad_ref)

    gain_grad_ref[...] += jnp.sum(normed_grad * centred, axis=0, keepdims=True)
    shift_grad_ref[...] += jnp.sum(normed_grad, axis=0, keepdims=True)
    down_grad_ref[...] += jnp.sum(grad, axis=0, keepdims=True)

    @pl.when(pl.program_id(0) == pl.num_programs(0) - 1)
    def _():
        devices = vectors_ref.shape[0]
        part = gain_grad_ref.shape[1] // devices
        row = lax.broadcasted_iota(jnp.int32, (16, 128), 0)
        total[...] = jnp.zeros_like(total)
        for turn in range(devices):
            for index, ref in enumerate((gain_grad_ref, shift_grad_ref, down_grad_ref)):
                total[:, index * part : (index + 1) * part] = ref[
                    :, turn * part : (turn + 1) * part
                ]
            high = total[...].astype(jnp.bfloat16).astype(jnp.float32)
            pair = jnp.where(row == 0, high, jnp.where(row == 1, total[...] - high, 0.0))
            vectors_ref[turn] = pair.astype(jnp.bfloat16)


def run_final(parts, input_rows, kept, sent, passed, tokens, stats, grad, gain):
    rows, width = tokens.shape
    lines = parts[0].shape[0]
    devices = lax.axis_size("seq")
    step = 512
    place = lax.axis_index("chan").astype(jnp.int32).reshape(1)

    def fixed(*shape):
        return pl.BlockSpec(shape, lambda i, p: (0, 0))

    def rowwise(columns):
        return pl.BlockSpec((step, columns), lambda i, p: (i, 0))

    def columns(count):
        return pl.BlockSpec((count, step), lambda i, p: (0, i))

    piece = pl.BlockSpec((1, step, width), lambda i, p: (0, i, 0))
    return pl.pallas_call(
        final_kernel,
        grid_spec=pltpu.PrefetchScalarGridSpec(
            num_scalar_prefetch=1,
            grid=(rows // step,),
            in_specs=[columns(lines)] * 4
            + [
                fixed(*input_rows.shape),
                piece,
                piece,
                rowwise(width),
                rowwise(width),
                rowwise(128),
                pl.BlockSpec((step, width), lambda i, p: (i, p[0])),
                fixed(1, width),
            ],
            out_specs=[rowwise(width), pl.BlockSpec((devices, 16, 128), lambda i, p: (0, 0, 0))],
            scratch_shapes=[pltpu.VMEM((1, width), jnp.float32)] * 3
            + [pltpu.VMEM((1, 128), jnp.float32)],
        ),
        out_shape=[
            jax.ShapeDtypeStruct((rows, width), jnp.float32),
            jax.ShapeDtypeStruct((devices, 16, 128), jnp.bfloat16),
        ],
        cost_estimate=cost(6),
    )(place, *parts, input_rows, kept, sent, passed, tokens, stats, grad, gain[None])


def grads_kernel(
    side_ref,
    outer_ref,
    normed_ref,
    mixed_ref,
    hidden_ref,
    up_ref,
    lifted_ref,
    down_send_ref,
    down_keep_ref,
    rest_send_ref,
    rest_keep_ref,
    whole,
    mix_whole,
):
    kept = side_ref[0]
    part = outer_ref.shape[1] // 2
    mix_part = mixed_ref.shape[0] // 2

    def half(scratch, size, side):
        return scratch[pl.ds(pl.multiple_of(side * size, size), size), :].astype(jnp.bfloat16)

    whole[...] = dot(outer_ref[...], hidden_ref[...], 0, 0)
    down_send_ref[0] = half(whole, part, 1 - kept)
    down_keep_ref[0] = half(whole, part, kept)
    whole[...] = dot(normed_ref[...], up_ref[...], 0, 0)
    rest_send_ref[0, :part, :] = half(whole, part, 1 - kept)
    rest_keep_ref[0, :part, :] = half(whole, part, kept)
    mix_whole[...] = dot(mixed_ref[...], lifted_ref[...], 1, 0)
    rest_send_ref[0, part:, :] = half(mix_whole, mix_part, 1 - kept)
    rest_keep_ref[0, part:, :] = half(mix_whole, mix_part, kept)


def run_grads(outer, normed, mixed, hidden, up, lifted):
    rows, full = outer.shape
    channels = mixed.shape[0]
    units = hidden.shape[1]
    devices = lax.axis_size("seq")
    half = devices // 2
    part, mix_part = full // devices, channels // devices
    side = (lax.axis_index("seq") & 1).astype(jnp.int32).reshape(1)

    def fixed(*shape):
        return pl.BlockSpec(shape, lambda i, p: (0, 0), pipeline_mode=pl.Buffered(1))

    whole = part + mix_part
    return pl.pallas_call(
        grads_kernel,
        grid_spec=pltpu.PrefetchScalarGridSpec(
            num_scalar_prefetch=1,
            grid=(half,),
            in_specs=[
                pl.BlockSpec((rows, 2 * part), lambda i, p: (0, i)),
                pl.BlockSpec((rows, 2 * part), lambda i, p: (0, i)),
                pl.BlockSpec((2 * mix_part, rows), lambda i, p: (i, 0)),
                fixed(rows, units),
                fixed(rows, units),
                fixed(rows, units),
            ],
            out_specs=[pl.BlockSpec((1, part, units), lambda i, p: (i, 0, 0))] * 2
            + [pl.BlockSpec((1, whole, units), lambda i, p: (i, 0, 0))] * 2,
            scratch_shapes=[
                pltpu.VMEM((2 * part, units), jnp.float32),
                pltpu.VMEM((2 * mix_part, units), jnp.float32),
            ],
        ),
        out_shape=[jax.ShapeDtypeStruct((half, part, units), jnp.bfloat16)] * 2
        + [jax.ShapeDtypeStruct((half, whole, units), jnp.bfloat16)] * 2,
        compiler_params=pltpu.CompilerParams(vmem_limit_bytes=VMEM),
        cost_estimate=cost(14),
    )(side, outer, normed, mixed, hidden, up, lifted)


def swap(value, distance):
    return lax.ppermute(value, "chan", [(i, i ^ distance) for i in range(4)])


def gather_parts(piece):
    far = swap(piece, 2)
    return piece, swap(piece, 1), far, swap(far, 1)


def after(value, *others):
    return lax.optimization_barrier((value,) + others)[0]


def to_channels(value, sequences):
    devices = lax.axis_size("seq")
    channels, tokens = value.shape
    share = channels // devices
    got = lax.all_to_all(value.reshape(devices, share, tokens), "seq", 0, 0, tiled=True)
    got = got.reshape(sequences, devices // sequences, share, tokens)
    return got.transpose(1, 0, 2, 3).reshape(devices // sequences, sequences * share, tokens)


def to_tokens(value, sequences):
    devices = lax.axis_size("seq")
    sources, count, tokens = value.shape
    share = count // sequences
    sent = value.reshape(sources, sequences, share, tokens).transpose(1, 0, 2, 3)
    got = lax.all_to_all(sent.reshape(devices, share, tokens), "seq", 0, 0, tiled=True)
    return got.reshape(devices * share, tokens)


def tile_rows(flat):
    width = flat.shape[-1]
    padded = -(-width // 128) * 128
    flat = jnp.pad(flat, [(0, 0)] * (flat.ndim - 1) + [(0, padded - width)])
    return flat.reshape(flat.shape[:-1] + (padded // 128, 128))


def planes(value, count):
    parts = []
    for _ in range(count):
        part = lax.reduce_precision(value, 8, 7)
        parts.append(part.astype(jnp.bfloat16))
        value = value - part
    return parts


def plain_grads(outer, normed, mixed, hidden, up, lifted):
    devices = lax.axis_size("seq")
    side = lax.axis_index("seq") & 1

    def parts(value):
        value = value.astype(jnp.bfloat16)
        return value.reshape(devices // 2, 2, value.shape[0] // devices, value.shape[1])

    def pick(value, index):
        return lax.dynamic_index_in_dim(value, index, 1, False)

    down = parts(dot(outer, hidden, 0, 0))
    rest = (parts(dot(normed, up, 0, 0)), parts(dot(mixed, lifted, 1, 0)))
    rest = jnp.concatenate(rest, axis=2)
    return (pick(down, 1 - side), pick(down, side), pick(rest, 1 - side), pick(rest, side))


def halve(sent, kept):
    devices = lax.axis_size("seq")
    got = lax.ppermute(sent, "seq", [(i, i ^ 1) for i in range(devices)])
    return (kept.astype(jnp.float32) + got.astype(jnp.float32)).astype(jnp.bfloat16)


def settle_apart(halves):
    devices = lax.axis_size("seq")
    if devices != 8:
        return settle(halves)
    line = lax.axis_index("seq") >> 1
    total = lax.dynamic_index_in_dim(halves, line, 0, False).astype(jnp.float32)
    for distance in (2, 3, 1):
        sent = lax.dynamic_index_in_dim(halves, line ^ distance, 0, False)
        pairs = [(i, i ^ (2 * distance)) for i in range(devices)]
        total += lax.ppermute(sent, "seq", pairs).astype(jnp.float32)
    return total


def settle(halves):
    devices = lax.axis_size("seq")
    groups = [[i for i in range(devices) if i & 1 == side] for side in (0, 1)]
    got = lax.all_to_all(halves, "seq", 0, 0, axis_index_groups=groups, tiled=True)
    return jnp.sum(got.astype(jnp.float32), axis=0)


def per_device(
    tokens,
    norm_gain,
    norm_shift,
    up_weight,
    up_bias,
    input_weight,
    input_bias,
    mix_weight,
    mix_bias,
    down_weight,
    down_bias,
    decay_rate,
    decay_freq,
    step_log,
    read_real,
    read_imag,
    skip_gain,
    out_grad,
):
    row_count, width = tokens.shape
    devices = lax.axis_size("seq")
    place = lax.axis_index("chan")
    sequences = devices * row_count // LENGTH
    feature_rows, channels = input_weight.shape
    units = up_weight.shape[1]
    share = channels // devices
    modes_here = decay_rate.shape[0]
    modes = modes_here * devices
    near = swap(tokens, 1)
    early_rows = row_count // 4
    far, far_late = swap(tokens[:early_rows], 2), swap(tokens[early_rows:], 2)
    token_parts = (tokens, near, far, far_late, swap(far, 1), swap(far_late, 1))

    pair = jnp.stack([norm_gain, norm_shift])
    pairs = jnp.stack([pair, swap(pair, 1), swap(pair, 2), swap(pair, 3)])
    pairs = jnp.stack([pairs[place ^ i] for i in range(4)])
    fronts = jnp.concatenate([up_weight, down_weight.T, mix_weight])
    pairs = after(pairs, far, fronts)
    fronts = lax.all_gather(fronts, "seq", axis=0)
    small = (pairs.reshape(-1), up_bias, input_bias, mix_bias, down_bias, decay_rate, decay_freq)
    sizes = [v.shape[0] for v in small]
    small = tile_rows(jnp.concatenate(small))
    reads = jnp.concatenate([read_real, read_imag], axis=1).reshape(devices, share, 2 * modes_here)
    reads = jnp.pad(reads, ((0, 0), (0, 0), (0, 128 - 2 * modes_here)))
    copies = jnp.broadcast_to(small, (devices,) + small.shape)
    exact = jnp.concatenate([reads, copies], axis=1)
    exact_rows = exact.shape[1]
    weights = jnp.broadcast_to(input_weight, (devices,) + input_weight.shape)
    got = jnp.concatenate(planes(exact, 3) + [weights], axis=1)
    got = lax.all_to_all(got, "seq", 0, 0, tiled=True)
    input_full = got[:, 3 * exact_rows :].reshape(4 * width, channels)

    def exact_part(start, stop):
        rows = [got[:, i * exact_rows + start : i * exact_rows + stop] for i in range(3)]
        rows = [r.astype(jnp.float32) for r in rows]
        return rows[0] + (rows[1] + rows[2])

    small = exact_part(share, exact_rows).reshape(devices, -1)
    parts, spot = [], 0
    for size in sizes:
        parts.append(small[:, spot : spot + size])
        spot += size
    affine = parts[0].reshape(devices, 4, 2, -1).transpose(2, 1, 0, 3).reshape(2, 4 * width)
    input_shift = parts[2].reshape(-1)

    normed, values_low, in_slope, pre_in, stats = run_norm(
        token_parts, affine, input_full, input_shift
    )
    values = to_channels(values_low, sequences)

    got = after(got, normed)
    parts = lax.optimization_barrier(tuple(parts) + (normed,))[:-1]
    reads = exact_part(0, share)[:, :, : 2 * modes_here].transpose(1, 0, 2)
    read_re = reads[:, :, :modes_here].reshape(share, modes)
    read_im = reads[:, :, modes_here:].reshape(share, modes)
    up_shift, _, mix_shift, down_shift, rate, freq = (p.reshape(-1) for p in parts[1:])

    spacing = jnp.exp(step_log)
    damping = spacing[:, None] * rate[None, :]
    rotation = spacing[:, None] * freq[None, :]
    inflow = -jnp.expm1(-damping)
    extents = 2.0 ** jnp.arange(8)[None, :, None]
    length = jnp.exp(-damping[:, None] * extents)
    angle = rotation[:, None] * extents
    power_re, power_im = length * jnp.cos(angle), length * jnp.sin(angle)

    def repeat(value):
        return jnp.tile(value, (sequences,) + (1,) * (value.ndim - 1))

    def rows(value_re, value_im):
        return repeat(jnp.concatenate([value_re, value_im], axis=1)[:, None])

    power, out_table, in_table, toeplitz = make_tables(
        repeat(power_re), repeat(power_im), repeat(read_re), repeat(read_im), repeat(inflow)
    )
    jump = rows(power_re[:, 7], power_im[:, 7])[:, 0]
    flow = rows(inflow, inflow)
    lead = rows(*cmul(read_re, read_im, power_re[:, 0], power_im[:, 0]))
    skip = repeat(skip_gain)

    pieces = gather_parts(after(input_full, normed))
    pieces = [lax.dynamic_slice_in_dim(p, place * width, width, 0) for p in pieces]
    input_rows = jnp.concatenate(pieces, axis=1)
    in_gain = jnp.dot(
        input_full.T.astype(jnp.float32), affine.T, precision=lax.Precision.HIGHEST
    )
    mixed, starts, values_split = run_forward(
        after(values, input_rows, in_gain), skip, jump, flow, lead, out_table, in_table, toeplitz
    )
    mixed_tokens = to_tokens(mixed, sequences)

    upper, up_slope, lifted_grad, channel_keep, channel_send, mix_bias_part = run_gate(
        after(normed, mixed), out_grad, fronts, 4 * channels, up_shift
    )
    channel_sent = swap(after(channel_send, mixed_tokens), 1)
    mixed_parts = gather_parts(mixed_tokens)
    channel_passed = (channel_keep[1] + channel_sent[1]).astype(jnp.bfloat16)
    channel_sum = channel_keep[0] + channel_sent[0]
    channel_far = swap(channel_passed, 2)
    mixed_grad = (channel_sum + channel_far.astype(jnp.float32)).astype(jnp.bfloat16)
    grads = to_channels(mixed_grad, sequences)

    (
        mixed_full,
        hidden,
        up_pre_grad,
        out_keep,
        out_send,
        feature_keep,
        feature_send,
        up_sums,
        up_bias_part,
    ) = run_mid(
        (after(mixed_parts[0], channel_passed),) + mixed_parts[1:],
        upper,
        up_slope,
        normed,
        fronts,
        mix_shift,
        affine,
    )
    out_sent, feature_sent = swap(out_send, 1), swap(feature_send, 1)

    def passed(keep, sent):
        return (keep[1].astype(jnp.float32) + sent[1].astype(jnp.float32)).astype(jnp.bfloat16)

    feature_passed = passed(feature_keep, feature_sent)
    out_passed = passed(out_keep, out_sent)
    make_grads = run_grads if feature_rows % 128 == 0 else plain_grads
    down_send, down_keep, rest_send, rest_keep = make_grads(
        out_grad, normed, mixed_full, after(hidden, mixed_grad), up_pre_grad, lifted_grad
    )
    feature_far = swap(feature_passed, 2)
    down_sent, rest_sent = after(down_send, grads), after(rest_send, grads)
    grads = after(grads, down_send, feature_passed, out_passed)
    values_grad, later, grads_split = run_backward(
        grads, skip, jump, flow, lead, out_table, in_table, toeplitz
    )
    values_back = to_tokens(after(values_grad, feature_far), sequences)
    out_far = swap(after(out_passed, values_grad), 2)
    sums, skip_sums = run_sums(grads_split, values_split, starts, later, power)
    down_half = halve(down_sent, after(down_keep, values_grad))
    rest_half = halve(rest_sent, after(rest_keep, values_grad, out_far))
    down_total = settle_apart(down_half)
    rest_total = settle(after(rest_half, values_back))
    down_weight_grad = down_total.T
    up_weight_grad, mix_weight_grad = rest_total[:feature_rows], rest_total[feature_rows:]
    payload, input_bias_part = run_payload(
        after(values_back, sums, rest_half, down_total), in_slope, pre_in, in_gain, input_shift, up_sums
    )
    payload_parts = gather_parts(payload)
    sums, skip_sums, up_bias_part, mix_bias_part, down_shift, gain_all, _ = lax.optimization_barrier(
        (sums, skip_sums, up_bias_part, mix_bias_part, down_shift, affine[0], payload)
    )
    gain_own = lax.dynamic_slice_in_dim(gain_all, place * width, width)
    input_part = dot(normed, after(payload, payload_parts[1])[:channels], 0, 1)
    input_grad, late_vectors = run_final(
        payload_parts,
        input_rows,
        feature_keep,
        feature_sent,
        feature_far,
        tokens,
        stats,
        out_grad,
        gain_own,
    )

    inputs = tokens.astype(jnp.float32)
    output = (
        out_keep[0].astype(jnp.float32)
        + out_sent[0].astype(jnp.float32)
        + out_far.astype(jnp.float32)
        + down_shift
        + inputs
    )

    sums = jnp.concatenate([sums[:, :4], sums[:, 4:8] * flow[:, :, :modes], sums[:, 8:]], axis=1)
    sums = jnp.sum(sums.reshape((sequences, share) + sums.shape[1:]), axis=0)
    skip_grad = jnp.sum(skip_sums.reshape(sequences, share, BLOCK), axis=(0, 2))
    out_zero = cmul(power_re[:, 0], power_im[:, 0], sums[:, 0], sums[:, 1])
    out_one = cmul(
        power_re[:, 0], power_im[:, 0], sums[:, 0] + sums[:, 2], sums[:, 1] + sums[:, 3]
    )
    chained = cmul(power_re[:, 7], power_im[:, 7], sums[:, 8], sums[:, 9])
    local_zero, local_one = (sums[:, 10], sums[:, 11]), (sums[:, 12], sums[:, 13])
    read_re_grad = out_zero[0] + inflow * local_zero[0]
    read_im_grad = -out_zero[1] - inflow * local_zero[1]
    turn = cmul(
        read_re, read_im, out_one[0] + inflow * local_one[0], out_one[1] + inflow * local_one[1]
    )
    turn_re = turn[0] + sums[:, 6] + BLOCK * chained[0]
    turn_im = turn[1] + sums[:, 7] + BLOCK * chained[1]
    inflow_grad = sums[:, 4] / inflow + read_re * local_zero[0] - read_im * local_zero[1]
    damping_grad = jnp.exp(-damping) * inflow_grad - turn_re
    rotation_grad = -turn_im
    step_log_grad = spacing * jnp.sum(
        rate[None, :] * damping_grad + freq[None, :] * rotation_grad, axis=1
    )
    rates = jnp.stack(
        [
            jnp.sum(spacing[:, None] * damping_grad, axis=0),
            jnp.sum(spacing[:, None] * rotation_grad, axis=0),
        ]
    )
    rates = rates + swap(rates, 1)
    rates = rates + swap(rates, 2)

    read_grads = jnp.stack([read_re_grad, read_im_grad], axis=1)
    read_grads = read_grads.reshape(share, 2, devices, modes_here).transpose(2, 0, 1, 3)
    read_grads = read_grads.reshape(devices, share, 2 * modes_here)
    read_grads = jnp.pad(read_grads, ((0, 0), (0, 0), (0, 128 - 2 * modes_here)))

    def line_up(vectors):
        vectors = [v.reshape(devices, -1) for v in vectors]
        sizes = [v.shape[1] for v in vectors]
        return tile_rows(jnp.concatenate(vectors, axis=1)), sizes

    def take_apart(flat, sizes):
        parts, spot = [], 0
        for size in sizes:
            parts.append(flat[spot : spot + size])
            spot += size
        return parts

    vectors, sizes = line_up(
        (
            up_bias_part,
            input_bias_part,
            mix_bias_part,
            rates[0],
            rates[1],
        )
    )
    input_part = input_part.reshape(devices, feature_rows, channels)
    parcel = jnp.concatenate([read_grads, vectors], axis=1)
    exact_rows = -(-parcel.shape[1] // 16) * 16
    parcel = jnp.pad(parcel, ((0, 0), (0, exact_rows - parcel.shape[1]), (0, 0)))
    parcel = jnp.concatenate(planes(parcel, 2) + [input_part.astype(jnp.bfloat16)], axis=1)
    late = jnp.concatenate([parcel, after(late_vectors, rest_total)], axis=1)
    late = lax.all_to_all(late, "seq", 0, 0, tiled=True).astype(jnp.float32)
    input_weight_grad = jnp.sum(late[:, 2 * exact_rows : 2 * exact_rows + feature_rows], axis=0)
    tail = jnp.sum(late[:, 2 * exact_rows + feature_rows :], axis=(0, 1))
    late = late[:, :exact_rows] + late[:, exact_rows : 2 * exact_rows]
    read_late = late[:, :share, : 2 * modes_here].reshape(channels, 2 * modes_here)
    late = take_apart(jnp.sum(late[:, share:], axis=0).reshape(-1), sizes)
    up_bias_grad, input_bias_grad, mix_bias_grad, rate_out, freq_out = late
    gain_grad, shift_grad, down_bias_grad = take_apart(tail, [width // devices] * 3)
    return (
        output,
        input_grad,
        gain_grad,
        shift_grad,
        up_weight_grad,
        up_bias_grad,
        input_weight_grad,
        input_bias_grad,
        mix_weight_grad,
        mix_bias_grad,
        down_weight_grad,
        down_bias_grad,
        rate_out,
        freq_out,
        step_log_grad,
        read_late[:, :modes_here],
        read_late[:, modes_here:],
        skip_grad,
    )


def solution(mesh):
    return jax.shard_map(
        per_device,
        mesh=mesh,
        in_specs=(
            P("seq", "chan"),
            P(("chan", "seq")),
            P(("chan", "seq")),
            P("seq", "chan"),
            P(("chan", "seq")),
            P("seq", "chan"),
            P(("chan", "seq")),
            P("seq", "chan"),
            P(("chan", "seq")),
            P("chan", "seq"),
            P(("chan", "seq")),
            P("seq"),
            P("seq"),
            P(("chan", "seq")),
            P("chan", "seq"),
            P("chan", "seq"),
            P(("chan", "seq")),
            P("seq", None),
        ),
        out_specs=(
            P("seq", "chan"),
            P("seq", "chan"),
            P(("chan", "seq")),
            P(("chan", "seq")),
            P("seq", "chan"),
            P(("chan", "seq")),
            P("seq", "chan"),
            P(("chan", "seq")),
            P("seq", "chan"),
            P(("chan", "seq")),
            P("chan", "seq"),
            P(("chan", "seq")),
            P("seq"),
            P("seq"),
            P(("chan", "seq")),
            P("chan", "seq"),
            P("chan", "seq"),
            P(("chan", "seq")),
        ),
        check_vma=False,
    )
```

```python
from functools import partial
import math

import jax
import jax.numpy as jnp
from jax import lax
from jax.experimental import pallas as pl
from jax.experimental.pallas import tpu as pltpu
from jax.sharding import PartitionSpec as P

D = 1024
LENGTH = 16384
EPSILON = 1e-05


BLOCK = 128
MEGA = 1024 * 1024
VMEM = 56 * MEGA


def dot(left, right, left_dim, right_dim):
    return lax.dot_general(
        left, right, (((left_dim,), (right_dim,)), ((), ())), preferred_element_type=jnp.float32
    )


def cmul(a_re, a_im, b_re, b_im):
    return (a_re * b_re - a_im * b_im, a_re * b_im + a_im * b_re)


def grow(first, reversed_rows, mode_powers, store):
    row = lax.broadcasted_iota(jnp.int32, (8, first[0].shape[1]), 0)
    exponent = 7 - row if reversed_rows else row
    part = (
        jnp.broadcast_to(first[0], row.shape),
        jnp.broadcast_to(first[1], row.shape),
    )
    for level in range(3):
        factor_re, factor_im = mode_powers(level)
        taken = (exponent >> level) & 1 == 1
        part = cmul(*part, jnp.where(taken, factor_re, 1.0), jnp.where(taken, factor_im, 0.0))
    spot = BLOCK - 8 if reversed_rows else 0
    store(spot, part[0], part[1])
    whole = part
    size, level = 8, 3
    while size < BLOCK:
        factor = mode_powers(level)
        fresh = cmul(*whole, *factor)
        spot = BLOCK - 2 * size if reversed_rows else size
        store(spot, *fresh)
        pair = (fresh, whole) if reversed_rows else (whole, fresh)
        whole = tuple(jnp.concatenate([p, q], axis=0) for p, q in zip(*pair))
        size, level = 2 * size, level + 1


def tables_kernel(
    power_re_ref,
    power_im_ref,
    read_re_ref,
    read_im_ref,
    inflow_ref,
    power_ref,
    out_table_ref,
    in_table_ref,
    toeplitz_ref,
):
    modes = power_re_ref.shape[2]
    lower, upper = slice(0, modes), slice(modes, 2 * modes)

    def mode_powers(level):
        return (power_re_ref[0, level : level + 1, :], power_im_ref[0, level : level + 1, :])

    inflow = inflow_ref[0]
    one, none = jnp.ones_like(inflow), jnp.zeros_like(inflow)

    def store_power(spot, part_re, part_im):
        rows = slice(spot, spot + part_re.shape[0])
        power_ref[0, rows, lower] = part_re
        power_ref[0, rows, upper] = part_im

    grow((one, none), False, mode_powers, store_power)
    exact = jnp.concatenate([power_ref[0, :, lower], -power_ref[0, :, upper]], axis=1)
    rounded = exact.astype(jnp.bfloat16)
    out_table_ref[0] = rounded
    rest = (exact - rounded.astype(jnp.float32)).astype(jnp.bfloat16)
    backward = []

    def store_in(spot, part_re, part_im):
        backward.append((spot, part_re, part_im))

    grow((one, none), True, mode_powers, store_in)
    backward.sort(key=lambda entry: entry[0])
    in_table_ref[0, :, lower] = jnp.concatenate([e[1] for e in backward], 0).astype(jnp.bfloat16)
    in_table_ref[0, :, upper] = jnp.concatenate([e[2] for e in backward], 0).astype(jnp.bfloat16)
    weight = jnp.concatenate([read_re_ref[0] * inflow, read_im_ref[0] * inflow], axis=1)
    high = weight.astype(jnp.bfloat16).astype(jnp.float32)
    row = lax.broadcasted_iota(jnp.int32, (16, 2 * modes), 0)
    probe = jnp.where(row == 0, high, jnp.where(row == 1, weight - high, 0.0))
    probe = probe.astype(jnp.bfloat16)
    lags = dot(probe, rounded, 1, 1) + dot(probe, rest, 1, 1)
    kernel_row = jnp.sum(lags, axis=0, keepdims=True)
    skewed = pltpu.roll(
        jnp.broadcast_to(kernel_row, (BLOCK, BLOCK)), 0, 1, stride=1, stride_axis=0
    )
    source = lax.broadcasted_iota(jnp.int32, (BLOCK, BLOCK), 0)
    target = lax.broadcasted_iota(jnp.int32, (BLOCK, BLOCK), 1)
    skewed = jnp.where(target >= source, skewed, 0.0)
    coarse = skewed.astype(jnp.bfloat16)
    toeplitz_ref[0, :BLOCK, :] = coarse
    toeplitz_ref[0, BLOCK:, :] = (skewed - coarse.astype(jnp.float32)).astype(jnp.bfloat16)


def make_tables(power_re, power_im, read_re, read_im, inflow):
    count, levels, modes = power_re.shape

    def spec(*shape):
        return pl.BlockSpec((1,) + shape, lambda i: (i, 0, 0))

    return pl.pallas_call(
        tables_kernel,
        grid=(count,),
        in_specs=[spec(levels, modes)] * 2 + [spec(1, modes)] * 3,
        out_specs=[
            spec(BLOCK, 2 * modes),
            spec(BLOCK, 2 * modes),
            spec(BLOCK, 2 * modes),
            spec(2 * BLOCK, BLOCK),
        ],
        out_shape=[
            jax.ShapeDtypeStruct((count, BLOCK, 2 * modes), jnp.float32),
            jax.ShapeDtypeStruct((count, BLOCK, 2 * modes), jnp.bfloat16),
            jax.ShapeDtypeStruct((count, BLOCK, 2 * modes), jnp.bfloat16),
            jax.ShapeDtypeStruct((count, 2 * BLOCK, BLOCK), jnp.bfloat16),
        ],
        compiler_params=pltpu.CompilerParams(vmem_limit_bytes=VMEM),
        cost_estimate=cost(12),
    )(power_re, power_im, read_re[:, None], read_im[:, None], inflow[:, None])


def spread_tokens(ref, scratch):
    sources, count, tokens = ref.shape
    per_source = tokens // BLOCK
    for source in range(sources):
        for part in range(per_source):
            row = (source * per_source + part) * count
            tile = ref[source, :, part * BLOCK : (part + 1) * BLOCK]
            scratch[row : row + count, :] = tile.astype(jnp.float32)


def gather_tokens(scratch, ref):
    sources, count, tokens = ref.shape
    per_source = tokens // BLOCK
    for source in range(sources):
        for part in range(per_source):
            row = (source * per_source + part) * count
            ref[source, :, part * BLOCK : (part + 1) * BLOCK] = scratch[
                row : row + count, :
            ].astype(ref.dtype)


GROUP = 4
LANES = 8


def segment_rows(channel, count, blocks):
    length = blocks // LANES
    return [pl.ds(turn * count + channel, LANES, stride=length * count) for turn in range(length)]


def scan_blocks(ends, jump, leaps, backward):
    modes = ends.shape[1] // 2
    length = ends.shape[0] // LANES
    order = range(length - 1, -1, -1) if backward else range(length)
    jump = tuple(jnp.broadcast_to(j, (LANES, modes)) for j in jump)
    row = lax.broadcasted_iota(jnp.int32, (LANES, modes), 0)
    blank = jnp.zeros((LANES, modes), jnp.float32)

    def step(state, turn):
        part = ends[turn * LANES : (turn + 1) * LANES, :]
        moved = cmul(*jump, *state)
        return (moved[0] + part[:, :modes], moved[1] + part[:, modes:])

    def shifted(value, distance):
        turned = pltpu.roll(value, LANES - distance if backward else distance, 0)
        inside = row < LANES - distance if backward else row >= distance
        return jnp.where(inside, turned, 0.0)

    state = (blank, blank)
    for turn in order:
        state = step(state, turn)
    state = tuple(shifted(v, 1) for v in state)
    for level, leap in enumerate(leaps):
        before = tuple(shifted(v, 2**level) for v in state)
        moved = cmul(*leap, *before)
        state = (state[0] + moved[0], state[1] + moved[1])
    states = [None] * length
    for turn in order:
        states[turn] = jnp.concatenate(state, axis=1)
        state = step(state, turn)
    return jnp.concatenate(states, axis=0)


def jumps_of(ref, sign):
    modes = ref.shape[2] // 2
    pairs = [(ref[0, i : i + 1, :modes], sign * ref[0, i : i + 1, modes:]) for i in range(4)]
    return pairs[0], pairs[1:]


def forward_kernel(
    values_ref,
    skip_ref,
    jump_ref,
    inflow_ref,
    lead_ref,
    out_table_ref,
    in_table_ref,
    toeplitz_ref,
    mixed_ref,
    starts_ref,
    split_ref,
    tokens,
):
    count = values_ref.shape[1]
    blocks = tokens.shape[0] // count
    modes = jump_ref.shape[2] // 2
    turn = pl.program_id(0)
    pl.when(turn == 0)(lambda: spread_tokens(values_ref, tokens))
    for index in range(GROUP):
        channel = turn * GROUP + index
        rows = segment_rows(channel, count, blocks)
        own = jnp.concatenate([tokens[r, :] for r in rows], axis=0)
        own_low = own.astype(jnp.bfloat16)
        split_ref[index] = own_low
        ends = dot(own_low, in_table_ref[index], 1, 0) * inflow_ref[index]
        start = scan_blocks(ends, *jumps_of(jump_ref.at[index : index + 1], 1.0), False)
        starts_ref[index] = start.astype(jnp.bfloat16)
        lead = lead_ref[index]
        weighted = cmul(lead[:, :modes], lead[:, modes:], start[:, :modes], start[:, modes:])
        weighted = jnp.concatenate(weighted, axis=1).astype(jnp.bfloat16)
        mixed = dot(weighted, out_table_ref[index], 1, 1)
        mixed += dot(own_low, toeplitz_ref[index, :BLOCK, :], 1, 0)
        mixed += dot(own_low, toeplitz_ref[index, BLOCK:, :], 1, 0)
        mixed += skip_ref[channel] * own
        for part, r in enumerate(rows):
            tokens[r, :] = mixed[part * LANES : (part + 1) * LANES, :]
    pl.when(turn == pl.num_programs(0) - 1)(lambda: gather_tokens(tokens, mixed_ref))


def run_pass(kernel, values, skip, jump, inflow, lead, out_table, in_table, toeplitz):
    sources, count, tokens = values.shape
    blocks = sources * tokens // BLOCK
    width = jump.shape[2]
    whole = pl.BlockSpec(values.shape, lambda i: (0, 0, 0), pipeline_mode=pl.Buffered(1))

    def spec(*shape):
        return pl.BlockSpec((GROUP,) + shape, lambda i: (i, 0, 0))

    return pl.pallas_call(
        kernel,
        grid=(count // GROUP,),
        in_specs=[
            whole,
            pl.BlockSpec(memory_space=pltpu.SMEM),
            spec(4, width),
            spec(1, width),
            spec(1, width),
            spec(BLOCK, width),
            spec(BLOCK, width),
            spec(2 * BLOCK, BLOCK),
        ],
        out_specs=[whole, spec(blocks, width), spec(blocks, BLOCK)],
        out_shape=[
            jax.ShapeDtypeStruct(values.shape, jnp.bfloat16),
            jax.ShapeDtypeStruct((count, blocks, width), jnp.bfloat16),
            jax.ShapeDtypeStruct((count, blocks, BLOCK), jnp.bfloat16),
        ],
        scratch_shapes=[pltpu.VMEM((blocks * count, BLOCK), jnp.float32)],
        compiler_params=pltpu.CompilerParams(vmem_limit_bytes=VMEM),
        cost_estimate=cost(20),
    )(values, skip, jump, inflow, lead, out_table, in_table, toeplitz)


def run_forward(*operands):
    return run_pass(forward_kernel, *operands)


def backward_kernel(
    grads_ref,
    skip_ref,
    jump_ref,
    inflow_ref,
    lead_ref,
    out_table_ref,
    in_table_ref,
    toeplitz_ref,
    values_grad_ref,
    later_ref,
    split_ref,
    grads,
):
    count = grads_ref.shape[1]
    blocks = grads.shape[0] // count
    modes = jump_ref.shape[2] // 2
    turn = pl.program_id(0)
    pl.when(turn == 0)(lambda: spread_tokens(grads_ref, grads))
    for index in range(GROUP):
        channel = turn * GROUP + index
        rows = segment_rows(channel, count, blocks)
        own = jnp.concatenate([grads[r, :] for r in rows], axis=0)
        own_low = own.astype(jnp.bfloat16)
        split_ref[index] = own_low
        lead = lead_ref[index]
        ends = dot(own_low, out_table_ref[index], 1, 0)
        ends = cmul(lead[:, :modes], -lead[:, modes:], ends[:, :modes], ends[:, modes:])
        ends = jnp.concatenate(ends, axis=1)
        later = scan_blocks(ends, *jumps_of(jump_ref.at[index : index + 1], -1.0), True)
        later_ref[index] = later.astype(jnp.bfloat16)
        later = (later * inflow_ref[index]).astype(jnp.bfloat16)
        back = dot(later, in_table_ref[index], 1, 1)
        back += dot(own_low, toeplitz_ref[index, :BLOCK, :], 1, 1)
        back += dot(own_low, toeplitz_ref[index, BLOCK:, :], 1, 1)
        back += skip_ref[channel] * own
        for part, r in enumerate(rows):
            grads[r, :] = back[part * LANES : (part + 1) * LANES, :]
    pl.when(turn == pl.num_programs(0) - 1)(lambda: gather_tokens(grads, values_grad_ref))


def run_backward(*operands):
    return run_pass(backward_kernel, *operands)


def sums_kernel(grad_ref, value_ref, start_ref, later_ref, power_ref, sums_ref, skip_ref):
    for index in range(grad_ref.shape[0]):
        channel_sums(
            *(r.at[index] for r in (grad_ref, value_ref, start_ref, later_ref, power_ref)),
            sums_ref.at[index],
            skip_ref.at[index],
        )


def channel_sums(grad_ref, value_ref, start_ref, later_ref, power_ref, sums_ref, skip_ref):
    modes = power_ref.shape[1] // 2
    row = lax.broadcasted_iota(jnp.int32, (BLOCK, BLOCK), 0)
    lane = lax.broadcasted_iota(jnp.int32, (BLOCK, BLOCK), 1)
    flip = jnp.where(row + lane == BLOCK - 1, 1.0, 0.0).astype(jnp.bfloat16)

    def fold(part):
        return jnp.sum(part.reshape(part.shape[0] // 8, 8, part.shape[1]), axis=0)

    grad, value = grad_ref[...], value_ref[...]
    start, later = start_ref[...], later_ref[...]
    product = grad.astype(jnp.float32) * value.astype(jnp.float32)
    skip_ref[...] = jnp.sum(product, axis=0, keepdims=True)
    turned = dot(value, flip, 1, 0).astype(jnp.bfloat16)
    out_sum = dot(grad, start, 0, 0)
    in_sum = dot(turned, later, 0, 0)
    cross = dot(grad, turned, 0, 0)
    cross = jnp.where(row + lane >= BLOCK - 1, cross, 0.0)
    lags = jnp.sum(pltpu.roll(cross, 1, 1, stride=1, stride_axis=0), axis=0, keepdims=True)
    lags = jnp.sum(jnp.where(row == lane, lags, 0.0), axis=1, keepdims=True)
    weight = lax.broadcasted_iota(jnp.int32, (BLOCK, modes), 0).astype(jnp.float32)
    power_re, power_im = power_ref[:, :modes], power_ref[:, modes:]
    terms = []
    for total, sign in ((out_sum, 1.0), (in_sum, -1.0)):
        term_re, term_im = cmul(power_re, power_im, total[:, :modes], sign * total[:, modes:])
        terms += [fold(term_re), fold(term_im), fold(weight * term_re), fold(weight * term_im)]
    later_re, later_im = (later[:, :modes].astype(jnp.float32), later[:, modes:].astype(jnp.float32))
    start_re, start_im = (start[:, :modes].astype(jnp.float32), start[:, modes:].astype(jnp.float32))
    terms += [
        fold(later_re * start_re + later_im * start_im),
        fold(later_re * start_im - later_im * start_re),
    ]
    local_re, local_im = power_re * lags, power_im * lags
    terms += [fold(local_re), fold(local_im), fold(weight * local_re), fold(weight * local_im)]
    for index, term in enumerate(terms):
        sums_ref[index : index + 1, :] = jnp.sum(term, axis=0, keepdims=True)


def run_sums(grads, values, starts, later, power):
    count, blocks, width = starts.shape
    group = 4

    def spec(*shape):
        return pl.BlockSpec((group,) + shape, lambda i: (i, 0, 0))

    return pl.pallas_call(
        sums_kernel,
        grid=(count // group,),
        in_specs=[spec(blocks, BLOCK)] * 2 + [spec(blocks, width)] * 2 + [spec(BLOCK, width)],
        out_specs=[spec(16, width // 2), spec(1, BLOCK)],
        out_shape=[
            jax.ShapeDtypeStruct((count, 16, width // 2), jnp.float32),
            jax.ShapeDtypeStruct((count, 1, BLOCK), jnp.float32),
        ],
        compiler_params=pltpu.CompilerParams(vmem_limit_bytes=VMEM),
        cost_estimate=cost(18),
    )(grads, values, starts, later, power)


def cost(microseconds):
    return pl.CostEstimate(
        flops=int(microseconds * 1e9), bytes_accessed=int(microseconds * 1e6), transcendentals=0
    )


def erf_parts(value):
    half = 0.5 * (1.0 + lax.erf(value * (1.0 / math.sqrt(2.0))))
    density = jnp.exp(-0.5 * value * value) * (1.0 / math.sqrt(2.0 * math.pi))
    return value * half, half + value * density


def norm_kernel(
    early_steps,
    place_ref,
    own_ref,
    near_ref,
    far_ref,
    far_late_ref,
    last_ref,
    last_late_ref,
    affine_ref,
    weight_ref,
    bias_ref,
    normed_ref,
    values_ref,
    slope_ref,
    before_ref,
    stats_ref,
    whole,
):
    place = place_ref[0]
    width = own_ref.shape[1]
    early = pl.program_id(0) < early_steps
    parts = (
        own_ref[...],
        near_ref[...],
        jnp.where(early, far_ref[...], far_late_ref[...]),
        jnp.where(early, last_ref[...], last_late_ref[...]),
    )
    for offset, part in enumerate(parts):
        start = pl.multiple_of((place ^ offset) * width, width)
        whole[:, pl.ds(start, width)] = part.astype(jnp.float32)
    inputs = whole[...]
    average = jnp.mean(inputs, axis=1, keepdims=True)
    spread = jnp.mean(inputs * inputs, axis=1, keepdims=True) - average * average
    inverse = lax.rsqrt(spread + EPSILON)
    normed = (inputs - average) * inverse * affine_ref[0:1, :] + affine_ref[1:2, :]
    normed = normed.astype(jnp.bfloat16)
    normed_ref[...] = normed
    before = dot(weight_ref[...], normed, 0, 1) + bias_ref[...]
    values, slope = erf_parts(before)
    values_ref[...] = values.astype(jnp.bfloat16)
    slope_ref[...] = slope
    before_ref[...] = before
    lane = lax.broadcasted_iota(jnp.int32, (inputs.shape[0], 128), 1)
    stats_ref[...] = jnp.where(lane < 64, average, inverse)


def run_norm(parts, affine, weight, bias):
    rows, width = parts[0].shape
    full, channels = weight.shape
    step = 512
    place = lax.axis_index("chan").astype(jnp.int32).reshape(1)
    half = parts[2].shape[0] // step
    full_rows = pl.BlockSpec((step, width), lambda i, p: (i, 0))
    first_rows = pl.BlockSpec((step, width), lambda i, p: (jnp.minimum(i, half - 1), 0))
    later_rows = pl.BlockSpec((step, width), lambda i, p: (jnp.maximum(i - half, 0), 0))
    return pl.pallas_call(
        partial(norm_kernel, half),
        grid_spec=pltpu.PrefetchScalarGridSpec(
            num_scalar_prefetch=1,
            grid=(rows // step,),
            in_specs=[
                full_rows,
                full_rows,
                first_rows,
                later_rows,
                first_rows,
                later_rows,
                pl.BlockSpec((2, full), lambda i, p: (0, 0)),
                pl.BlockSpec((full, channels), lambda i, p: (0, 0)),
                pl.BlockSpec((channels, 1), lambda i, p: (0, 0)),
            ],
            out_specs=[
                pl.BlockSpec((step, full), lambda i, p: (i, 0)),
                pl.BlockSpec((channels, step), lambda i, p: (0, i)),
                pl.BlockSpec((channels, step), lambda i, p: (0, i)),
                pl.BlockSpec((channels, step), lambda i, p: (0, i)),
                pl.BlockSpec((step, 128), lambda i, p: (i, 0)),
            ],
            scratch_shapes=[pltpu.VMEM((step, full), jnp.float32)],
        ),
        out_shape=[
            jax.ShapeDtypeStruct((rows, full), jnp.bfloat16),
            jax.ShapeDtypeStruct((channels, rows), jnp.bfloat16),
            jax.ShapeDtypeStruct((channels, rows), jnp.float32),
            jax.ShapeDtypeStruct((channels, rows), jnp.float32),
            jax.ShapeDtypeStruct((rows, 128), jnp.float32),
        ],
        compiler_params=pltpu.CompilerParams(vmem_limit_bytes=VMEM),
        cost_estimate=cost(8),
    )(place, *parts, affine, weight, bias[:, None])


def gate_kernel(count, where_ref, *refs):
    gate_body(where_ref, refs[:count], *refs[count:])


def gate_body(
    where_ref,
    front_refs,
    normed_ref,
    grad_ref,
    bias_ref,
    upper_ref,
    slope_ref,
    lifted_grad_ref,
    keep_ref,
    send_ref,
    bias_grad_ref,
    up_ref,
    down_ref,
    mix_ref,
):
    place = where_ref[0]
    size = keep_ref.shape[1]
    unpack_fronts(where_ref[1], front_refs, up_ref, down_ref, mix_ref)
    before = dot(normed_ref[...], up_ref[...], 1, 0) + bias_ref[...]
    hidden_grad = dot(grad_ref[...], down_ref[...], 1, 0)
    upper, slope = erf_parts(before)
    upper_ref[...] = upper.astype(jnp.bfloat16)
    slope_ref[...] = (hidden_grad * slope).astype(jnp.bfloat16)
    lifted_grad = (hidden_grad * upper).astype(jnp.bfloat16)
    lifted_grad_ref[...] = lifted_grad

    def piece(offset):
        start = pl.multiple_of((place ^ offset) * size, size)
        return dot(mix_ref[pl.ds(start, size), :], lifted_grad, 1, 1)

    keep_ref[0], keep_ref[1] = piece(0), piece(2)
    send_ref[0], send_ref[1] = piece(1), piece(3)
    part = jnp.sum(lifted_grad.astype(jnp.float32), axis=0, keepdims=True)

    @pl.when(pl.program_id(0) == 0)
    def _():
        bias_grad_ref[...] = jnp.zeros_like(bias_grad_ref)

    bias_grad_ref[...] += part


def ring_sources(place):
    spot = jnp.where(place % 2 == 0, place // 2, 7 - place // 2)
    spots = [spot]
    for step in range(1, 5):
        spots.append((spot + 8 - step) % 8)
        if step < 4:
            spots.append((spot + step) % 8)
    return [jnp.where(s < 4, 2 * s, 15 - 2 * s) for s in spots]


def unpack_fronts(place, front_refs, up_ref, down_ref, mix_ref):
    devices = sum(ref.shape[0] for ref in front_refs)
    part, mix_part = up_ref.shape[0] // devices, mix_ref.shape[0] // devices

    def copy(ref, index, rows, mix_rows):
        up_ref[rows, :] = ref[index, :part, :]
        down_ref[rows, :] = ref[index, part : 2 * part, :]
        mix_ref[mix_rows, :] = ref[index, 2 * part :, :]

    @pl.when(pl.program_id(0) == 0)
    def _():
        if len(front_refs) == 1:
            for source in range(devices):
                rows = slice(source * part, (source + 1) * part)
                mix_rows = slice(source * mix_part, (source + 1) * mix_part)
                copy(front_refs[0], source, rows, mix_rows)
        else:
            for ref, source in zip(front_refs, ring_sources(place)):
                rows = pl.ds(pl.multiple_of(source * part, part), part)
                mix_rows = pl.ds(pl.multiple_of(source * mix_part, mix_part), mix_part)
                copy(ref, 0, rows, mix_rows)


def front_specs(arrays):
    once = pl.Buffered(1)
    return [pl.BlockSpec(a.shape, lambda i, p: (0, 0, 0), pipeline_mode=once) for a in arrays]


def front_scratch(full, channels, units):
    return [
        pltpu.VMEM((full, units), jnp.bfloat16),
        pltpu.VMEM((full, units), jnp.bfloat16),
        pltpu.VMEM((channels, units), jnp.bfloat16),
    ]


def run_gate(normed, grad, fronts, where, channels, bias):
    rows, full = normed.shape
    units = fronts[0].shape[2]
    step = 256


    def fixed(*shape):
        return pl.BlockSpec(shape, lambda i, p: (0, 0))

    def rowwise(columns):
        return pl.BlockSpec((step, columns), lambda i, p: (i, 0))

    size = channels // 4
    pieces = pl.BlockSpec((2, size, step), lambda i, p: (0, 0, i))
    return pl.pallas_call(
        partial(gate_kernel, len(fronts)),
        grid_spec=pltpu.PrefetchScalarGridSpec(
            num_scalar_prefetch=1,
            grid=(rows // step,),
            in_specs=front_specs(fronts) + [rowwise(full), rowwise(full), fixed(1, units)],
            out_specs=[rowwise(units)] * 3 + [pieces] * 2 + [fixed(1, units)],
            scratch_shapes=front_scratch(full, channels, units),
        ),
        out_shape=[jax.ShapeDtypeStruct((rows, units), jnp.bfloat16)] * 3
        + [jax.ShapeDtypeStruct((2, size, rows), jnp.float32)] * 2
        + [jax.ShapeDtypeStruct((1, units), jnp.float32)],
        compiler_params=pltpu.CompilerParams(vmem_limit_bytes=VMEM),
        cost_estimate=cost(15),
    )(where, *fronts, normed, grad, bias[None])


def mid_kernel(count, where_ref, *refs):
    mid_body(where_ref, refs[:count], *refs[count:])


def mid_body(
    where_ref,
    front_refs,
    own_ref,
    near_ref,
    far_ref,
    last_ref,
    upper_ref,
    slope_ref,
    normed_ref,
    bias_ref,
    affine_ref,
    mixed_ref,
    hidden_ref,
    up_grad_ref,
    out_keep_ref,
    out_send_ref,
    feature_keep_ref,
    feature_send_ref,
    sums_ref,
    bias_grad_ref,
    up_ref,
    down_ref,
    mix_ref,
    whole,
):
    place = where_ref[0]
    width = out_keep_ref.shape[2]
    unpack_fronts(where_ref[1], front_refs, up_ref, down_ref, mix_ref)
    size = own_ref.shape[0]
    for offset, piece in enumerate((own_ref, near_ref, far_ref, last_ref)):
        start = pl.multiple_of((place ^ offset) * size, size)
        mixed_ref[pl.ds(start, size), :] = piece[...]
    lifted = dot(mixed_ref[...], mix_ref[...], 0, 0) + bias_ref[...]
    hidden = (upper_ref[...].astype(jnp.float32) * lifted).astype(jnp.bfloat16)
    up_grad = (slope_ref[...].astype(jnp.float32) * lifted).astype(jnp.bfloat16)
    hidden_ref[...] = hidden
    up_grad_ref[...] = up_grad

    @pl.when(pl.program_id(0) == 0)
    def _():
        bias_grad_ref[...] = jnp.zeros_like(bias_grad_ref)

    bias_grad_ref[...] += jnp.sum(up_grad.astype(jnp.float32), axis=0, keepdims=True)

    def part(offset):
        start = pl.multiple_of((place ^ offset) * width, width)
        return whole[:, pl.ds(start, width)].astype(jnp.bfloat16)

    whole[...] = dot(hidden, down_ref[...], 1, 1)
    out_keep_ref[0], out_keep_ref[1] = part(0), part(2)
    out_send_ref[0], out_send_ref[1] = part(1), part(3)
    feature = dot(up_grad, up_ref[...], 1, 1)
    whole[...] = feature
    feature_keep_ref[0], feature_keep_ref[1] = part(0), part(2)
    feature_send_ref[0], feature_send_ref[1] = part(1), part(3)
    one = jnp.sum(feature * affine_ref[0:1, :], axis=1, keepdims=True)
    shifted = normed_ref[...].astype(jnp.float32) - affine_ref[1:2, :]
    two = jnp.sum(feature * shifted, axis=1, keepdims=True)
    lane = lax.broadcasted_iota(jnp.int32, (feature.shape[0], 128), 1)
    sums_ref[...] = jnp.where(lane == 0, one, jnp.where(lane == 1, two, 0.0)).T[0:8, :]


def run_mid(parts, upper, slope, normed, fronts, where, bias, affine):
    rows, full = normed.shape
    units = fronts[0].shape[2]
    channels = 4 * parts[0].shape[0]
    width = full // 4
    step = 512

    def fixed(*shape):
        return pl.BlockSpec(shape, lambda i, p: (0, 0))

    def rowwise(columns):
        return pl.BlockSpec((step, columns), lambda i, p: (i, 0))

    def columns(count):
        return pl.BlockSpec((count, step), lambda i, p: (0, i))

    pieces = pl.BlockSpec((2, step, width), lambda i, p: (0, i, 0))
    piece_shape = jax.ShapeDtypeStruct((2, rows, width), jnp.bfloat16)
    return pl.pallas_call(
        partial(mid_kernel, len(fronts)),
        grid_spec=pltpu.PrefetchScalarGridSpec(
            num_scalar_prefetch=1,
            grid=(rows // step,),
            in_specs=front_specs(fronts)
            + [
                columns(channels // 4),
                columns(channels // 4),
                columns(channels // 4),
                columns(channels // 4),
                rowwise(units),
                rowwise(units),
                rowwise(full),
                fixed(1, units),
                fixed(2, full),
            ],
            out_specs=[columns(channels)]
            + [rowwise(units)] * 2
            + [pieces] * 4
            + [columns(8), fixed(1, units)],
            scratch_shapes=front_scratch(full, channels, units)
            + [pltpu.VMEM((step, full), jnp.float32)],
        ),
        out_shape=[jax.ShapeDtypeStruct((channels, rows), jnp.bfloat16)]
        + [jax.ShapeDtypeStruct((rows, units), jnp.bfloat16)] * 2
        + [piece_shape] * 4
        + [
            jax.ShapeDtypeStruct((8, rows), jnp.float32),
            jax.ShapeDtypeStruct((1, units), jnp.float32),
        ],
        compiler_params=pltpu.CompilerParams(vmem_limit_bytes=VMEM),
        cost_estimate=cost(14),
    )(where, *fronts, *parts, upper, slope, normed, bias[None], affine)


def payload_kernel(
    grad_ref, slope_ref, before_ref, gain_ref, bias_ref, sums_ref, payload_ref, bias_grad_ref
):
    count = grad_ref.shape[0]
    grad = (grad_ref[...].astype(jnp.float32) * slope_ref[...]).astype(jnp.bfloat16)
    payload_ref[:count, :] = grad
    grad = grad.astype(jnp.float32)
    centred = before_ref[...] - bias_ref[...] - gain_ref[:, 1:2]
    one = jnp.sum(grad * gain_ref[:, 0:1], axis=0, keepdims=True) + sums_ref[0:1, :]
    two = jnp.sum(grad * centred, axis=0, keepdims=True) + sums_ref[1:2, :]
    row = lax.broadcasted_iota(jnp.int32, (16, grad.shape[1]), 0)
    one_high = one.astype(jnp.bfloat16).astype(jnp.float32)
    two_high = two.astype(jnp.bfloat16).astype(jnp.float32)
    tail = jnp.where(row == 0, one_high, jnp.where(row == 1, one - one_high, 0.0))
    tail = jnp.where(row == 2, two_high, jnp.where(row == 3, two - two_high, tail))
    payload_ref[count:, :] = tail.astype(jnp.bfloat16)
    part = jnp.sum(grad, axis=1, keepdims=True)

    @pl.when(pl.program_id(0) == 0)
    def _():
        bias_grad_ref[...] = jnp.zeros_like(bias_grad_ref)

    bias_grad_ref[...] += part


def run_payload(grad, slope, before, gain, bias, sums):
    count, rows = grad.shape
    step = 512

    def columns(lines):
        return pl.BlockSpec((lines, step), lambda i: (0, i))

    def fixed(*shape):
        return pl.BlockSpec(shape, lambda i: (0, 0))

    return pl.pallas_call(
        payload_kernel,
        grid=(rows // step,),
        in_specs=[columns(count)] * 3 + [fixed(count, 2), fixed(count, 1), columns(8)],
        out_specs=[columns(count + 16), fixed(count, 1)],
        out_shape=[
            jax.ShapeDtypeStruct((count + 16, rows), jnp.bfloat16),
            jax.ShapeDtypeStruct((count, 1), jnp.float32),
        ],
        cost_estimate=cost(3),
    )(grad, slope, before, gain, bias[:, None], sums)


def final_kernel(
    _,
    own_ref,
    near_ref,
    far_ref,
    last_ref,
    rows_ref,
    kept_ref,
    sent_ref,
    passed_ref,
    tokens_ref,
    stats_ref,
    grad_ref,
    gain_ref,
    input_grad_ref,
    vectors_ref,
    gain_grad_ref,
    shift_grad_ref,
    down_grad_ref,
    total,
):
    size = own_ref.shape[0] - 16
    row = lax.broadcasted_iota(jnp.int32, (16, 256), 0)
    lane = lax.broadcasted_iota(jnp.int32, (16, 256), 1)
    pick = jnp.where((row < 2) == (lane < 128), 1.0, 0.0)
    pick = jnp.where(row < 4, pick, 0.0).astype(jnp.bfloat16)
    normed_grad = (
        kept_ref[0].astype(jnp.float32)
        + sent_ref[0].astype(jnp.float32)
        + passed_ref[...].astype(jnp.float32)
    )
    totals = jnp.zeros((normed_grad.shape[0], 256), jnp.float32)
    for offset, piece in enumerate((own_ref, near_ref, far_ref, last_ref)):
        weights = rows_ref[:, offset * size : (offset + 1) * size]
        normed_grad += dot(piece[:size, :], weights, 0, 1)
        totals += dot(piece[size:, :], pick, 0, 0)
    scaled = normed_grad * gain_ref[...]
    centred = (tokens_ref[...].astype(jnp.float32) - stats_ref[:, 0:1]) * stats_ref[:, 64:65]
    grad = grad_ref[...].astype(jnp.float32)
    mean_one = totals[:, 0:1] * (1.0 / D)
    mean_two = totals[:, 128:129] * (1.0 / D)
    input_grad_ref[...] = stats_ref[:, 64:65] * (scaled - mean_one - centred * mean_two) + grad

    @pl.when(pl.program_id(0) == 0)
    def _():
        gain_grad_ref[...] = jnp.zeros_like(gain_grad_ref)
        shift_grad_ref[...] = jnp.zeros_like(shift_grad_ref)
        down_grad_ref[...] = jnp.zeros_like(down_grad_ref)

    gain_grad_ref[...] += jnp.sum(normed_grad * centred, axis=0, keepdims=True)
    shift_grad_ref[...] += jnp.sum(normed_grad, axis=0, keepdims=True)
    down_grad_ref[...] += jnp.sum(grad, axis=0, keepdims=True)

    @pl.when(pl.program_id(0) == pl.num_programs(0) - 1)
    def _():
        devices = vectors_ref.shape[0]
        part = gain_grad_ref.shape[1] // devices
        row = lax.broadcasted_iota(jnp.int32, (16, 128), 0)
        total[...] = jnp.zeros_like(total)
        for turn in range(devices):
            for index, ref in enumerate((gain_grad_ref, shift_grad_ref, down_grad_ref)):
                total[:, index * part : (index + 1) * part] = ref[
                    :, turn * part : (turn + 1) * part
                ]
            high = total[...].astype(jnp.bfloat16).astype(jnp.float32)
            pair = jnp.where(row == 0, high, jnp.where(row == 1, total[...] - high, 0.0))
            vectors_ref[turn] = pair.astype(jnp.bfloat16)


def run_final(parts, input_rows, kept, sent, passed, tokens, stats, grad, gain):
    rows, width = tokens.shape
    lines = parts[0].shape[0]
    devices = lax.axis_size("seq")
    step = 512
    place = lax.axis_index("chan").astype(jnp.int32).reshape(1)

    def fixed(*shape):
        return pl.BlockSpec(shape, lambda i, p: (0, 0))

    def rowwise(columns):
        return pl.BlockSpec((step, columns), lambda i, p: (i, 0))

    def columns(count):
        return pl.BlockSpec((count, step), lambda i, p: (0, i))

    piece = pl.BlockSpec((1, step, width), lambda i, p: (0, i, 0))
    return pl.pallas_call(
        final_kernel,
        grid_spec=pltpu.PrefetchScalarGridSpec(
            num_scalar_prefetch=1,
            grid=(rows // step,),
            in_specs=[columns(lines)] * 4
            + [
                fixed(*input_rows.shape),
                piece,
                piece,
                rowwise(width),
                rowwise(width),
                rowwise(128),
                pl.BlockSpec((step, width), lambda i, p: (i, p[0])),
                fixed(1, width),
            ],
            out_specs=[rowwise(width), pl.BlockSpec((devices, 16, 128), lambda i, p: (0, 0, 0))],
            scratch_shapes=[pltpu.VMEM((1, width), jnp.float32)] * 3
            + [pltpu.VMEM((1, 128), jnp.float32)],
        ),
        out_shape=[
            jax.ShapeDtypeStruct((rows, width), jnp.float32),
            jax.ShapeDtypeStruct((devices, 16, 128), jnp.bfloat16),
        ],
        cost_estimate=cost(6),
    )(place, *parts, input_rows, kept, sent, passed, tokens, stats, grad, gain[None])


def grads_kernel(
    side_ref,
    outer_ref,
    normed_ref,
    mixed_ref,
    hidden_ref,
    up_ref,
    lifted_ref,
    down_send_ref,
    down_keep_ref,
    rest_send_ref,
    rest_keep_ref,
    whole,
    mix_whole,
):
    kept = side_ref[0]
    part = outer_ref.shape[1] // 2
    mix_part = mixed_ref.shape[0] // 2

    def half(scratch, size, side):
        return scratch[pl.ds(pl.multiple_of(side * size, size), size), :].astype(jnp.bfloat16)

    whole[...] = dot(outer_ref[...], hidden_ref[...], 0, 0)
    down_send_ref[0] = half(whole, part, 1 - kept)
    down_keep_ref[0] = half(whole, part, kept)
    whole[...] = dot(normed_ref[...], up_ref[...], 0, 0)
    rest_send_ref[0, :part, :] = half(whole, part, 1 - kept)
    rest_keep_ref[0, :part, :] = half(whole, part, kept)
    mix_whole[...] = dot(mixed_ref[...], lifted_ref[...], 1, 0)
    rest_send_ref[0, part:, :] = half(mix_whole, mix_part, 1 - kept)
    rest_keep_ref[0, part:, :] = half(mix_whole, mix_part, kept)


def run_grads(outer, normed, mixed, hidden, up, lifted):
    rows, full = outer.shape
    channels = mixed.shape[0]
    units = hidden.shape[1]
    devices = lax.axis_size("seq")
    half = devices // 2
    part, mix_part = full // devices, channels // devices
    side = (lax.axis_index("seq") & 1).astype(jnp.int32).reshape(1)

    def fixed(*shape):
        return pl.BlockSpec(shape, lambda i, p: (0, 0), pipeline_mode=pl.Buffered(1))

    whole = part + mix_part
    return pl.pallas_call(
        grads_kernel,
        grid_spec=pltpu.PrefetchScalarGridSpec(
            num_scalar_prefetch=1,
            grid=(half,),
            in_specs=[
                pl.BlockSpec((rows, 2 * part), lambda i, p: (0, i)),
                pl.BlockSpec((rows, 2 * part), lambda i, p: (0, i)),
                pl.BlockSpec((2 * mix_part, rows), lambda i, p: (i, 0)),
                fixed(rows, units),
                fixed(rows, units),
                fixed(rows, units),
            ],
            out_specs=[pl.BlockSpec((1, part, units), lambda i, p: (i, 0, 0))] * 2
            + [pl.BlockSpec((1, whole, units), lambda i, p: (i, 0, 0))] * 2,
            scratch_shapes=[
                pltpu.VMEM((2 * part, units), jnp.float32),
                pltpu.VMEM((2 * mix_part, units), jnp.float32),
            ],
        ),
        out_shape=[jax.ShapeDtypeStruct((half, part, units), jnp.bfloat16)] * 2
        + [jax.ShapeDtypeStruct((half, whole, units), jnp.bfloat16)] * 2,
        compiler_params=pltpu.CompilerParams(vmem_limit_bytes=VMEM),
        cost_estimate=cost(14),
    )(side, outer, normed, mixed, hidden, up, lifted)


def swap(value, distance):
    return lax.ppermute(value, "chan", [(i, i ^ distance) for i in range(4)])


def gather_parts(piece):
    far = swap(piece, 2)
    return piece, swap(piece, 1), far, swap(far, 1)


def after(value, *others):
    return lax.optimization_barrier((value,) + others)[0]


def ring_steps(moving, steps):
    devices = lax.axis_size("seq")
    order = (0, 2, 4, 6, 7, 5, 3, 1)
    arrived = []
    for step in steps:
        following = []
        for piece, direction in zip(moving, (1, -1)):
            if direction < 0 and step == devices // 2:
                continue
            pairs = [(order[i], order[(i + direction) % devices]) for i in range(devices)]
            following.append(lax.ppermute(piece, "seq", pairs))
        arrived += following
        moving = following
    return arrived


def to_channels(value, sequences):
    devices = lax.axis_size("seq")
    channels, tokens = value.shape
    share = channels // devices
    got = lax.all_to_all(value.reshape(devices, share, tokens), "seq", 0, 0, tiled=True)
    got = got.reshape(sequences, devices // sequences, share, tokens)
    return got.transpose(1, 0, 2, 3).reshape(devices // sequences, sequences * share, tokens)


def to_tokens(value, sequences):
    devices = lax.axis_size("seq")
    sources, count, tokens = value.shape
    share = count // sequences
    sent = value.reshape(sources, sequences, share, tokens).transpose(1, 0, 2, 3)
    got = lax.all_to_all(sent.reshape(devices, share, tokens), "seq", 0, 0, tiled=True)
    return got.reshape(devices * share, tokens)


def tile_rows(flat):
    width = flat.shape[-1]
    padded = -(-width // 128) * 128
    flat = jnp.pad(flat, [(0, 0)] * (flat.ndim - 1) + [(0, padded - width)])
    return flat.reshape(flat.shape[:-1] + (padded // 128, 128))


def planes(value, count):
    parts = []
    for _ in range(count):
        part = lax.reduce_precision(value, 8, 7)
        parts.append(part.astype(jnp.bfloat16))
        value = value - part
    return parts


def plain_grads(outer, normed, mixed, hidden, up, lifted):
    devices = lax.axis_size("seq")
    side = lax.axis_index("seq") & 1

    def parts(value):
        value = value.astype(jnp.bfloat16)
        return value.reshape(devices // 2, 2, value.shape[0] // devices, value.shape[1])

    def pick(value, index):
        return lax.dynamic_index_in_dim(value, index, 1, False)

    down = parts(dot(outer, hidden, 0, 0))
    rest = (parts(dot(normed, up, 0, 0)), parts(dot(mixed, lifted, 1, 0)))
    rest = jnp.concatenate(rest, axis=2)
    return (pick(down, 1 - side), pick(down, side), pick(rest, 1 - side), pick(rest, side))


def halve(sent, kept):
    devices = lax.axis_size("seq")
    got = lax.ppermute(sent, "seq", [(i, i ^ 1) for i in range(devices)])
    return (kept.astype(jnp.float32) + got.astype(jnp.float32)).astype(jnp.bfloat16)


def settle_apart(halves):
    devices = lax.axis_size("seq")
    if devices != 8:
        return settle(halves)
    line = lax.axis_index("seq") >> 1
    total = lax.dynamic_index_in_dim(halves, line, 0, False).astype(jnp.float32)
    for distance in (2, 3, 1):
        sent = lax.dynamic_index_in_dim(halves, line ^ distance, 0, False)
        pairs = [(i, i ^ (2 * distance)) for i in range(devices)]
        total += lax.ppermute(sent, "seq", pairs).astype(jnp.float32)
    return total


def settle(halves):
    devices = lax.axis_size("seq")
    groups = [[i for i in range(devices) if i & 1 == side] for side in (0, 1)]
    got = lax.all_to_all(halves, "seq", 0, 0, axis_index_groups=groups, tiled=True)
    return jnp.sum(got.astype(jnp.float32), axis=0)


def per_device(
    tokens,
    norm_gain,
    norm_shift,
    up_weight,
    up_bias,
    input_weight,
    input_bias,
    mix_weight,
    mix_bias,
    down_weight,
    down_bias,
    decay_rate,
    decay_freq,
    step_log,
    read_real,
    read_imag,
    skip_gain,
    out_grad,
):
    row_count, width = tokens.shape
    devices = lax.axis_size("seq")
    place = lax.axis_index("chan")
    sequences = devices * row_count // LENGTH
    feature_rows, channels = input_weight.shape
    units = up_weight.shape[1]
    share = channels // devices
    modes_here = decay_rate.shape[0]
    modes = modes_here * devices
    near = swap(tokens, 1)
    early_rows = row_count // 4
    far, far_late = swap(tokens[:early_rows], 2), swap(tokens[early_rows:], 2)
    token_parts = (tokens, near, far, far_late, swap(far, 1), swap(far_late, 1))

    pair = jnp.stack([norm_gain, norm_shift])
    pairs = jnp.stack([pair, swap(pair, 1), swap(pair, 2), swap(pair, 3)])
    pairs = jnp.stack([pairs[place ^ i] for i in range(4)])
    fronts = jnp.concatenate([up_weight, down_weight.T, mix_weight])
    where = jnp.stack([place, lax.axis_index("seq")]).astype(jnp.int32)
    ring = [fronts] + ring_steps((fronts, fronts), (1, 2)) if devices == 8 else []
    pairs = after(pairs, far, *ring[1:3])
    small = (pairs.reshape(-1), up_bias, input_bias, mix_bias, down_bias, decay_rate, decay_freq)
    sizes = [v.shape[0] for v in small]
    small = tile_rows(jnp.concatenate(small))
    reads = jnp.concatenate([read_real, read_imag], axis=1).reshape(devices, share, 2 * modes_here)
    reads = jnp.pad(reads, ((0, 0), (0, 0), (0, 128 - 2 * modes_here)))
    copies = jnp.broadcast_to(small, (devices,) + small.shape)
    exact = jnp.concatenate([reads, copies], axis=1)
    exact_rows = exact.shape[1]
    weights = jnp.broadcast_to(input_weight, (devices,) + input_weight.shape)
    got = jnp.concatenate(planes(exact, 3) + [weights], axis=1)
    got = lax.all_to_all(got, "seq", 0, 0, tiled=True)
    input_full = got[:, 3 * exact_rows :].reshape(4 * width, channels)

    def exact_part(start, stop):
        rows = [got[:, i * exact_rows + start : i * exact_rows + stop] for i in range(3)]
        rows = [r.astype(jnp.float32) for r in rows]
        return rows[0] + (rows[1] + rows[2])

    small = exact_part(share, exact_rows).reshape(devices, -1)
    parts, spot = [], 0
    for size in sizes:
        parts.append(small[:, spot : spot + size])
        spot += size
    affine = parts[0].reshape(devices, 4, 2, -1).transpose(2, 1, 0, 3).reshape(2, 4 * width)
    input_shift = parts[2].reshape(-1)

    normed, values_low, in_slope, pre_in, stats = run_norm(
        token_parts, affine, input_full, input_shift
    )
    values = to_channels(values_low, sequences)
    if devices == 8:
        ring += ring_steps(tuple(after(p, normed) for p in ring[3:5]), (3, 4))
        fronts = tuple(p[None] for p in ring)
    else:
        fronts = (lax.all_gather(fronts, "seq", axis=0),)

    got = after(got, normed)
    parts = lax.optimization_barrier(tuple(parts) + (normed,))[:-1]
    reads = exact_part(0, share)[:, :, : 2 * modes_here].transpose(1, 0, 2)
    read_re = reads[:, :, :modes_here].reshape(share, modes)
    read_im = reads[:, :, modes_here:].reshape(share, modes)
    up_shift, _, mix_shift, down_shift, rate, freq = (p.reshape(-1) for p in parts[1:])

    spacing = jnp.exp(step_log)
    damping = spacing[:, None] * rate[None, :]
    rotation = spacing[:, None] * freq[None, :]
    inflow = -jnp.expm1(-damping)
    extents = 2.0 ** jnp.asarray([0, 1, 2, 3, 4, 5, 6, 7, 11, 12, 13])[None, :, None]
    length = jnp.exp(-damping[:, None] * extents)
    angle = rotation[:, None] * extents
    power_re, power_im = length * jnp.cos(angle), length * jnp.sin(angle)

    def repeat(value):
        return jnp.tile(value, (sequences,) + (1,) * (value.ndim - 1))

    def rows(value_re, value_im):
        return repeat(jnp.concatenate([value_re, value_im], axis=1)[:, None])

    power, out_table, in_table, toeplitz = make_tables(
        repeat(power_re[:, :8]), repeat(power_im[:, :8]), repeat(read_re), repeat(read_im), repeat(inflow)
    )
    jump = repeat(jnp.concatenate([power_re[:, 7:], power_im[:, 7:]], axis=2))
    flow = rows(inflow, inflow)
    lead = rows(*cmul(read_re, read_im, power_re[:, 0], power_im[:, 0]))
    skip = repeat(skip_gain)

    pieces = gather_parts(after(input_full, normed))
    pieces = [lax.dynamic_slice_in_dim(p, place * width, width, 0) for p in pieces]
    input_rows = jnp.concatenate(pieces, axis=1)
    in_gain = jnp.dot(
        input_full.T.astype(jnp.float32), affine.T, precision=lax.Precision.HIGHEST
    )
    mixed, starts, values_split = run_forward(
        after(values, input_rows, in_gain, *ring[5:7]), skip, jump, flow, lead, out_table, in_table, toeplitz
    )
    mixed_tokens = to_tokens(after(mixed, *ring[7:8]), sequences)

    upper, up_slope, lifted_grad, channel_keep, channel_send, mix_bias_part = run_gate(
        after(normed, mixed), out_grad, fronts, where, 4 * channels, up_shift
    )
    channel_sent = swap(after(channel_send, mixed_tokens), 1)
    mixed_parts = gather_parts(mixed_tokens)
    channel_passed = (channel_keep[1] + channel_sent[1]).astype(jnp.bfloat16)
    channel_sum = channel_keep[0] + channel_sent[0]
    channel_far = swap(channel_passed, 2)
    mixed_grad = (channel_sum + channel_far.astype(jnp.float32)).astype(jnp.bfloat16)
    grads = to_channels(mixed_grad, sequences)

    (
        mixed_full,
        hidden,
        up_pre_grad,
        out_keep,
        out_send,
        feature_keep,
        feature_send,
        up_sums,
        up_bias_part,
    ) = run_mid(
        (after(mixed_parts[0], channel_passed),) + mixed_parts[1:],
        upper,
        up_slope,
        normed,
        fronts,
        where,
        mix_shift,
        affine,
    )
    out_sent, feature_sent = swap(out_send, 1), swap(feature_send, 1)

    def passed(keep, sent):
        return (keep[1].astype(jnp.float32) + sent[1].astype(jnp.float32)).astype(jnp.bfloat16)

    feature_passed = passed(feature_keep, feature_sent)
    out_passed = passed(out_keep, out_sent)
    make_grads = run_grads if feature_rows % 128 == 0 else plain_grads
    down_send, down_keep, rest_send, rest_keep = make_grads(
        out_grad, normed, mixed_full, after(hidden, mixed_grad), up_pre_grad, lifted_grad
    )
    feature_far = swap(feature_passed, 2)
    down_sent, rest_sent = after(down_send, grads), after(rest_send, grads)
    grads = after(grads, down_send, feature_passed, out_passed)
    values_grad, later, grads_split = run_backward(
        grads, skip, jump, flow, lead, out_table, in_table, toeplitz
    )
    values_back = to_tokens(after(values_grad, feature_far), sequences)
    out_far = swap(after(out_passed, values_grad), 2)
    sums, skip_sums = run_sums(grads_split, values_split, starts, later, power)
    down_half = halve(down_sent, after(down_keep, values_grad))
    rest_half = halve(rest_sent, after(rest_keep, values_grad, out_far))
    down_total = settle_apart(down_half)
    rest_total = settle(after(rest_half, values_back))
    down_weight_grad = down_total.T
    up_weight_grad, mix_weight_grad = rest_total[:feature_rows], rest_total[feature_rows:]
    payload, input_bias_part = run_payload(
        after(values_back, sums, rest_half, down_total), in_slope, pre_in, in_gain, input_shift, up_sums
    )
    payload_parts = gather_parts(payload)
    sums, skip_sums, up_bias_part, mix_bias_part, down_shift, gain_all, _ = lax.optimization_barrier(
        (sums, skip_sums, up_bias_part, mix_bias_part, down_shift, affine[0], payload)
    )
    gain_own = lax.dynamic_slice_in_dim(gain_all, place * width, width)
    input_grad, late_vectors = run_final(
        payload_parts,
        input_rows,
        feature_keep,
        feature_sent,
        feature_far,
        tokens,
        stats,
        out_grad,
        gain_own,
    )

    inputs = tokens.astype(jnp.float32)
    output = (
        out_keep[0].astype(jnp.float32)
        + out_sent[0].astype(jnp.float32)
        + out_far.astype(jnp.float32)
        + down_shift
        + inputs
    )

    sums = jnp.concatenate([sums[:, :4], sums[:, 4:8] * flow[:, :, :modes], sums[:, 8:]], axis=1)
    sums = jnp.sum(sums.reshape((sequences, share) + sums.shape[1:]), axis=0)
    skip_grad = jnp.sum(skip_sums.reshape(sequences, share, BLOCK), axis=(0, 2))
    out_zero = cmul(power_re[:, 0], power_im[:, 0], sums[:, 0], sums[:, 1])
    out_one = cmul(
        power_re[:, 0], power_im[:, 0], sums[:, 0] + sums[:, 2], sums[:, 1] + sums[:, 3]
    )
    chained = cmul(power_re[:, 7], power_im[:, 7], sums[:, 8], sums[:, 9])
    local_zero, local_one = (sums[:, 10], sums[:, 11]), (sums[:, 12], sums[:, 13])
    read_re_grad = out_zero[0] + inflow * local_zero[0]
    read_im_grad = -out_zero[1] - inflow * local_zero[1]
    turn = cmul(
        read_re, read_im, out_one[0] + inflow * local_one[0], out_one[1] + inflow * local_one[1]
    )
    turn_re = turn[0] + sums[:, 6] + BLOCK * chained[0]
    turn_im = turn[1] + sums[:, 7] + BLOCK * chained[1]
    inflow_grad = sums[:, 4] / inflow + read_re * local_zero[0] - read_im * local_zero[1]
    damping_grad = jnp.exp(-damping) * inflow_grad - turn_re
    rotation_grad = -turn_im
    step_log_grad = spacing * jnp.sum(
        rate[None, :] * damping_grad + freq[None, :] * rotation_grad, axis=1
    )
    rates = jnp.stack(
        [
            jnp.sum(spacing[:, None] * damping_grad, axis=0),
            jnp.sum(spacing[:, None] * rotation_grad, axis=0),
        ]
    )
    rates = rates + swap(rates, 1)
    input_part = dot(normed, after(payload, rates)[:channels], 0, 1)
    rates = rates + swap(rates, 2)

    read_grads = jnp.stack([read_re_grad, read_im_grad], axis=1)
    read_grads = read_grads.reshape(share, 2, devices, modes_here).transpose(2, 0, 1, 3)
    read_grads = read_grads.reshape(devices, share, 2 * modes_here)
    read_grads = jnp.pad(read_grads, ((0, 0), (0, 0), (0, 128 - 2 * modes_here)))

    def line_up(vectors):
        vectors = [v.reshape(devices, -1) for v in vectors]
        sizes = [v.shape[1] for v in vectors]
        return tile_rows(jnp.concatenate(vectors, axis=1)), sizes

    def take_apart(flat, sizes):
        parts, spot = [], 0
        for size in sizes:
            parts.append(flat[spot : spot + size])
            spot += size
        return parts

    vectors, sizes = line_up(
        (
            up_bias_part,
            input_bias_part,
            mix_bias_part,
            rates[0],
            rates[1],
        )
    )
    input_part = input_part.reshape(devices, feature_rows, channels)
    parcel = jnp.concatenate([read_grads, vectors], axis=1)
    exact_rows = -(-parcel.shape[1] // 16) * 16
    parcel = jnp.pad(parcel, ((0, 0), (0, exact_rows - parcel.shape[1]), (0, 0)))
    parcel = jnp.concatenate(planes(parcel, 2) + [input_part.astype(jnp.bfloat16)], axis=1)
    late = jnp.concatenate([parcel, after(late_vectors, rest_total)], axis=1)
    late = lax.all_to_all(late, "seq", 0, 0, tiled=True).astype(jnp.float32)
    input_weight_grad = jnp.sum(late[:, 2 * exact_rows : 2 * exact_rows + feature_rows], axis=0)
    tail = jnp.sum(late[:, 2 * exact_rows + feature_rows :], axis=(0, 1))
    late = late[:, :exact_rows] + late[:, exact_rows : 2 * exact_rows]
    read_late = late[:, :share, : 2 * modes_here].reshape(channels, 2 * modes_here)
    late = take_apart(jnp.sum(late[:, share:], axis=0).reshape(-1), sizes)
    up_bias_grad, input_bias_grad, mix_bias_grad, rate_out, freq_out = late
    gain_grad, shift_grad, down_bias_grad = take_apart(tail, [width // devices] * 3)
    return (
        output,
        input_grad,
        gain_grad,
        shift_grad,
        up_weight_grad,
        up_bias_grad,
        input_weight_grad,
        input_bias_grad,
        mix_weight_grad,
        mix_bias_grad,
        down_weight_grad,
        down_bias_grad,
        rate_out,
        freq_out,
        step_log_grad,
        read_late[:, :modes_here],
        read_late[:, modes_here:],
        skip_grad,
    )


def solution(mesh):
    return jax.shard_map(
        per_device,
        mesh=mesh,
        in_specs=(
            P("seq", "chan"),
            P(("chan", "seq")),
            P(("chan", "seq")),
            P("seq", "chan"),
            P(("chan", "seq")),
            P("seq", "chan"),
            P(("chan", "seq")),
            P("seq", "chan"),
            P(("chan", "seq")),
            P("chan", "seq"),
            P(("chan", "seq")),
            P("seq"),
            P("seq"),
            P(("chan", "seq")),
            P("chan", "seq"),
            P("chan", "seq"),
            P(("chan", "seq")),
            P("seq", None),
        ),
        out_specs=(
            P("seq", "chan"),
            P("seq", "chan"),
            P(("chan", "seq")),
            P(("chan", "seq")),
            P("seq", "chan"),
            P(("chan", "seq")),
            P("seq", "chan"),
            P(("chan", "seq")),
            P("seq", "chan"),
            P(("chan", "seq")),
            P("chan", "seq"),
            P(("chan", "seq")),
            P("seq"),
            P("seq"),
            P(("chan", "seq")),
            P("chan", "seq"),
            P("chan", "seq"),
            P(("chan", "seq")),
        ),
        check_vma=False,
    )
```

```python
from functools import partial
import math

import jax
import jax.numpy as jnp
from jax import lax
from jax.experimental import pallas as pl
from jax.experimental.pallas import tpu as pltpu
from jax.sharding import PartitionSpec as P

D = 1024
LENGTH = 16384
EPSILON = 1e-05


BLOCK = 128
MEGA = 1024 * 1024
VMEM = 56 * MEGA


def dot(left, right, left_dim, right_dim):
    return lax.dot_general(
        left, right, (((left_dim,), (right_dim,)), ((), ())), preferred_element_type=jnp.float32
    )


def cmul(a_re, a_im, b_re, b_im):
    return (a_re * b_re - a_im * b_im, a_re * b_im + a_im * b_re)


def grow(first, reversed_rows, mode_powers, store):
    row = lax.broadcasted_iota(jnp.int32, (8, first[0].shape[1]), 0)
    exponent = 7 - row if reversed_rows else row
    part = (
        jnp.broadcast_to(first[0], row.shape),
        jnp.broadcast_to(first[1], row.shape),
    )
    for level in range(3):
        factor_re, factor_im = mode_powers(level)
        taken = (exponent >> level) & 1 == 1
        part = cmul(*part, jnp.where(taken, factor_re, 1.0), jnp.where(taken, factor_im, 0.0))
    spot = BLOCK - 8 if reversed_rows else 0
    store(spot, part[0], part[1])
    whole = part
    size, level = 8, 3
    while size < BLOCK:
        factor = mode_powers(level)
        fresh = cmul(*whole, *factor)
        spot = BLOCK - 2 * size if reversed_rows else size
        store(spot, *fresh)
        pair = (fresh, whole) if reversed_rows else (whole, fresh)
        whole = tuple(jnp.concatenate([p, q], axis=0) for p, q in zip(*pair))
        size, level = 2 * size, level + 1


def tables_kernel(
    power_re_ref,
    power_im_ref,
    read_re_ref,
    read_im_ref,
    inflow_ref,
    power_ref,
    out_table_ref,
    in_table_ref,
    toeplitz_ref,
):
    modes = power_re_ref.shape[2]
    lower, upper = slice(0, modes), slice(modes, 2 * modes)

    def mode_powers(level):
        return (power_re_ref[0, level : level + 1, :], power_im_ref[0, level : level + 1, :])

    inflow = inflow_ref[0]
    one, none = jnp.ones_like(inflow), jnp.zeros_like(inflow)

    def store_power(spot, part_re, part_im):
        rows = slice(spot, spot + part_re.shape[0])
        power_ref[0, rows, lower] = part_re
        power_ref[0, rows, upper] = part_im

    grow((one, none), False, mode_powers, store_power)
    exact = jnp.concatenate([power_ref[0, :, lower], -power_ref[0, :, upper]], axis=1)
    rounded = exact.astype(jnp.bfloat16)
    out_table_ref[0] = rounded
    rest = (exact - rounded.astype(jnp.float32)).astype(jnp.bfloat16)
    backward = []

    def store_in(spot, part_re, part_im):
        backward.append((spot, part_re, part_im))

    grow((one, none), True, mode_powers, store_in)
    backward.sort(key=lambda entry: entry[0])
    in_table_ref[0, :, lower] = jnp.concatenate([e[1] for e in backward], 0).astype(jnp.bfloat16)
    in_table_ref[0, :, upper] = jnp.concatenate([e[2] for e in backward], 0).astype(jnp.bfloat16)
    weight = jnp.concatenate([read_re_ref[0] * inflow, read_im_ref[0] * inflow], axis=1)
    high = weight.astype(jnp.bfloat16).astype(jnp.float32)
    row = lax.broadcasted_iota(jnp.int32, (16, 2 * modes), 0)
    probe = jnp.where(row == 0, high, jnp.where(row == 1, weight - high, 0.0))
    probe = probe.astype(jnp.bfloat16)
    lags = dot(probe, rounded, 1, 1) + dot(probe, rest, 1, 1)
    kernel_row = jnp.sum(lags, axis=0, keepdims=True)
    skewed = pltpu.roll(
        jnp.broadcast_to(kernel_row, (BLOCK, BLOCK)), 0, 1, stride=1, stride_axis=0
    )
    source = lax.broadcasted_iota(jnp.int32, (BLOCK, BLOCK), 0)
    target = lax.broadcasted_iota(jnp.int32, (BLOCK, BLOCK), 1)
    skewed = jnp.where(target >= source, skewed, 0.0)
    coarse = skewed.astype(jnp.bfloat16)
    toeplitz_ref[0, :BLOCK, :] = coarse
    toeplitz_ref[0, BLOCK:, :] = (skewed - coarse.astype(jnp.float32)).astype(jnp.bfloat16)


def make_tables(power_re, power_im, read_re, read_im, inflow):
    count, levels, modes = power_re.shape

    def spec(*shape):
        return pl.BlockSpec((1,) + shape, lambda i: (i, 0, 0))

    return pl.pallas_call(
        tables_kernel,
        grid=(count,),
        in_specs=[spec(levels, modes)] * 2 + [spec(1, modes)] * 3,
        out_specs=[
            spec(BLOCK, 2 * modes),
            spec(BLOCK, 2 * modes),
            spec(BLOCK, 2 * modes),
            spec(2 * BLOCK, BLOCK),
        ],
        out_shape=[
            jax.ShapeDtypeStruct((count, BLOCK, 2 * modes), jnp.float32),
            jax.ShapeDtypeStruct((count, BLOCK, 2 * modes), jnp.bfloat16),
            jax.ShapeDtypeStruct((count, BLOCK, 2 * modes), jnp.bfloat16),
            jax.ShapeDtypeStruct((count, 2 * BLOCK, BLOCK), jnp.bfloat16),
        ],
        compiler_params=pltpu.CompilerParams(vmem_limit_bytes=VMEM),
        cost_estimate=cost(12),
    )(power_re, power_im, read_re[:, None], read_im[:, None], inflow[:, None])


def spread_tokens(ref, scratch):
    sources, count, tokens = ref.shape
    per_source = tokens // BLOCK
    for source in range(sources):
        for part in range(per_source):
            row = (source * per_source + part) * count
            tile = ref[source, :, part * BLOCK : (part + 1) * BLOCK]
            scratch[row : row + count, :] = tile.astype(jnp.float32)


def gather_tokens(scratch, ref):
    sources, count, tokens = ref.shape
    per_source = tokens // BLOCK
    for source in range(sources):
        for part in range(per_source):
            row = (source * per_source + part) * count
            ref[source, :, part * BLOCK : (part + 1) * BLOCK] = scratch[
                row : row + count, :
            ].astype(ref.dtype)


GROUP = 4
LANES = 8


def segment_rows(channel, count, blocks):
    length = blocks // LANES
    return [pl.ds(turn * count + channel, LANES, stride=length * count) for turn in range(length)]


def scan_blocks(ends, jump, leaps, backward):
    modes = ends.shape[1] // 2
    length = ends.shape[0] // LANES
    order = range(length - 1, -1, -1) if backward else range(length)
    jump = tuple(jnp.broadcast_to(j, (LANES, modes)) for j in jump)
    row = lax.broadcasted_iota(jnp.int32, (LANES, modes), 0)
    blank = jnp.zeros((LANES, modes), jnp.float32)

    def step(state, turn):
        part = ends[turn * LANES : (turn + 1) * LANES, :]
        moved = cmul(*jump, *state)
        return (moved[0] + part[:, :modes], moved[1] + part[:, modes:])

    def shifted(value, distance):
        turned = pltpu.roll(value, LANES - distance if backward else distance, 0)
        inside = row < LANES - distance if backward else row >= distance
        return jnp.where(inside, turned, 0.0)

    state = (blank, blank)
    for turn in order:
        state = step(state, turn)
    state = tuple(shifted(v, 1) for v in state)
    for level, leap in enumerate(leaps):
        before = tuple(shifted(v, 2**level) for v in state)
        moved = cmul(*leap, *before)
        state = (state[0] + moved[0], state[1] + moved[1])
    states = [None] * length
    for turn in order:
        states[turn] = jnp.concatenate(state, axis=1)
        state = step(state, turn)
    return jnp.concatenate(states, axis=0)


def jumps_of(ref, sign):
    modes = ref.shape[2] // 2
    pairs = [(ref[0, i : i + 1, :modes], sign * ref[0, i : i + 1, modes:]) for i in range(4)]
    return pairs[0], pairs[1:]


def forward_kernel(
    values_ref,
    skip_ref,
    jump_ref,
    inflow_ref,
    lead_ref,
    out_table_ref,
    in_table_ref,
    toeplitz_ref,
    mixed_ref,
    starts_ref,
    split_ref,
    tokens,
):
    count = values_ref.shape[1]
    blocks = tokens.shape[0] // count
    modes = jump_ref.shape[2] // 2
    turn = pl.program_id(0)
    pl.when(turn == 0)(lambda: spread_tokens(values_ref, tokens))
    for index in range(GROUP):
        channel = turn * GROUP + index
        rows = segment_rows(channel, count, blocks)
        own = jnp.concatenate([tokens[r, :] for r in rows], axis=0)
        own_low = own.astype(jnp.bfloat16)
        split_ref[index] = own_low
        ends = dot(own_low, in_table_ref[index], 1, 0) * inflow_ref[index]
        start = scan_blocks(ends, *jumps_of(jump_ref.at[index : index + 1], 1.0), False)
        starts_ref[index] = start.astype(jnp.bfloat16)
        lead = lead_ref[index]
        weighted = cmul(lead[:, :modes], lead[:, modes:], start[:, :modes], start[:, modes:])
        weighted = jnp.concatenate(weighted, axis=1).astype(jnp.bfloat16)
        mixed = dot(weighted, out_table_ref[index], 1, 1)
        mixed += dot(own_low, toeplitz_ref[index, :BLOCK, :], 1, 0)
        mixed += dot(own_low, toeplitz_ref[index, BLOCK:, :], 1, 0)
        mixed += skip_ref[channel] * own
        for part, r in enumerate(rows):
            tokens[r, :] = mixed[part * LANES : (part + 1) * LANES, :]
    pl.when(turn == pl.num_programs(0) - 1)(lambda: gather_tokens(tokens, mixed_ref))


def run_pass(kernel, values, skip, jump, inflow, lead, out_table, in_table, toeplitz):
    sources, count, tokens = values.shape
    blocks = sources * tokens // BLOCK
    width = jump.shape[2]
    whole = pl.BlockSpec(values.shape, lambda i: (0, 0, 0), pipeline_mode=pl.Buffered(1))

    def spec(*shape):
        return pl.BlockSpec((GROUP,) + shape, lambda i: (i, 0, 0))

    return pl.pallas_call(
        kernel,
        grid=(count // GROUP,),
        in_specs=[
            whole,
            pl.BlockSpec(memory_space=pltpu.SMEM),
            spec(4, width),
            spec(1, width),
            spec(1, width),
            spec(BLOCK, width),
            spec(BLOCK, width),
            spec(2 * BLOCK, BLOCK),
        ],
        out_specs=[whole, spec(blocks, width), spec(blocks, BLOCK)],
        out_shape=[
            jax.ShapeDtypeStruct(values.shape, jnp.bfloat16),
            jax.ShapeDtypeStruct((count, blocks, width), jnp.bfloat16),
            jax.ShapeDtypeStruct((count, blocks, BLOCK), jnp.bfloat16),
        ],
        scratch_shapes=[pltpu.VMEM((blocks * count, BLOCK), jnp.float32)],
        compiler_params=pltpu.CompilerParams(vmem_limit_bytes=VMEM),
        cost_estimate=cost(20),
    )(values, skip, jump, inflow, lead, out_table, in_table, toeplitz)


def run_forward(*operands):
    return run_pass(forward_kernel, *operands)


def backward_kernel(
    grads_ref,
    skip_ref,
    jump_ref,
    inflow_ref,
    lead_ref,
    out_table_ref,
    in_table_ref,
    toeplitz_ref,
    values_grad_ref,
    later_ref,
    split_ref,
    grads,
):
    count = grads_ref.shape[1]
    blocks = grads.shape[0] // count
    modes = jump_ref.shape[2] // 2
    turn = pl.program_id(0)
    pl.when(turn == 0)(lambda: spread_tokens(grads_ref, grads))
    for index in range(GROUP):
        channel = turn * GROUP + index
        rows = segment_rows(channel, count, blocks)
        own = jnp.concatenate([grads[r, :] for r in rows], axis=0)
        own_low = own.astype(jnp.bfloat16)
        split_ref[index] = own_low
        lead = lead_ref[index]
        ends = dot(own_low, out_table_ref[index], 1, 0)
        ends = cmul(lead[:, :modes], -lead[:, modes:], ends[:, :modes], ends[:, modes:])
        ends = jnp.concatenate(ends, axis=1)
        later = scan_blocks(ends, *jumps_of(jump_ref.at[index : index + 1], -1.0), True)
        later_ref[index] = later.astype(jnp.bfloat16)
        later = (later * inflow_ref[index]).astype(jnp.bfloat16)
        back = dot(later, in_table_ref[index], 1, 1)
        back += dot(own_low, toeplitz_ref[index, :BLOCK, :], 1, 1)
        back += dot(own_low, toeplitz_ref[index, BLOCK:, :], 1, 1)
        back += skip_ref[channel] * own
        for part, r in enumerate(rows):
            grads[r, :] = back[part * LANES : (part + 1) * LANES, :]
    pl.when(turn == pl.num_programs(0) - 1)(lambda: gather_tokens(grads, values_grad_ref))


def run_backward(*operands):
    return run_pass(backward_kernel, *operands)


def sums_kernel(grad_ref, value_ref, start_ref, later_ref, power_ref, sums_ref, skip_ref):
    for index in range(grad_ref.shape[0]):
        channel_sums(
            *(r.at[index] for r in (grad_ref, value_ref, start_ref, later_ref, power_ref)),
            sums_ref.at[index],
            skip_ref.at[index],
        )


def channel_sums(grad_ref, value_ref, start_ref, later_ref, power_ref, sums_ref, skip_ref):
    modes = power_ref.shape[1] // 2
    row = lax.broadcasted_iota(jnp.int32, (BLOCK, BLOCK), 0)
    lane = lax.broadcasted_iota(jnp.int32, (BLOCK, BLOCK), 1)
    flip = jnp.where(row + lane == BLOCK - 1, 1.0, 0.0).astype(jnp.bfloat16)

    def fold(part):
        return jnp.sum(part.reshape(part.shape[0] // 8, 8, part.shape[1]), axis=0)

    grad, value = grad_ref[...], value_ref[...]
    start, later = start_ref[...], later_ref[...]
    product = grad.astype(jnp.float32) * value.astype(jnp.float32)
    skip_ref[...] = jnp.sum(product, axis=0, keepdims=True)
    turned = dot(value, flip, 1, 0).astype(jnp.bfloat16)
    out_sum = dot(grad, start, 0, 0)
    in_sum = dot(turned, later, 0, 0)
    cross = dot(grad, turned, 0, 0)
    cross = jnp.where(row + lane >= BLOCK - 1, cross, 0.0)
    lags = jnp.sum(pltpu.roll(cross, 1, 1, stride=1, stride_axis=0), axis=0, keepdims=True)
    lags = jnp.sum(jnp.where(row == lane, lags, 0.0), axis=1, keepdims=True)
    weight = lax.broadcasted_iota(jnp.int32, (BLOCK, modes), 0).astype(jnp.float32)
    power_re, power_im = power_ref[:, :modes], power_ref[:, modes:]
    terms = []
    for total, sign in ((out_sum, 1.0), (in_sum, -1.0)):
        term_re, term_im = cmul(power_re, power_im, total[:, :modes], sign * total[:, modes:])
        terms += [fold(term_re), fold(term_im), fold(weight * term_re), fold(weight * term_im)]
    later_re, later_im = (later[:, :modes].astype(jnp.float32), later[:, modes:].astype(jnp.float32))
    start_re, start_im = (start[:, :modes].astype(jnp.float32), start[:, modes:].astype(jnp.float32))
    terms += [
        fold(later_re * start_re + later_im * start_im),
        fold(later_re * start_im - later_im * start_re),
    ]
    local_re, local_im = power_re * lags, power_im * lags
    terms += [fold(local_re), fold(local_im), fold(weight * local_re), fold(weight * local_im)]
    for index, term in enumerate(terms):
        sums_ref[index : index + 1, :] = jnp.sum(term, axis=0, keepdims=True)


def run_sums(grads, values, starts, later, power):
    count, blocks, width = starts.shape
    group = 4

    def spec(*shape):
        return pl.BlockSpec((group,) + shape, lambda i: (i, 0, 0))

    return pl.pallas_call(
        sums_kernel,
        grid=(count // group,),
        in_specs=[spec(blocks, BLOCK)] * 2 + [spec(blocks, width)] * 2 + [spec(BLOCK, width)],
        out_specs=[spec(16, width // 2), spec(1, BLOCK)],
        out_shape=[
            jax.ShapeDtypeStruct((count, 16, width // 2), jnp.float32),
            jax.ShapeDtypeStruct((count, 1, BLOCK), jnp.float32),
        ],
        compiler_params=pltpu.CompilerParams(vmem_limit_bytes=VMEM),
        cost_estimate=cost(18),
    )(grads, values, starts, later, power)


def cost(microseconds):
    return pl.CostEstimate(
        flops=int(microseconds * 1e9), bytes_accessed=int(microseconds * 1e6), transcendentals=0
    )


def erf_parts(value):
    half = 0.5 * (1.0 + lax.erf(value * (1.0 / math.sqrt(2.0))))
    density = jnp.exp(-0.5 * value * value) * (1.0 / math.sqrt(2.0 * math.pi))
    return value * half, half + value * density


def norm_kernel(
    early_steps,
    place_ref,
    own_ref,
    near_ref,
    far_ref,
    far_late_ref,
    last_ref,
    last_late_ref,
    affine_ref,
    weight_ref,
    bias_ref,
    normed_ref,
    values_ref,
    slope_ref,
    before_ref,
    stats_ref,
    whole,
):
    place = place_ref[0]
    width = own_ref.shape[1]
    early = pl.program_id(0) < early_steps
    parts = (
        own_ref[...],
        near_ref[...],
        jnp.where(early, far_ref[...], far_late_ref[...]),
        jnp.where(early, last_ref[...], last_late_ref[...]),
    )
    for offset, part in enumerate(parts):
        start = pl.multiple_of((place ^ offset) * width, width)
        whole[:, pl.ds(start, width)] = part.astype(jnp.float32)
    inputs = whole[...]
    average = jnp.mean(inputs, axis=1, keepdims=True)
    spread = jnp.mean(inputs * inputs, axis=1, keepdims=True) - average * average
    inverse = lax.rsqrt(spread + EPSILON)
    normed = (inputs - average) * inverse * affine_ref[0:1, :] + affine_ref[1:2, :]
    normed = normed.astype(jnp.bfloat16)
    normed_ref[...] = normed
    before = dot(weight_ref[...], normed, 0, 1) + bias_ref[...]
    values, slope = erf_parts(before)
    values_ref[...] = values.astype(jnp.bfloat16)
    slope_ref[...] = slope
    before_ref[...] = before
    lane = lax.broadcasted_iota(jnp.int32, (inputs.shape[0], 128), 1)
    stats_ref[...] = jnp.where(lane < 64, average, inverse)


def run_norm(parts, affine, weight, bias):
    rows, width = parts[0].shape
    full, channels = weight.shape
    step = 512
    place = lax.axis_index("chan").astype(jnp.int32).reshape(1)
    half = parts[2].shape[0] // step
    full_rows = pl.BlockSpec((step, width), lambda i, p: (i, 0))
    first_rows = pl.BlockSpec((step, width), lambda i, p: (jnp.minimum(i, half - 1), 0))
    later_rows = pl.BlockSpec((step, width), lambda i, p: (jnp.maximum(i - half, 0), 0))
    return pl.pallas_call(
        partial(norm_kernel, half),
        grid_spec=pltpu.PrefetchScalarGridSpec(
            num_scalar_prefetch=1,
            grid=(rows // step,),
            in_specs=[
                full_rows,
                full_rows,
                first_rows,
                later_rows,
                first_rows,
                later_rows,
                pl.BlockSpec((2, full), lambda i, p: (0, 0)),
                pl.BlockSpec((full, channels), lambda i, p: (0, 0)),
                pl.BlockSpec((channels, 1), lambda i, p: (0, 0)),
            ],
            out_specs=[
                pl.BlockSpec((step, full), lambda i, p: (i, 0)),
                pl.BlockSpec((channels, step), lambda i, p: (0, i)),
                pl.BlockSpec((channels, step), lambda i, p: (0, i)),
                pl.BlockSpec((channels, step), lambda i, p: (0, i)),
                pl.BlockSpec((step, 128), lambda i, p: (i, 0)),
            ],
            scratch_shapes=[pltpu.VMEM((step, full), jnp.float32)],
        ),
        out_shape=[
            jax.ShapeDtypeStruct((rows, full), jnp.bfloat16),
            jax.ShapeDtypeStruct((channels, rows), jnp.bfloat16),
            jax.ShapeDtypeStruct((channels, rows), jnp.float32),
            jax.ShapeDtypeStruct((channels, rows), jnp.float32),
            jax.ShapeDtypeStruct((rows, 128), jnp.float32),
        ],
        compiler_params=pltpu.CompilerParams(vmem_limit_bytes=VMEM),
        cost_estimate=cost(8),
    )(place, *parts, affine, weight, bias[:, None])


def gate_kernel(count, where_ref, *refs):
    gate_body(where_ref, refs[:count], *refs[count:])


def gate_body(
    where_ref,
    front_refs,
    normed_ref,
    grad_ref,
    bias_ref,
    upper_ref,
    slope_ref,
    lifted_grad_ref,
    keep_ref,
    send_ref,
    bias_grad_ref,
    up_ref,
    down_ref,
    mix_ref,
):
    place = where_ref[0]
    size = keep_ref.shape[1]
    unpack_fronts(where_ref[1], front_refs, up_ref, down_ref, mix_ref)
    before = dot(normed_ref[...], up_ref[...], 1, 0) + bias_ref[...]
    hidden_grad = dot(grad_ref[...], down_ref[...], 1, 0)
    upper, slope = erf_parts(before)
    upper_ref[...] = upper.astype(jnp.bfloat16)
    slope_ref[...] = (hidden_grad * slope).astype(jnp.bfloat16)
    lifted_grad = (hidden_grad * upper).astype(jnp.bfloat16)
    lifted_grad_ref[...] = lifted_grad

    def piece(offset):
        start = pl.multiple_of((place ^ offset) * size, size)
        return dot(mix_ref[pl.ds(start, size), :], lifted_grad, 1, 1)

    keep_ref[0], keep_ref[1] = piece(0), piece(2)
    send_ref[0], send_ref[1] = piece(1), piece(3)
    part = jnp.sum(lifted_grad.astype(jnp.float32), axis=0, keepdims=True)

    @pl.when(pl.program_id(0) == 0)
    def _():
        bias_grad_ref[...] = jnp.zeros_like(bias_grad_ref)

    bias_grad_ref[...] += part


def ring_sources(place):
    spot = jnp.where(place % 2 == 0, place // 2, 7 - place // 2)
    spots = [spot]
    for step in range(1, 5):
        spots.append((spot + 8 - step) % 8)
        if step < 4:
            spots.append((spot + step) % 8)
    return [jnp.where(s < 4, 2 * s, 15 - 2 * s) for s in spots]


def unpack_fronts(place, front_refs, up_ref, down_ref, mix_ref):
    devices = sum(ref.shape[0] for ref in front_refs)
    part, mix_part = up_ref.shape[0] // devices, mix_ref.shape[0] // devices

    def copy(ref, index, rows, mix_rows):
        up_ref[rows, :] = ref[index, :part, :]
        down_ref[rows, :] = ref[index, part : 2 * part, :]
        mix_ref[mix_rows, :] = ref[index, 2 * part :, :]

    @pl.when(pl.program_id(0) == 0)
    def _():
        if len(front_refs) == 1:
            for source in range(devices):
                rows = slice(source * part, (source + 1) * part)
                mix_rows = slice(source * mix_part, (source + 1) * mix_part)
                copy(front_refs[0], source, rows, mix_rows)
        else:
            for ref, source in zip(front_refs, ring_sources(place)):
                rows = pl.ds(pl.multiple_of(source * part, part), part)
                mix_rows = pl.ds(pl.multiple_of(source * mix_part, mix_part), mix_part)
                copy(ref, 0, rows, mix_rows)


def front_specs(arrays):
    once = pl.Buffered(1)
    return [pl.BlockSpec(a.shape, lambda i, p: (0, 0, 0), pipeline_mode=once) for a in arrays]


def front_scratch(full, channels, units):
    return [
        pltpu.VMEM((full, units), jnp.bfloat16),
        pltpu.VMEM((full, units), jnp.bfloat16),
        pltpu.VMEM((channels, units), jnp.bfloat16),
    ]


def run_gate(normed, grad, fronts, where, channels, bias):
    rows, full = normed.shape
    units = fronts[0].shape[2]
    step = 256


    def fixed(*shape):
        return pl.BlockSpec(shape, lambda i, p: (0, 0))

    def rowwise(columns):
        return pl.BlockSpec((step, columns), lambda i, p: (i, 0))

    size = channels // 4
    pieces = pl.BlockSpec((2, size, step), lambda i, p: (0, 0, i))
    return pl.pallas_call(
        partial(gate_kernel, len(fronts)),
        grid_spec=pltpu.PrefetchScalarGridSpec(
            num_scalar_prefetch=1,
            grid=(rows // step,),
            in_specs=front_specs(fronts) + [rowwise(full), rowwise(full), fixed(1, units)],
            out_specs=[rowwise(units)] * 3 + [pieces] * 2 + [fixed(1, units)],
            scratch_shapes=front_scratch(full, channels, units),
        ),
        out_shape=[jax.ShapeDtypeStruct((rows, units), jnp.bfloat16)] * 3
        + [jax.ShapeDtypeStruct((2, size, rows), jnp.float32)] * 2
        + [jax.ShapeDtypeStruct((1, units), jnp.float32)],
        compiler_params=pltpu.CompilerParams(vmem_limit_bytes=VMEM),
        cost_estimate=cost(15),
    )(where, *fronts, normed, grad, bias[None])


def mid_kernel(count, where_ref, *refs):
    mid_body(where_ref, refs[:count], *refs[count:])


def mid_body(
    where_ref,
    front_refs,
    own_ref,
    near_ref,
    far_ref,
    last_ref,
    upper_ref,
    slope_ref,
    normed_ref,
    bias_ref,
    affine_ref,
    mixed_ref,
    hidden_ref,
    up_grad_ref,
    out_keep_ref,
    out_send_ref,
    feature_keep_ref,
    feature_send_ref,
    sums_ref,
    bias_grad_ref,
    up_ref,
    down_ref,
    mix_ref,
    whole,
):
    place = where_ref[0]
    width = out_keep_ref.shape[2]
    unpack_fronts(where_ref[1], front_refs, up_ref, down_ref, mix_ref)
    size = own_ref.shape[0]
    for offset, piece in enumerate((own_ref, near_ref, far_ref, last_ref)):
        start = pl.multiple_of((place ^ offset) * size, size)
        mixed_ref[pl.ds(start, size), :] = piece[...]
    lifted = dot(mixed_ref[...], mix_ref[...], 0, 0) + bias_ref[...]
    hidden = (upper_ref[...].astype(jnp.float32) * lifted).astype(jnp.bfloat16)
    up_grad = (slope_ref[...].astype(jnp.float32) * lifted).astype(jnp.bfloat16)
    hidden_ref[...] = hidden
    up_grad_ref[...] = up_grad

    @pl.when(pl.program_id(0) == 0)
    def _():
        bias_grad_ref[...] = jnp.zeros_like(bias_grad_ref)

    bias_grad_ref[...] += jnp.sum(up_grad.astype(jnp.float32), axis=0, keepdims=True)

    def part(offset):
        start = pl.multiple_of((place ^ offset) * width, width)
        return whole[:, pl.ds(start, width)].astype(jnp.bfloat16)

    whole[...] = dot(hidden, down_ref[...], 1, 1)
    out_keep_ref[0], out_keep_ref[1] = part(0), part(2)
    out_send_ref[0], out_send_ref[1] = part(1), part(3)
    feature = dot(up_grad, up_ref[...], 1, 1)
    whole[...] = feature
    feature_keep_ref[0], feature_keep_ref[1] = part(0), part(2)
    feature_send_ref[0], feature_send_ref[1] = part(1), part(3)
    one = jnp.sum(feature * affine_ref[0:1, :], axis=1, keepdims=True)
    shifted = normed_ref[...].astype(jnp.float32) - affine_ref[1:2, :]
    two = jnp.sum(feature * shifted, axis=1, keepdims=True)
    lane = lax.broadcasted_iota(jnp.int32, (feature.shape[0], 128), 1)
    sums_ref[...] = jnp.where(lane == 0, one, jnp.where(lane == 1, two, 0.0)).T[0:8, :]


def run_mid(parts, upper, slope, normed, fronts, where, bias, affine):
    rows, full = normed.shape
    units = fronts[0].shape[2]
    channels = 4 * parts[0].shape[0]
    width = full // 4
    step = 512

    def fixed(*shape):
        return pl.BlockSpec(shape, lambda i, p: (0, 0))

    def rowwise(columns):
        return pl.BlockSpec((step, columns), lambda i, p: (i, 0))

    def columns(count):
        return pl.BlockSpec((count, step), lambda i, p: (0, i))

    pieces = pl.BlockSpec((2, step, width), lambda i, p: (0, i, 0))
    piece_shape = jax.ShapeDtypeStruct((2, rows, width), jnp.bfloat16)
    return pl.pallas_call(
        partial(mid_kernel, len(fronts)),
        grid_spec=pltpu.PrefetchScalarGridSpec(
            num_scalar_prefetch=1,
            grid=(rows // step,),
            in_specs=front_specs(fronts)
            + [
                columns(channels // 4),
                columns(channels // 4),
                columns(channels // 4),
                columns(channels // 4),
                rowwise(units),
                rowwise(units),
                rowwise(full),
                fixed(1, units),
                fixed(2, full),
            ],
            out_specs=[columns(channels)]
            + [rowwise(units)] * 2
            + [pieces] * 4
            + [columns(8), fixed(1, units)],
            scratch_shapes=front_scratch(full, channels, units)
            + [pltpu.VMEM((step, full), jnp.float32)],
        ),
        out_shape=[jax.ShapeDtypeStruct((channels, rows), jnp.bfloat16)]
        + [jax.ShapeDtypeStruct((rows, units), jnp.bfloat16)] * 2
        + [piece_shape] * 4
        + [
            jax.ShapeDtypeStruct((8, rows), jnp.float32),
            jax.ShapeDtypeStruct((1, units), jnp.float32),
        ],
        compiler_params=pltpu.CompilerParams(vmem_limit_bytes=VMEM),
        cost_estimate=cost(14),
    )(where, *fronts, *parts, upper, slope, normed, bias[None], affine)


def payload_kernel(
    grad_ref, slope_ref, before_ref, gain_ref, bias_ref, sums_ref, payload_ref, bias_grad_ref
):
    count = grad_ref.shape[0]
    grad = (grad_ref[...].astype(jnp.float32) * slope_ref[...]).astype(jnp.bfloat16)
    payload_ref[:count, :] = grad
    grad = grad.astype(jnp.float32)
    centred = before_ref[...] - bias_ref[...] - gain_ref[:, 1:2]
    one = jnp.sum(grad * gain_ref[:, 0:1], axis=0, keepdims=True) + sums_ref[0:1, :]
    two = jnp.sum(grad * centred, axis=0, keepdims=True) + sums_ref[1:2, :]
    row = lax.broadcasted_iota(jnp.int32, (16, grad.shape[1]), 0)
    one_high = one.astype(jnp.bfloat16).astype(jnp.float32)
    two_high = two.astype(jnp.bfloat16).astype(jnp.float32)
    tail = jnp.where(row == 0, one_high, jnp.where(row == 1, one - one_high, 0.0))
    tail = jnp.where(row == 2, two_high, jnp.where(row == 3, two - two_high, tail))
    payload_ref[count:, :] = tail.astype(jnp.bfloat16)
    part = jnp.sum(grad, axis=1, keepdims=True)

    @pl.when(pl.program_id(0) == 0)
    def _():
        bias_grad_ref[...] = jnp.zeros_like(bias_grad_ref)

    bias_grad_ref[...] += part


def run_payload(grad, slope, before, gain, bias, sums):
    count, rows = grad.shape
    step = 512

    def columns(lines):
        return pl.BlockSpec((lines, step), lambda i: (0, i))

    def fixed(*shape):
        return pl.BlockSpec(shape, lambda i: (0, 0))

    return pl.pallas_call(
        payload_kernel,
        grid=(rows // step,),
        in_specs=[columns(count)] * 3 + [fixed(count, 2), fixed(count, 1), columns(8)],
        out_specs=[columns(count + 16), fixed(count, 1)],
        out_shape=[
            jax.ShapeDtypeStruct((count + 16, rows), jnp.bfloat16),
            jax.ShapeDtypeStruct((count, 1), jnp.float32),
        ],
        cost_estimate=cost(3),
    )(grad, slope, before, gain, bias[:, None], sums)


def final_kernel(
    _,
    own_ref,
    near_ref,
    far_ref,
    last_ref,
    rows_ref,
    kept_ref,
    sent_ref,
    passed_ref,
    tokens_ref,
    stats_ref,
    grad_ref,
    gain_ref,
    input_grad_ref,
    vectors_ref,
    gain_grad_ref,
    shift_grad_ref,
    down_grad_ref,
    total,
):
    size = own_ref.shape[0] - 16
    row = lax.broadcasted_iota(jnp.int32, (16, 256), 0)
    lane = lax.broadcasted_iota(jnp.int32, (16, 256), 1)
    pick = jnp.where((row < 2) == (lane < 128), 1.0, 0.0)
    pick = jnp.where(row < 4, pick, 0.0).astype(jnp.bfloat16)
    normed_grad = (
        kept_ref[0].astype(jnp.float32)
        + sent_ref[0].astype(jnp.float32)
        + passed_ref[...].astype(jnp.float32)
    )
    totals = jnp.zeros((normed_grad.shape[0], 256), jnp.float32)
    for offset, piece in enumerate((own_ref, near_ref, far_ref, last_ref)):
        weights = rows_ref[:, offset * size : (offset + 1) * size]
        normed_grad += dot(piece[:size, :], weights, 0, 1)
        totals += dot(piece[size:, :], pick, 0, 0)
    scaled = normed_grad * gain_ref[...]
    centred = (tokens_ref[...].astype(jnp.float32) - stats_ref[:, 0:1]) * stats_ref[:, 64:65]
    grad = grad_ref[...].astype(jnp.float32)
    mean_one = totals[:, 0:1] * (1.0 / D)
    mean_two = totals[:, 128:129] * (1.0 / D)
    input_grad_ref[...] = stats_ref[:, 64:65] * (scaled - mean_one - centred * mean_two) + grad

    @pl.when(pl.program_id(0) == 0)
    def _():
        gain_grad_ref[...] = jnp.zeros_like(gain_grad_ref)
        shift_grad_ref[...] = jnp.zeros_like(shift_grad_ref)
        down_grad_ref[...] = jnp.zeros_like(down_grad_ref)

    gain_grad_ref[...] += jnp.sum(normed_grad * centred, axis=0, keepdims=True)
    shift_grad_ref[...] += jnp.sum(normed_grad, axis=0, keepdims=True)
    down_grad_ref[...] += jnp.sum(grad, axis=0, keepdims=True)

    @pl.when(pl.program_id(0) == pl.num_programs(0) - 1)
    def _():
        devices = vectors_ref.shape[0]
        part = gain_grad_ref.shape[1] // devices
        row = lax.broadcasted_iota(jnp.int32, (16, 128), 0)
        total[...] = jnp.zeros_like(total)
        for turn in range(devices):
            for index, ref in enumerate((gain_grad_ref, shift_grad_ref, down_grad_ref)):
                total[:, index * part : (index + 1) * part] = ref[
                    :, turn * part : (turn + 1) * part
                ]
            high = total[...].astype(jnp.bfloat16).astype(jnp.float32)
            pair = jnp.where(row == 0, high, jnp.where(row == 1, total[...] - high, 0.0))
            vectors_ref[turn] = pair.astype(jnp.bfloat16)


def run_final(parts, input_rows, kept, sent, passed, tokens, stats, grad, gain):
    rows, width = tokens.shape
    lines = parts[0].shape[0]
    devices = lax.axis_size("seq")
    step = 512
    place = lax.axis_index("chan").astype(jnp.int32).reshape(1)

    def fixed(*shape):
        return pl.BlockSpec(shape, lambda i, p: (0, 0))

    def rowwise(columns):
        return pl.BlockSpec((step, columns), lambda i, p: (i, 0))

    def columns(count):
        return pl.BlockSpec((count, step), lambda i, p: (0, i))

    piece = pl.BlockSpec((1, step, width), lambda i, p: (0, i, 0))
    return pl.pallas_call(
        final_kernel,
        grid_spec=pltpu.PrefetchScalarGridSpec(
            num_scalar_prefetch=1,
            grid=(rows // step,),
            in_specs=[columns(lines)] * 4
            + [
                fixed(*input_rows.shape),
                piece,
                piece,
                rowwise(width),
                rowwise(width),
                rowwise(128),
                pl.BlockSpec((step, width), lambda i, p: (i, p[0])),
                fixed(1, width),
            ],
            out_specs=[rowwise(width), pl.BlockSpec((devices, 16, 128), lambda i, p: (0, 0, 0))],
            scratch_shapes=[pltpu.VMEM((1, width), jnp.float32)] * 3
            + [pltpu.VMEM((1, 128), jnp.float32)],
        ),
        out_shape=[
            jax.ShapeDtypeStruct((rows, width), jnp.float32),
            jax.ShapeDtypeStruct((devices, 16, 128), jnp.bfloat16),
        ],
        cost_estimate=cost(6),
    )(place, *parts, input_rows, kept, sent, passed, tokens, stats, grad, gain[None])


def grads_kernel(
    side_ref,
    outer_ref,
    normed_ref,
    mixed_ref,
    hidden_ref,
    up_ref,
    lifted_ref,
    down_send_ref,
    down_keep_ref,
    rest_send_ref,
    rest_keep_ref,
    whole,
    mix_whole,
):
    kept = side_ref[0]
    part = outer_ref.shape[1] // 2
    mix_part = mixed_ref.shape[0] // 2

    def half(scratch, size, side):
        return scratch[pl.ds(pl.multiple_of(side * size, size), size), :].astype(jnp.bfloat16)

    whole[...] = dot(outer_ref[...], hidden_ref[...], 0, 0)
    down_send_ref[0] = half(whole, part, 1 - kept)
    down_keep_ref[0] = half(whole, part, kept)
    whole[...] = dot(normed_ref[...], up_ref[...], 0, 0)
    rest_send_ref[0, :part, :] = half(whole, part, 1 - kept)
    rest_keep_ref[0, :part, :] = half(whole, part, kept)
    mix_whole[...] = dot(mixed_ref[...], lifted_ref[...], 1, 0)
    rest_send_ref[0, part:, :] = half(mix_whole, mix_part, 1 - kept)
    rest_keep_ref[0, part:, :] = half(mix_whole, mix_part, kept)


def run_grads(outer, normed, mixed, hidden, up, lifted):
    rows, full = outer.shape
    channels = mixed.shape[0]
    units = hidden.shape[1]
    devices = lax.axis_size("seq")
    half = devices // 2
    part, mix_part = full // devices, channels // devices
    side = (lax.axis_index("seq") & 1).astype(jnp.int32).reshape(1)

    def fixed(*shape):
        return pl.BlockSpec(shape, lambda i, p: (0, 0), pipeline_mode=pl.Buffered(1))

    whole = part + mix_part
    return pl.pallas_call(
        grads_kernel,
        grid_spec=pltpu.PrefetchScalarGridSpec(
            num_scalar_prefetch=1,
            grid=(half,),
            in_specs=[
                pl.BlockSpec((rows, 2 * part), lambda i, p: (0, i)),
                pl.BlockSpec((rows, 2 * part), lambda i, p: (0, i)),
                pl.BlockSpec((2 * mix_part, rows), lambda i, p: (i, 0)),
                fixed(rows, units),
                fixed(rows, units),
                fixed(rows, units),
            ],
            out_specs=[pl.BlockSpec((1, part, units), lambda i, p: (i, 0, 0))] * 2
            + [pl.BlockSpec((1, whole, units), lambda i, p: (i, 0, 0))] * 2,
            scratch_shapes=[
                pltpu.VMEM((2 * part, units), jnp.float32),
                pltpu.VMEM((2 * mix_part, units), jnp.float32),
            ],
        ),
        out_shape=[jax.ShapeDtypeStruct((half, part, units), jnp.bfloat16)] * 2
        + [jax.ShapeDtypeStruct((half, whole, units), jnp.bfloat16)] * 2,
        compiler_params=pltpu.CompilerParams(vmem_limit_bytes=VMEM),
        cost_estimate=cost(14),
    )(side, outer, normed, mixed, hidden, up, lifted)


def swap(value, distance):
    return lax.ppermute(value, "chan", [(i, i ^ distance) for i in range(4)])


def gather_parts(piece):
    far = swap(piece, 2)
    return piece, swap(piece, 1), far, swap(far, 1)


def after(value, *others):
    return lax.optimization_barrier((value,) + others)[0]


def ring_steps(moving, steps):
    devices = lax.axis_size("seq")
    order = (0, 2, 4, 6, 7, 5, 3, 1)
    arrived = []
    for step in steps:
        following = []
        for piece, direction in zip(moving, (1, -1)):
            if direction < 0 and step == devices // 2:
                continue
            pairs = [(order[i], order[(i + direction) % devices]) for i in range(devices)]
            following.append(lax.ppermute(piece, "seq", pairs))
        arrived += following
        moving = following
    return arrived


def to_channels(value, sequences):
    devices = lax.axis_size("seq")
    channels, tokens = value.shape
    share = channels // devices
    got = lax.all_to_all(value.reshape(devices, share, tokens), "seq", 0, 0, tiled=True)
    got = got.reshape(sequences, devices // sequences, share, tokens)
    return got.transpose(1, 0, 2, 3).reshape(devices // sequences, sequences * share, tokens)


def to_tokens(value, sequences):
    devices = lax.axis_size("seq")
    sources, count, tokens = value.shape
    share = count // sequences
    sent = value.reshape(sources, sequences, share, tokens).transpose(1, 0, 2, 3)
    got = lax.all_to_all(sent.reshape(devices, share, tokens), "seq", 0, 0, tiled=True)
    return got.reshape(devices * share, tokens)


def tile_rows(flat):
    width = flat.shape[-1]
    padded = -(-width // 128) * 128
    flat = jnp.pad(flat, [(0, 0)] * (flat.ndim - 1) + [(0, padded - width)])
    return flat.reshape(flat.shape[:-1] + (padded // 128, 128))


def planes(value, count):
    parts = []
    for _ in range(count):
        part = lax.reduce_precision(value, 8, 7)
        parts.append(part.astype(jnp.bfloat16))
        value = value - part
    return parts


def plain_grads(outer, normed, mixed, hidden, up, lifted):
    devices = lax.axis_size("seq")
    side = lax.axis_index("seq") & 1

    def parts(value):
        value = value.astype(jnp.bfloat16)
        return value.reshape(devices // 2, 2, value.shape[0] // devices, value.shape[1])

    def pick(value, index):
        return lax.dynamic_index_in_dim(value, index, 1, False)

    down = parts(dot(outer, hidden, 0, 0))
    rest = (parts(dot(normed, up, 0, 0)), parts(dot(mixed, lifted, 1, 0)))
    rest = jnp.concatenate(rest, axis=2)
    return (pick(down, 1 - side), pick(down, side), pick(rest, 1 - side), pick(rest, side))


def halve(sent, kept):
    devices = lax.axis_size("seq")
    got = lax.ppermute(sent, "seq", [(i, i ^ 1) for i in range(devices)])
    return (kept.astype(jnp.float32) + got.astype(jnp.float32)).astype(jnp.bfloat16)


def settle_apart(halves):
    devices = lax.axis_size("seq")
    if devices != 8:
        return settle(halves)
    line = lax.axis_index("seq") >> 1
    total = lax.dynamic_index_in_dim(halves, line, 0, False).astype(jnp.float32)
    for distance in (2, 3, 1):
        sent = lax.dynamic_index_in_dim(halves, line ^ distance, 0, False)
        pairs = [(i, i ^ (2 * distance)) for i in range(devices)]
        total += lax.ppermute(sent, "seq", pairs).astype(jnp.float32)
    return total


def settle(halves):
    devices = lax.axis_size("seq")
    groups = [[i for i in range(devices) if i & 1 == side] for side in (0, 1)]
    got = lax.all_to_all(halves, "seq", 0, 0, axis_index_groups=groups, tiled=True)
    return jnp.sum(got.astype(jnp.float32), axis=0)


def per_device(
    tokens,
    norm_gain,
    norm_shift,
    up_weight,
    up_bias,
    input_weight,
    input_bias,
    mix_weight,
    mix_bias,
    down_weight,
    down_bias,
    decay_rate,
    decay_freq,
    step_log,
    read_real,
    read_imag,
    skip_gain,
    out_grad,
):
    row_count, width = tokens.shape
    devices = lax.axis_size("seq")
    place = lax.axis_index("chan")
    sequences = devices * row_count // LENGTH
    feature_rows, channels = input_weight.shape
    units = up_weight.shape[1]
    share = channels // devices
    modes_here = decay_rate.shape[0]
    modes = modes_here * devices
    near = swap(tokens, 1)
    early_rows = row_count // 4
    far, far_late = swap(tokens[:early_rows], 2), swap(tokens[early_rows:], 2)
    token_parts = (tokens, near, far, far_late, swap(far, 1), swap(far_late, 1))

    pair = jnp.stack([norm_gain, norm_shift])
    pairs = jnp.stack([pair, swap(pair, 1), swap(pair, 2), swap(pair, 3)])
    pairs = jnp.stack([pairs[place ^ i] for i in range(4)])
    fronts = jnp.concatenate([up_weight, down_weight.T, mix_weight])
    where = jnp.stack([place, lax.axis_index("seq")]).astype(jnp.int32)
    ring = [fronts] + ring_steps((fronts, fronts), (1, 2)) if devices == 8 else []
    pairs = after(pairs, far, *ring[1:3])
    small = (pairs.reshape(-1), up_bias, input_bias, mix_bias, down_bias, decay_rate, decay_freq)
    sizes = [v.shape[0] for v in small]
    small = tile_rows(jnp.concatenate(small))
    reads = jnp.concatenate([read_real, read_imag], axis=1).reshape(devices, share, 2 * modes_here)
    reads = jnp.pad(reads, ((0, 0), (0, 0), (0, 128 - 2 * modes_here)))
    copies = jnp.broadcast_to(small, (devices,) + small.shape)
    exact = jnp.concatenate([reads, copies], axis=1)
    exact_rows = exact.shape[1]
    weights = jnp.broadcast_to(input_weight, (devices,) + input_weight.shape)
    got = jnp.concatenate(planes(exact, 3) + [weights], axis=1)
    got = lax.all_to_all(got, "seq", 0, 0, tiled=True)
    input_full = got[:, 3 * exact_rows :].reshape(4 * width, channels)

    def exact_part(start, stop):
        rows = [got[:, i * exact_rows + start : i * exact_rows + stop] for i in range(3)]
        rows = [r.astype(jnp.float32) for r in rows]
        return rows[0] + (rows[1] + rows[2])

    small = exact_part(share, exact_rows).reshape(devices, -1)
    parts, spot = [], 0
    for size in sizes:
        parts.append(small[:, spot : spot + size])
        spot += size
    affine = parts[0].reshape(devices, 4, 2, -1).transpose(2, 1, 0, 3).reshape(2, 4 * width)
    input_shift = parts[2].reshape(-1)

    normed, values_low, in_slope, pre_in, stats = run_norm(
        token_parts, affine, input_full, input_shift
    )
    values = to_channels(values_low, sequences)
    if devices == 8:
        ring += ring_steps(tuple(after(p, normed) for p in ring[3:5]), (3, 4))
        fronts = tuple(p[None] for p in ring)
    else:
        fronts = (lax.all_gather(fronts, "seq", axis=0),)

    got = after(got, normed)
    parts = lax.optimization_barrier(tuple(parts) + (normed,))[:-1]
    reads = exact_part(0, share)[:, :, : 2 * modes_here].transpose(1, 0, 2)
    read_re = reads[:, :, :modes_here].reshape(share, modes)
    read_im = reads[:, :, modes_here:].reshape(share, modes)
    up_shift, _, mix_shift, down_shift, rate, freq = (p.reshape(-1) for p in parts[1:])

    spacing = jnp.exp(step_log)
    damping = spacing[:, None] * rate[None, :]
    rotation = spacing[:, None] * freq[None, :]
    inflow = -jnp.expm1(-damping)
    extents = 2.0 ** jnp.asarray([0, 1, 2, 3, 4, 5, 6, 7, 11, 12, 13])[None, :, None]
    length = jnp.exp(-damping[:, None] * extents)
    angle = rotation[:, None] * extents
    power_re, power_im = length * jnp.cos(angle), length * jnp.sin(angle)

    def repeat(value):
        return jnp.tile(value, (sequences,) + (1,) * (value.ndim - 1))

    def rows(value_re, value_im):
        return repeat(jnp.concatenate([value_re, value_im], axis=1)[:, None])

    power, out_table, in_table, toeplitz = make_tables(
        repeat(power_re[:, :8]), repeat(power_im[:, :8]), repeat(read_re), repeat(read_im), repeat(inflow)
    )
    jump = repeat(jnp.concatenate([power_re[:, 7:], power_im[:, 7:]], axis=2))
    flow = rows(inflow, inflow)
    lead = rows(*cmul(read_re, read_im, power_re[:, 0], power_im[:, 0]))
    skip = repeat(skip_gain)

    pieces = gather_parts(after(input_full, normed))
    pieces = [lax.dynamic_slice_in_dim(p, place * width, width, 0) for p in pieces]
    input_rows = jnp.concatenate(pieces, axis=1)
    in_gain = jnp.dot(
        input_full.T.astype(jnp.float32), affine.T, precision=lax.Precision.HIGHEST
    )
    mixed, starts, values_split = run_forward(
        after(values, input_rows, in_gain, *ring[5:6]), skip, jump, flow, lead, out_table, in_table, toeplitz
    )
    mixed_tokens = to_tokens(after(mixed, *ring[6:8]), sequences)

    upper, up_slope, lifted_grad, channel_keep, channel_send, mix_bias_part = run_gate(
        after(normed, mixed), out_grad, fronts, where, 4 * channels, up_shift
    )
    channel_sent = swap(after(channel_send, mixed_tokens), 1)
    mixed_parts = gather_parts(mixed_tokens)
    channel_passed = channel_keep[1] + channel_sent[1]
    channel_sum = channel_keep[0] + channel_sent[0]
    channel_far = swap(channel_passed, 2)
    mixed_grad = (channel_sum + channel_far).astype(jnp.bfloat16)
    grads = to_channels(mixed_grad, sequences)

    (
        mixed_full,
        hidden,
        up_pre_grad,
        out_keep,
        out_send,
        feature_keep,
        feature_send,
        up_sums,
        up_bias_part,
    ) = run_mid(
        (after(mixed_parts[0], channel_passed),) + mixed_parts[1:],
        upper,
        up_slope,
        normed,
        fronts,
        where,
        mix_shift,
        affine,
    )
    out_sent, feature_sent = swap(out_send, 1), swap(feature_send, 1)

    def passed(keep, sent):
        return (keep[1].astype(jnp.float32) + sent[1].astype(jnp.float32)).astype(jnp.bfloat16)

    feature_passed = passed(feature_keep, feature_sent)
    out_passed = passed(out_keep, out_sent)
    make_grads = run_grads if feature_rows % 128 == 0 else plain_grads
    down_send, down_keep, rest_send, rest_keep = make_grads(
        out_grad, normed, mixed_full, after(hidden, mixed_grad), up_pre_grad, lifted_grad
    )
    feature_far = swap(feature_passed, 2)
    down_sent, rest_sent = after(down_send, grads), after(rest_send, grads)
    grads = after(grads, down_send, feature_passed, out_passed)
    values_grad, later, grads_split = run_backward(
        grads, skip, jump, flow, lead, out_table, in_table, toeplitz
    )
    values_back = to_tokens(after(values_grad, feature_far), sequences)
    out_far = swap(after(out_passed, values_grad, feature_far), 2)
    sums, skip_sums = run_sums(grads_split, values_split, starts, later, power)
    down_half = halve(down_sent, after(down_keep, values_grad))
    rest_half = halve(rest_sent, after(rest_keep, values_grad))
    down_total = settle_apart(down_half)
    rest_total = settle(after(rest_half, values_back))
    down_weight_grad = down_total.T
    up_weight_grad, mix_weight_grad = rest_total[:feature_rows], rest_total[feature_rows:]
    payload, input_bias_part = run_payload(
        after(values_back, sums, rest_half, down_total, out_far), in_slope, pre_in, in_gain, input_shift, up_sums
    )
    payload_parts = gather_parts(payload)
    sums, skip_sums, up_bias_part, mix_bias_part, down_shift, gain_all, _ = lax.optimization_barrier(
        (sums, skip_sums, up_bias_part, mix_bias_part, down_shift, affine[0], payload)
    )
    gain_own = lax.dynamic_slice_in_dim(gain_all, place * width, width)
    input_grad, late_vectors = run_final(
        payload_parts,
        input_rows,
        feature_keep,
        feature_sent,
        feature_far,
        tokens,
        stats,
        out_grad,
        gain_own,
    )

    inputs = tokens.astype(jnp.float32)
    output = (
        out_keep[0].astype(jnp.float32)
        + out_sent[0].astype(jnp.float32)
        + out_far.astype(jnp.float32)
        + down_shift
        + inputs
    )

    sums = jnp.concatenate([sums[:, :4], sums[:, 4:8] * flow[:, :, :modes], sums[:, 8:]], axis=1)
    sums = jnp.sum(sums.reshape((sequences, share) + sums.shape[1:]), axis=0)
    skip_grad = jnp.sum(skip_sums.reshape(sequences, share, BLOCK), axis=(0, 2))
    out_zero = cmul(power_re[:, 0], power_im[:, 0], sums[:, 0], sums[:, 1])
    out_one = cmul(
        power_re[:, 0], power_im[:, 0], sums[:, 0] + sums[:, 2], sums[:, 1] + sums[:, 3]
    )
    chained = cmul(power_re[:, 7], power_im[:, 7], sums[:, 8], sums[:, 9])
    local_zero, local_one = (sums[:, 10], sums[:, 11]), (sums[:, 12], sums[:, 13])
    read_re_grad = out_zero[0] + inflow * local_zero[0]
    read_im_grad = -out_zero[1] - inflow * local_zero[1]
    turn = cmul(
        read_re, read_im, out_one[0] + inflow * local_one[0], out_one[1] + inflow * local_one[1]
    )
    turn_re = turn[0] + sums[:, 6] + BLOCK * chained[0]
    turn_im = turn[1] + sums[:, 7] + BLOCK * chained[1]
    inflow_grad = sums[:, 4] / inflow + read_re * local_zero[0] - read_im * local_zero[1]
    damping_grad = jnp.exp(-damping) * inflow_grad - turn_re
    rotation_grad = -turn_im
    step_log_grad = spacing * jnp.sum(
        rate[None, :] * damping_grad + freq[None, :] * rotation_grad, axis=1
    )
    rates = jnp.stack(
        [
            jnp.sum(spacing[:, None] * damping_grad, axis=0),
            jnp.sum(spacing[:, None] * rotation_grad, axis=0),
        ]
    )
    rates = rates + swap(rates, 1)
    input_part = dot(normed, after(payload, rates)[:channels], 0, 1)
    rates = rates + swap(rates, 2)

    read_grads = jnp.stack([read_re_grad, read_im_grad], axis=1)
    read_grads = read_grads.reshape(share, 2, devices, modes_here).transpose(2, 0, 1, 3)
    read_grads = read_grads.reshape(devices, share, 2 * modes_here)
    read_grads = jnp.pad(read_grads, ((0, 0), (0, 0), (0, 128 - 2 * modes_here)))

    def line_up(vectors):
        vectors = [v.reshape(devices, -1) for v in vectors]
        sizes = [v.shape[1] for v in vectors]
        return tile_rows(jnp.concatenate(vectors, axis=1)), sizes

    def take_apart(flat, sizes):
        parts, spot = [], 0
        for size in sizes:
            parts.append(flat[spot : spot + size])
            spot += size
        return parts

    vectors, sizes = line_up(
        (
            up_bias_part,
            input_bias_part,
            mix_bias_part,
            rates[0],
            rates[1],
        )
    )
    input_part = input_part.reshape(devices, feature_rows, channels)
    parcel = jnp.concatenate([read_grads, vectors], axis=1)
    exact_rows = -(-parcel.shape[1] // 16) * 16
    parcel = jnp.pad(parcel, ((0, 0), (0, exact_rows - parcel.shape[1]), (0, 0)))
    parcel = jnp.concatenate(planes(parcel, 2) + [input_part.astype(jnp.bfloat16)], axis=1)
    late = jnp.concatenate([parcel, after(late_vectors, rest_total)], axis=1)
    late = lax.all_to_all(late, "seq", 0, 0, tiled=True).astype(jnp.float32)
    input_weight_grad = jnp.sum(late[:, 2 * exact_rows : 2 * exact_rows + feature_rows], axis=0)
    tail = jnp.sum(late[:, 2 * exact_rows + feature_rows :], axis=(0, 1))
    late = late[:, :exact_rows] + late[:, exact_rows : 2 * exact_rows]
    read_late = late[:, :share, : 2 * modes_here].reshape(channels, 2 * modes_here)
    late = take_apart(jnp.sum(late[:, share:], axis=0).reshape(-1), sizes)
    up_bias_grad, input_bias_grad, mix_bias_grad, rate_out, freq_out = late
    gain_grad, shift_grad, down_bias_grad = take_apart(tail, [width // devices] * 3)
    return (
        output,
        input_grad,
        gain_grad,
        shift_grad,
        up_weight_grad,
        up_bias_grad,
        input_weight_grad,
        input_bias_grad,
        mix_weight_grad,
        mix_bias_grad,
        down_weight_grad,
        down_bias_grad,
        rate_out,
        freq_out,
        step_log_grad,
        read_late[:, :modes_here],
        read_late[:, modes_here:],
        skip_grad,
    )


def solution(mesh):
    return jax.shard_map(
        per_device,
        mesh=mesh,
        in_specs=(
            P("seq", "chan"),
            P(("chan", "seq")),
            P(("chan", "seq")),
            P("seq", "chan"),
            P(("chan", "seq")),
            P("seq", "chan"),
            P(("chan", "seq")),
            P("seq", "chan"),
            P(("chan", "seq")),
            P("chan", "seq"),
            P(("chan", "seq")),
            P("seq"),
            P("seq"),
            P(("chan", "seq")),
            P("chan", "seq"),
            P("chan", "seq"),
            P(("chan", "seq")),
            P("seq", None),
        ),
        out_specs=(
            P("seq", "chan"),
            P("seq", "chan"),
            P(("chan", "seq")),
            P(("chan", "seq")),
            P("seq", "chan"),
            P(("chan", "seq")),
            P("seq", "chan"),
            P(("chan", "seq")),
            P("seq", "chan"),
            P(("chan", "seq")),
            P("chan", "seq"),
            P(("chan", "seq")),
            P("seq"),
            P("seq"),
            P(("chan", "seq")),
            P("chan", "seq"),
            P("chan", "seq"),
            P(("chan", "seq")),
        ),
        check_vma=False,
    )
```
